512 devices in a mesh: sub: 64 (over z, y), grp: 8 (over x, core).
Axes of the slice: x: 4, y: 8, z: 8, core: 2. Of those that a mesh axis runs over, the one named last changes fastest.
Arguments:
- vectors: bfloat16 [8, 64, 1024, 512], P('grp', 'sub'), may hold values from -6 to 6
- blocks: bfloat16 [8, 64, 1024, 1024], P('grp', 'sub'), may hold values from -0.1875 to 0.1875
- basis: bfloat16 [8, 64, 1024, 128], P('grp', 'sub'), may hold values from -0.25 to 0.25
- transfer: bfloat16 [8, 64, 9, 128, 128], P('grp', 'sub'), as said below
- coupling: bfloat16 [8, 64, 9, 128, 128], P('grp', 'sub'), as said below
Outputs:
- applied: bfloat16 [8, 64, 1024, 512], P('grp', 'sub')
The draws below stay inside these ranges and needn't reach their ends.
Inputs may be any that keep to these rules, and one draw needn't show every extreme that they name: transfer[g, s, l] is the same for all leaves g * 64 + s of one level-l node. coupling[g, s, l] is the same for all leaves g * 64 + s of one level-l node.
All inputs are finite; a program needn't handle non-finite values.
Results may differ from the reference program's by a relative error of at most 0.0047.
Values may be sent and summed in bfloat16 or wider, within the bound.
A program may use at most 64 MiB of HBM per device.

```python
import jax
import jax.numpy as jnp
from jax import lax

LEAF = 1024
RANK = 128
VECS = 512
LEVELS = 9
N_SUB = 64
N_GRP = 8


def path_copies(base, leaves):
    stacked = []
    for level in range(LEVELS):
        owners = jnp.left_shift(jnp.right_shift(jnp.arange(leaves, dtype=jnp.int32), level), level)
        stacked.append(base[owners, level])
    return jnp.stack(stacked, axis=1).reshape(N_GRP, N_SUB, LEVELS, RANK, RANK)


def draw_transfer(key, part):
    key = jax.random.fold_in(key, 11)
    leaves = N_GRP * N_SUB
    scale = (RANK * 99 // 70) ** (-0.5)
    base = jax.random.normal(key, (leaves, LEVELS, RANK, RANK), jnp.float32)
    return (path_copies(base, leaves) * scale).astype(jnp.bfloat16)


def draw_coupling(key, part):
    key = jax.random.fold_in(key, 23)
    leaves = N_GRP * N_SUB
    scale = RANK ** (-0.5)
    base = jax.random.normal(key, (leaves, LEVELS, RANK, RANK), jnp.float32)
    return (path_copies(base, leaves) * scale).astype(jnp.bfloat16)


def steps_of(key, extent, cuts, least, largest):
    def one(dim, blocks):
        heights = jax.random.uniform(jax.random.fold_in(jax.random.fold_in(key, 6), dim), (blocks,), jnp.float32, least / len(cuts), largest / len(cuts))
        return jnp.repeat(jnp.exp(heights), extent[dim] // blocks).reshape((-1,) + (1,) * (len(extent) - dim - 1))

    factor_of = one(*cuts[0])
    for cut in cuts[1:]:
        factor_of = factor_of * one(*cut)
    return factor_of


def gaussian(stream_key, extent, deviation, limit, shards=(), held_as=jnp.bfloat16):
    values = deviation * jax.random.normal(stream_key, extent, jnp.float32)
    if shards:
        values = values * steps_of(stream_key, extent, shards, -0.22, 0.18)
    return jnp.clip(values, -limit, limit).astype(held_as)


def setup_inputs(seed: int = 0) -> dict:
    seeds = jax.random.split(jax.random.key(seed), 6)
    vectors = gaussian(seeds[0], (N_GRP, N_SUB, LEAF, VECS), 1.0, 6.0, ((0, 8), (1, 64)))
    blocks = gaussian(seeds[1], (N_GRP, N_SUB, LEAF, LEAF), LEAF ** -0.5, 0.1875, ((0, 8), (1, 64)))
    basis = gaussian(seeds[2], (N_GRP, N_SUB, LEAF, RANK), (LEAF // 2) ** -0.5, 0.25, ((0, 8), (1, 64)))
    transfer = draw_transfer(jax.random.fold_in(seeds[5], 71), 0)
    coupling = draw_coupling(jax.random.fold_in(seeds[5], 71), 0)
    return {"vectors": vectors, "blocks": blocks, "basis": basis, "transfer": transfer, "coupling": coupling}


def reference(vectors, blocks, basis, transfer, coupling):
    leaves = N_GRP * N_SUB
    flat_x = vectors.reshape(leaves, LEAF, VECS)
    flat_d = blocks.reshape(leaves, LEAF, LEAF)
    flat_u = basis.reshape(leaves, LEAF, RANK)
    trans_all = transfer.reshape(leaves, LEVELS, RANK, RANK)
    coup_all = coupling.reshape(leaves, LEVELS, RANK, RANK)

    def project(pair):
        return jnp.dot(pair[0].T, pair[1], preferred_element_type=jnp.float32)

    current = lax.map(project, (flat_u, flat_x))
    siblings = []
    for level in range(LEVELS):
        count = leaves >> level
        rsel = trans_all[::2 ** level, level].astype(jnp.float32)
        proj = jnp.einsum('nab,nav->nbv', rsel, current, precision=lax.Precision.HIGHEST)
        siblings.append(current.reshape(count // 2, 2, RANK, VECS)[:, ::-1].reshape(count, RANK, VECS))
        current = proj[0::2] + proj[1::2]
    far = jnp.zeros((1, RANK, VECS), jnp.float32)
    for level in reversed(range(LEVELS)):
        parent = jnp.repeat(far, 2, axis=0)
        rsel = trans_all[::2 ** level, level].astype(jnp.float32)
        bsel = coup_all[::2 ** level, level].astype(jnp.float32)
        far = jnp.einsum('nab,nbv->nav', bsel, siblings[level], precision=lax.Precision.HIGHEST) + jnp.einsum('nab,nbv->nav', rsel, parent, precision=lax.Precision.HIGHEST)
    far_bf = far.astype(jnp.bfloat16)

    def finish(group):
        near = jnp.dot(group[0], group[1], preferred_element_type=jnp.float32)
        return (near + jnp.dot(group[2], group[3], preferred_element_type=jnp.float32)).astype(jnp.bfloat16)

    applied = lax.map(finish, (flat_d, flat_x, flat_u, far_bf))
    return applied.reshape(N_GRP, N_SUB, LEAF, VECS)
```

```python
import functools

import jax
import jax.numpy as jnp
from jax import lax
from jax.experimental import pallas as pl
from jax.experimental.pallas import tpu as pltpu
from jax.sharding import PartitionSpec as P

MESH = pl.DeviceIdType.MESH
BF = jnp.bfloat16
F32 = jnp.float32


def dot(left, right):
    return jnp.dot(left, right, preferred_element_type=F32)


def dot_nt(left, right):
    return lax.dot_general(left, right, (((1,), (1,)), ((), ())), preferred_element_type=F32)


def dot_tn(left, right):
    return lax.dot_general(left, right, (((0,), (0,)), ((), ())), preferred_element_type=F32)


def split(value):
    high = value.astype(BF)
    return high, (value - high.astype(F32)).astype(BF)


def flip(index, offset):
    out = index
    for bit in range(offset.bit_length()):
        if offset >> bit & 1:
            out = out + (1 << bit) * (1 - 2 * ((index // (1 << bit)) % 2))
    return out


def level_of(offset):
    return offset.bit_length() - 1


def wait_bytes(ref, sem):
    pltpu.make_async_copy(ref, ref, sem).wait()


def up_weight(product):
    high, low = split(product)
    return jnp.concatenate([high, high, low], axis=0)


def up_exact(matrix):
    return jnp.concatenate([matrix, matrix, jnp.zeros_like(matrix)], axis=0)


def wide(value):
    high, low = split(value)
    return jnp.concatenate([high, low, high], axis=1)


def times_exact(product, matrix):
    high, low = split(product)
    return dot(high, matrix) + dot(low, matrix)


def kernel(dims, x_hbm, d_hbm, u_hbm, t_hbm, b_hbm, o_hbm,
           xv, dv, uv, tv, bv, near, ov,
           wy, wyl, wz, wzl, wxl, vy, vyl, vz, vzl, vx,
           h_send, h_recv, cy_send, cy_recv, cl_send, cl_recv, sl_send, sl_recv,
           cz_send, cz_recv, zs_send, zs_recv, x_send, x_recv,
           far_z_send, far_z, far_y_send, far_y,
           load_sem, store_sem, send_sem, recv_sem):
    ly, lz, lx = dims
    ny, nz, nx = 1 << ly, 1 << lz, 1 << lx
    leaf, vecs = x_hbm.shape
    yblk = vecs // ny
    zblk = yblk // nz
    sub, grp = lax.axis_index("sub"), lax.axis_index("grp")
    y, z = sub % ny, sub // ny

    def y_peer(j):
        return {"sub": z * ny + flip(y, j)}

    def z_peer(j):
        return {"sub": flip(z, j) * ny + y}

    def x_peer(j):
        return {"grp": flip(grp, j)}

    def rows(index, size):
        return pl.ds(pl.multiple_of(index * size, size), size)

    def send(src, dst, group, peer):
        pltpu.make_async_remote_copy(
            src_ref=src, dst_ref=dst, send_sem=send_sem.at[group], recv_sem=recv_sem.at[group],
            device_id=peer, device_id_type=MESH,
        ).start()

    barrier = pltpu.get_barrier_semaphore()
    peers = [y_peer(j) for j in range(1, ny)] + [z_peer(j) for j in range(1, nz)] + [x_peer(j) for j in range(1, nx)]
    for peer in peers:
        pl.semaphore_signal(barrier, inc=1, device_id=peer, device_id_type=MESH)

    loads = [pltpu.make_async_copy(src, dst, load_sem.at[i]) for i, (src, dst) in enumerate(
        ((t_hbm, tv), (u_hbm, uv), (x_hbm, xv), (b_hbm, bv), (d_hbm, dv)))]
    for load in loads:
        load.start()

    loads[0].wait()

    def climb(base, levels):
        product = tv[base].astype(F32)
        chain = [product]
        for level in range(1, levels):
            product = times_exact(product, tv[base + level])
            chain.append(product)
        return chain

    ty = climb(0, ly)
    wy[...] = up_weight(ty[ly - 1])
    wyl[...] = jnp.concatenate([up_exact(tv[0])] + [up_weight(ty[i]) for i in range(1, ly - 1)], axis=1)

    loads[1].wait()
    loads[2].wait()
    hat = dot_tn(xv[...], uv[...])
    hat_w = wide(hat)
    cy = dot(hat_w, wy[...])
    cy_send[...] = cy.astype(BF)
    pl.semaphore_wait(barrier, len(peers))
    for j in range(1, ny):
        send(cy_send.at[rows(flip(y, j), yblk)], cy_recv.at[j], 0, y_peer(j))
    cl = dot(hat_w, wyl[...])
    for i in range(ly - 1):
        cl_send[i] = cl[:, i * 128:(i + 1) * 128].astype(BF)
    for j in range(1, ny):
        send(cl_send.at[:, rows(flip(y, j), yblk)], cl_recv.at[j], 1, y_peer(j))
    h_send[...] = hat.astype(BF)
    send(h_send, h_recv, 2, y_peer(1))

    tz = climb(ly, lz)
    wz[...] = up_weight(tz[lz - 1])
    if lz > 1:
        wzl[...] = jnp.concatenate([up_exact(tv[ly])] + [up_weight(tz[i]) for i in range(1, lz - 1)], axis=1)
    tx = climb(ly + lz, lx)
    if lx > 1:
        wxl[...] = jnp.concatenate([up_exact(tv[ly + lz])] + [up_weight(tx[i]) for i in range(1, lx - 1)], axis=1)

    loads[4].wait()
    tile = leaf // 4

    @pl.loop(0, 4)
    def _(step):
        at = pl.ds(pl.multiple_of(step * tile, tile), tile)
        near[at, :] = dot(dv[at, :], xv[...])

    wait_bytes(cy_recv.at[pl.ds(1, ny - 1)], recv_sem.at[0])
    mid = cy_send[rows(y, yblk), :].astype(F32)
    for j in range(1, ny):
        mid = mid + cy_recv[j].astype(F32)
    mid_w = wide(mid)
    cz_send[...] = dot(mid_w, wz[...])
    for j in range(1, nz):
        send(cz_send.at[rows(flip(z, j), zblk)], cz_recv.at[j], 3, z_peer(j))
    zs_send[0] = mid.astype(BF)
    if lz > 1:
        zl = dot(mid_w, wzl[...])
        for i in range(lz - 1):
            zs_send[i + 1] = zl[:, i * 128:(i + 1) * 128].astype(BF)
    for j in range(1, nz):
        send(zs_send.at[level_of(j)], zs_recv.at[j], 4, z_peer(j))

    wait_bytes(cl_recv.at[pl.ds(1, ny - 1)], recv_sem.at[1])
    for i in range(ly - 1):
        level = i + 1
        own = cl_send[i, rows(y, yblk), :].astype(F32)
        parts = [own] + [cl_recv[j, i].astype(F32) for j in range(1, ny)]
        sums = []
        for node in range(ny >> level):
            sums.append(functools.reduce(jnp.add, parts[node << level:(node + 1) << level]).astype(BF))
        for pair in range(ny // 2):
            sl_send[pair, i] = sums[(pair >> (level - 1)) ^ 1]
    for j in range(1, ny):
        send(sl_send.at[j // 2], sl_recv.at[:, rows(y, yblk)], 5, y_peer(j))
    sl_recv[:, rows(y, yblk), :] = sl_send[0]

    loads[3].wait()

    def down(products, base, levels, doubled):
        parts = [bv[base]] * doubled
        for i in range(1, levels):
            high, low = split(times_exact(products[i - 1], bv[base + i]))
            parts += [high, high, low] if doubled > 1 or base else [high, low]
        return jnp.concatenate(parts, axis=1)

    vx[...] = down(tx, ly + lz, lx, 2)

    wait_bytes(cz_recv.at[pl.ds(1, nz - 1)], recv_sem.at[3])
    top = cz_send[rows(z, zblk), :]
    for j in range(1, nz):
        top = top + cz_recv[j]
    x_send[0] = top
    if lx > 1:
        xl = dot(wide(top), wxl[...])
        for i in range(lx - 1):
            x_send[i + 1] = xl[:, i * 128:(i + 1) * 128]
    for j in range(1, nx):
        send(x_send.at[level_of(j)], x_recv.at[j], 6, x_peer(j))

    vz[...] = down(tz, ly, lz, 1)
    high, low = split(tz[lz - 1])
    vzl[...] = jnp.concatenate([high, high, low], axis=1)
    vy[...] = down(ty, 0, ly, 1)
    high, low = split(ty[ly - 1])
    vyl[...] = jnp.concatenate([high, low], axis=1)

    wait_bytes(x_recv.at[pl.ds(1, nx - 1)], recv_sem.at[6])
    parts = list(split(x_recv[1]))
    for level in range(1, lx):
        high, low = split(functools.reduce(jnp.add, [x_recv[j] for j in range(1 << level, 2 << level)]))
        parts += [high, low, high]
    far_z_send[...] = dot_nt(jnp.concatenate(parts, axis=1), vx[...])
    for j in range(1, nz):
        send(far_z_send, far_z.at[rows(z, zblk)], 7, z_peer(j))
    far_z[rows(z, zblk), :] = far_z_send[...]

    wait_bytes(zs_recv.at[pl.ds(1, nz - 1)], recv_sem.at[4])
    parts = [zs_recv[1]]
    for level in range(1, lz):
        high, low = split(functools.reduce(jnp.add, [zs_recv[j].astype(F32) for j in range(1 << level, 2 << level)]))
        parts += [high, low, high]
    mid_far = dot_nt(jnp.concatenate(parts, axis=1), vz[...])
    wait_bytes(far_z.at[pl.ds(0, (nz - 1) * zblk)], recv_sem.at[7])
    mid_far = mid_far + dot_nt(wide(far_z[...]), vzl[...])
    far_y_send[...] = mid_far.astype(BF)
    for j in range(1, ny):
        send(far_y_send, far_y.at[rows(y, yblk)], 8, y_peer(j))
    far_y[rows(y, yblk), :] = far_y_send[...]

    wait_bytes(h_recv, recv_sem.at[2])
    wait_bytes(sl_recv.at[:, pl.ds(0, (ny - 1) * yblk)], recv_sem.at[5])
    parts = [h_recv[...]]
    for i in range(ly - 1):
        parts += [sl_recv[i]] * 2
    far = dot_nt(jnp.concatenate(parts, axis=1), vy[...])
    wait_bytes(far_y.at[pl.ds(0, (ny - 1) * yblk)], recv_sem.at[8])
    last = far_y[...]
    far = far + dot_nt(jnp.concatenate([last, last], axis=1), vyl[...])
    far_bf = far.astype(BF)
    stores = []
    for step in range(4):
        at = pl.ds(step * tile, tile)
        ov[at, :] = (near[at, :] + dot_nt(uv[at, :], far_bf)).astype(BF)
        store = pltpu.make_async_copy(ov.at[at], o_hbm.at[at], store_sem.at[step])
        store.start()
        stores.append(store)

    wait_bytes(cy_send.at[pl.ds(0, (ny - 1) * yblk)], send_sem.at[0])
    wait_bytes(cl_send.at[:, pl.ds(0, (ny - 1) * yblk)], send_sem.at[1])
    wait_bytes(h_send, send_sem.at[2])
    wait_bytes(cz_recv.at[pl.ds(1, nz - 1)], send_sem.at[3])
    wait_bytes(zs_recv.at[pl.ds(1, nz - 1)], send_sem.at[4])
    wait_bytes(sl_recv.at[:, pl.ds(0, (ny - 1) * yblk)], send_sem.at[5])
    wait_bytes(x_recv.at[pl.ds(1, nx - 1)], send_sem.at[6])
    wait_bytes(far_z.at[pl.ds(0, (nz - 1) * zblk)], send_sem.at[7])
    wait_bytes(far_y.at[pl.ds(0, (ny - 1) * yblk)], send_sem.at[8])
    for store in stores:
        store.wait()


def solution(mesh):
    sub_levels = mesh.shape["sub"].bit_length() - 1
    ly = (sub_levels + 1) // 2
    lz = sub_levels - ly
    lx = mesh.shape["grp"].bit_length() - 1
    dims = (ly, lz, lx)
    ny, nz, nx = 1 << ly, 1 << lz, 1 << lx

    def body(vectors, blocks, basis, transfer, coupling):
        leaf, vecs = vectors.shape[2:]
        rank = basis.shape[3]
        levels = transfer.shape[2]
        yblk, zblk = vecs // ny, vecs // ny // nz
        scratch = [
            pltpu.VMEM((leaf, vecs), BF),
            pltpu.VMEM((leaf, leaf), BF),
            pltpu.VMEM((leaf, rank), BF),
            pltpu.VMEM((levels, rank, rank), BF),
            pltpu.VMEM((levels, rank, rank), BF),
            pltpu.VMEM((leaf, vecs), F32),
            pltpu.VMEM((leaf, vecs), BF),
            pltpu.VMEM((3 * rank, rank), BF),
            pltpu.VMEM((3 * rank, max(1, ly - 1) * rank), BF),
            pltpu.VMEM((3 * rank, rank), BF),
            pltpu.VMEM((3 * rank, max(1, lz - 1) * rank), BF),
            pltpu.VMEM((3 * rank, max(1, lx - 1) * rank), BF),
            pltpu.VMEM((rank, (2 * ly - 1) * rank), BF),
            pltpu.VMEM((rank, 2 * rank), BF),
            pltpu.VMEM((rank, (3 * lz - 2) * rank), BF),
            pltpu.VMEM((rank, 3 * rank), BF),
            pltpu.VMEM((rank, (3 * lx - 1) * rank), BF),
            pltpu.VMEM((vecs, rank), BF),
            pltpu.VMEM((vecs, rank), BF),
            pltpu.VMEM((vecs, rank), BF),
            pltpu.VMEM((ny, yblk, rank), BF),
            pltpu.VMEM((ly - 1, vecs, rank), BF),
            pltpu.VMEM((ny, ly - 1, yblk, rank), BF),
            pltpu.VMEM((ny // 2, ly - 1, yblk, rank), BF),
            pltpu.VMEM((ly - 1, vecs, rank), BF),
            pltpu.VMEM((yblk, rank), F32),
            pltpu.VMEM((nz, zblk, rank), F32),
            pltpu.VMEM((lz, yblk, rank), BF),
            pltpu.VMEM((nz, yblk, rank), BF),
            pltpu.VMEM((lx, zblk, rank), F32),
            pltpu.VMEM((nx, zblk, rank), F32),
            pltpu.VMEM((zblk, rank), F32),
            pltpu.VMEM((yblk, rank), F32),
            pltpu.VMEM((yblk, rank), BF),
            pltpu.VMEM((vecs, rank), BF),
            pltpu.SemaphoreType.DMA((5,)),
            pltpu.SemaphoreType.DMA((4,)),
            pltpu.SemaphoreType.DMA((9,)),
            pltpu.SemaphoreType.DMA((9,)),
        ]
        anywhere = pl.BlockSpec(memory_space=pl.ANY)
        out = pl.pallas_call(
            functools.partial(kernel, dims),
            out_shape=jax.ShapeDtypeStruct((leaf, vecs), BF),
            in_specs=[anywhere] * 5,
            out_specs=anywhere,
            scratch_shapes=scratch,
            compiler_params=pltpu.CompilerParams(
                collective_id=0, has_side_effects=True, vmem_limit_bytes=48 * 1024 * 1024,
            ),
        )(vectors[0, 0], blocks[0, 0], basis[0, 0], transfer[0, 0], coupling[0, 0])
        return out[None, None]

    return jax.shard_map(
        body,
        mesh=mesh,
        in_specs=(
            P("grp", "sub", None, None),
            P("grp", "sub", None, None),
            P("grp", "sub", None, None),
            P("grp", "sub", None, None, None),
            P("grp", "sub", None, None, None),
        ),
        out_specs=P("grp", "sub", None, None),
        check_vma=False,
    )
```

```python
import functools

import jax
import jax.numpy as jnp
from jax import lax
from jax.experimental import pallas as pl
from jax.experimental.pallas import tpu as pltpu
from jax.sharding import PartitionSpec as P

MESH = pl.DeviceIdType.MESH
BF = jnp.bfloat16
F32 = jnp.float32


def dot(left, right):
    return jnp.dot(left, right, preferred_element_type=F32)


def dot_nt(left, right):
    return lax.dot_general(left, right, (((1,), (1,)), ((), ())), preferred_element_type=F32)


def dot_tn(left, right):
    return lax.dot_general(left, right, (((0,), (0,)), ((), ())), preferred_element_type=F32)


def split(value):
    high = value.astype(BF)
    return high, (value - high.astype(F32)).astype(BF)


def flip(index, offset):
    out = index
    for bit in range(offset.bit_length()):
        if offset >> bit & 1:
            out = out + (1 << bit) * (1 - 2 * ((index // (1 << bit)) % 2))
    return out


def level_of(offset):
    return offset.bit_length() - 1


def wait_bytes(ref, sem):
    pltpu.make_async_copy(ref, ref, sem).wait()


def up_weight(product):
    high, low = split(product)
    return jnp.concatenate([high, high, low], axis=0)


def up_exact(matrix):
    return jnp.concatenate([matrix, matrix, jnp.zeros_like(matrix)], axis=0)


def wide(value):
    high, low = split(value)
    return jnp.concatenate([high, low, high], axis=1)


def times_exact(product, matrix):
    high, low = split(product)
    return dot(high, matrix) + dot(low, matrix)


def kernel(dims, x_hbm, d_hbm, u_hbm, t_hbm, b_hbm, o_hbm,
           xv, dv, uv, ut, tv, bv, near, ov,
           wy, wyl, wz, wzl, wxl, vy, vyl, vz, vzl, vx,
           h_send, h_recv, cy_send, cy_recv, cl_send, cl_recv, sl_send, sl_recv,
           cz_send, cz_recv, zs_send, zs_recv, x_send, x_recv,
           far_z_send, far_z, far_y_send, far_y,
           load_sem, store_sem, send_sem, recv_sem):
    ly, lz, lx = dims
    ny, nz, nx = 1 << ly, 1 << lz, 1 << lx
    leaf, vecs = x_hbm.shape
    yblk = vecs // ny
    zblk = yblk // nz
    sub, grp = lax.axis_index("sub"), lax.axis_index("grp")
    y, z = sub % ny, sub // ny

    def y_peer(j):
        return {"sub": z * ny + flip(y, j)}

    def z_peer(j):
        return {"sub": flip(z, j) * ny + y}

    def x_peer(j):
        return {"grp": flip(grp, j)}

    def rows(index, size):
        return pl.ds(pl.multiple_of(index * size, size), size)

    def send(src, dst, group, peer):
        pltpu.make_async_remote_copy(
            src_ref=src, dst_ref=dst, send_sem=send_sem.at[group], recv_sem=recv_sem.at[group],
            device_id=peer, device_id_type=MESH,
        ).start()

    head = leaf // 2
    loads = {}
    for i, (name, src, dst) in enumerate((
        ("t0", t_hbm.at[pl.ds(0, ly)], tv.at[pl.ds(0, ly)]),
        ("u", u_hbm, uv),
        ("x0", x_hbm.at[pl.ds(0, head)], xv.at[pl.ds(0, head)]),
        ("x1", x_hbm.at[pl.ds(head, head)], xv.at[pl.ds(head, head)]),
        ("t1", t_hbm.at[pl.ds(ly, lz + lx)], tv.at[pl.ds(ly, lz + lx)]),
        ("b", b_hbm, bv),
        ("d", d_hbm, dv),
    )):
        loads[name] = pltpu.make_async_copy(src, dst, load_sem.at[i])
        loads[name].start()

    barrier = pltpu.get_barrier_semaphore()
    peers = [y_peer(j) for j in range(1, ny)] + [z_peer(j) for j in range(1, nz)] + [x_peer(j) for j in range(1, nx)]
    for peer in peers:
        pl.semaphore_signal(barrier, inc=1, device_id=peer, device_id_type=MESH)

    def climb(base, levels):
        product = tv[base].astype(F32)
        chain = [product]
        for level in range(1, levels):
            product = times_exact(product, tv[base + level])
            chain.append(product)
        return chain

    def down(products, base, levels, doubled):
        parts = [bv[base]] * doubled
        for i in range(1, levels):
            high, low = split(times_exact(products[i - 1], bv[base + i]))
            parts += [high, high, low] if doubled > 1 or base else [high, low]
        return jnp.concatenate(parts, axis=1)

    def near_part(part, parts):
        size = vecs // parts
        at = pl.ds(part * size, size)
        near[:, at] = dot(dv[...], xv[:, at])

    loads["t0"].wait()
    ty = climb(0, ly)
    wy[...] = up_weight(ty[ly - 1])
    loads["u"].wait()
    ut[...] = uv[...].T

    loads["x0"].wait()
    hat_t = dot(ut[:, :head], xv[:head, :])
    loads["x1"].wait()
    hat = (hat_t + dot(ut[:, head:], xv[head:, :])).T
    hat_w = wide(hat)
    cy = dot(hat_w, wy[...])
    cy_send[...] = cy.astype(BF)
    pl.semaphore_wait(barrier, len(peers))
    for j in range(1, ny):
        send(cy_send.at[rows(flip(y, j), yblk)], cy_recv.at[j], 0, y_peer(j))

    wyl[...] = jnp.concatenate([up_exact(tv[0])] + [up_weight(ty[i]) for i in range(1, ly - 1)], axis=1)
    cl = dot(hat_w, wyl[...])
    for i in range(ly - 1):
        cl_send[i] = cl[:, i * 128:(i + 1) * 128].astype(BF)
    for j in range(1, ny):
        send(cl_send.at[:, rows(flip(y, j), yblk)], cl_recv.at[j], 1, y_peer(j))
    h_send[...] = hat.astype(BF)
    send(h_send, h_recv, 2, y_peer(1))
    loads["t1"].wait()
    tz = climb(ly, lz)
    wz[...] = up_weight(tz[lz - 1])

    wait_bytes(cy_recv.at[pl.ds(1, ny - 1)], recv_sem.at[0])
    mid = cy_send[rows(y, yblk), :].astype(F32)
    for j in range(1, ny):
        mid = mid + cy_recv[j].astype(F32)
    mid_w = wide(mid)
    cz_send[...] = dot(mid_w, wz[...])
    for j in range(1, nz):
        send(cz_send.at[rows(flip(z, j), zblk)], cz_recv.at[j], 3, z_peer(j))

    zs_send[0] = mid.astype(BF)
    if lz > 1:
        wzl[...] = jnp.concatenate([up_exact(tv[ly])] + [up_weight(tz[i]) for i in range(1, lz - 1)], axis=1)
        zl = dot(mid_w, wzl[...])
        for i in range(lz - 1):
            zs_send[i + 1] = zl[:, i * 128:(i + 1) * 128].astype(BF)
    for j in range(1, nz):
        send(zs_send.at[level_of(j)], zs_recv.at[j], 4, z_peer(j))
    tx = climb(ly + lz, lx)
    if lx > 1:
        wxl[...] = jnp.concatenate([up_exact(tv[ly + lz])] + [up_weight(tx[i]) for i in range(1, lx - 1)], axis=1)

    wait_bytes(cz_recv.at[pl.ds(1, nz - 1)], recv_sem.at[3])
    top = cz_send[rows(z, zblk), :]
    for j in range(1, nz):
        top = top + cz_recv[j]
    x_send[0] = top
    if lx > 1:
        xl = dot(wide(top), wxl[...])
        for i in range(lx - 1):
            x_send[i + 1] = xl[:, i * 128:(i + 1) * 128]
    for j in range(1, nx):
        send(x_send.at[level_of(j)], x_recv.at[j], 6, x_peer(j))

    wait_bytes(cl_recv.at[pl.ds(1, ny - 1)], recv_sem.at[1])
    for i in range(ly - 1):
        level = i + 1
        own = cl_send[i, rows(y, yblk), :].astype(F32)
        parts = [own] + [cl_recv[j, i].astype(F32) for j in range(1, ny)]
        sums = []
        for node in range(ny >> level):
            sums.append(functools.reduce(jnp.add, parts[node << level:(node + 1) << level]).astype(BF))
        for pair in range(ny // 2):
            sl_send[pair, i] = sums[(pair >> (level - 1)) ^ 1]
    for j in range(1, ny):
        send(sl_send.at[j // 2], sl_recv.at[:, rows(y, yblk)], 5, y_peer(j))
    sl_recv[:, rows(y, yblk), :] = sl_send[0]
    loads["b"].wait()
    vx[...] = down(tx, ly + lz, lx, 2)

    wait_bytes(x_recv.at[pl.ds(1, nx - 1)], recv_sem.at[6])
    parts = list(split(x_recv[1]))
    for level in range(1, lx):
        high, low = split(functools.reduce(jnp.add, [x_recv[j] for j in range(1 << level, 2 << level)]))
        parts += [high, low, high]
    far_z_send[...] = dot_nt(jnp.concatenate(parts, axis=1), vx[...])
    for j in range(1, nz):
        send(far_z_send, far_z.at[rows(z, zblk)], 7, z_peer(j))
    far_z[rows(z, zblk), :] = far_z_send[...]

    vz[...] = down(tz, ly, lz, 1)
    high, low = split(tz[lz - 1])
    vzl[...] = jnp.concatenate([high, high, low], axis=1)
    wait_bytes(zs_recv.at[pl.ds(1, nz - 1)], recv_sem.at[4])
    parts = [zs_recv[1]]
    for level in range(1, lz):
        high, low = split(functools.reduce(jnp.add, [zs_recv[j].astype(F32) for j in range(1 << level, 2 << level)]))
        parts += [high, low, high]
    mid_far = dot_nt(jnp.concatenate(parts, axis=1), vz[...])
    loads["d"].wait()
    near_part(0, 2)
    wait_bytes(far_z.at[pl.ds(0, (nz - 1) * zblk)], recv_sem.at[7])
    mid_far = mid_far + dot_nt(wide(far_z[...]), vzl[...])
    far_y_send[...] = mid_far.astype(BF)
    for j in range(1, ny):
        send(far_y_send, far_y.at[rows(y, yblk)], 8, y_peer(j))
    far_y[rows(y, yblk), :] = far_y_send[...]

    vy[...] = down(ty, 0, ly, 1)
    high, low = split(ty[ly - 1])
    vyl[...] = jnp.concatenate([high, low], axis=1)
    wait_bytes(h_recv, recv_sem.at[2])
    wait_bytes(sl_recv.at[:, pl.ds(0, (ny - 1) * yblk)], recv_sem.at[5])
    parts = [h_recv[...]]
    for i in range(ly - 1):
        parts += [sl_recv[i]] * 2
    far = dot_nt(jnp.concatenate(parts, axis=1), vy[...])
    near_part(1, 2)
    wait_bytes(far_y.at[pl.ds(0, (ny - 1) * yblk)], recv_sem.at[8])
    last = far_y[...]
    far = far + dot_nt(jnp.concatenate([last, last], axis=1), vyl[...])
    far_bf = far.astype(BF)
    tile = leaf // 4
    stores = []
    for step in range(4):
        at = pl.ds(step * tile, tile)
        ov[at, :] = (near[at, :] + dot_nt(uv[at, :], far_bf)).astype(BF)
        store = pltpu.make_async_copy(ov.at[at], o_hbm.at[at], store_sem.at[step])
        store.start()
        stores.append(store)

    wait_bytes(cy_send.at[pl.ds(0, (ny - 1) * yblk)], send_sem.at[0])
    wait_bytes(cl_send.at[:, pl.ds(0, (ny - 1) * yblk)], send_sem.at[1])
    wait_bytes(h_send, send_sem.at[2])
    wait_bytes(cz_recv.at[pl.ds(1, nz - 1)], send_sem.at[3])
    wait_bytes(zs_recv.at[pl.ds(1, nz - 1)], send_sem.at[4])
    wait_bytes(sl_recv.at[:, pl.ds(0, (ny - 1) * yblk)], send_sem.at[5])
    wait_bytes(x_recv.at[pl.ds(1, nx - 1)], send_sem.at[6])
    wait_bytes(far_z.at[pl.ds(0, (nz - 1) * zblk)], send_sem.at[7])
    wait_bytes(far_y.at[pl.ds(0, (ny - 1) * yblk)], send_sem.at[8])
    for store in stores:
        store.wait()


def solution(mesh):
    sub_levels = mesh.shape["sub"].bit_length() - 1
    ly = (sub_levels + 1) // 2
    lz = sub_levels - ly
    lx = mesh.shape["grp"].bit_length() - 1
    dims = (ly, lz, lx)
    ny, nz, nx = 1 << ly, 1 << lz, 1 << lx

    def body(vectors, blocks, basis, transfer, coupling):
        leaf, vecs = vectors.shape[2:]
        rank = basis.shape[3]
        levels = transfer.shape[2]
        yblk, zblk = vecs // ny, vecs // ny // nz
        scratch = [
            pltpu.VMEM((leaf, vecs), BF),
            pltpu.VMEM((leaf, leaf), BF),
            pltpu.VMEM((leaf, rank), BF),
            pltpu.VMEM((rank, leaf), BF),
            pltpu.VMEM((levels, rank, rank), BF),
            pltpu.VMEM((levels, rank, rank), BF),
            pltpu.VMEM((leaf, vecs), F32),
            pltpu.VMEM((leaf, vecs), BF),
            pltpu.VMEM((3 * rank, rank), BF),
            pltpu.VMEM((3 * rank, max(1, ly - 1) * rank), BF),
            pltpu.VMEM((3 * rank, rank), BF),
            pltpu.VMEM((3 * rank, max(1, lz - 1) * rank), BF),
            pltpu.VMEM((3 * rank, max(1, lx - 1) * rank), BF),
            pltpu.VMEM((rank, (2 * ly - 1) * rank), BF),
            pltpu.VMEM((rank, 2 * rank), BF),
            pltpu.VMEM((rank, (3 * lz - 2) * rank), BF),
            pltpu.VMEM((rank, 3 * rank), BF),
            pltpu.VMEM((rank, (3 * lx - 1) * rank), BF),
            pltpu.VMEM((vecs, rank), BF),
            pltpu.VMEM((vecs, rank), BF),
            pltpu.VMEM((vecs, rank), BF),
            pltpu.VMEM((ny, yblk, rank), BF),
            pltpu.VMEM((ly - 1, vecs, rank), BF),
            pltpu.VMEM((ny, ly - 1, yblk, rank), BF),
            pltpu.VMEM((ny // 2, ly - 1, yblk, rank), BF),
            pltpu.VMEM((ly - 1, vecs, rank), BF),
            pltpu.VMEM((yblk, rank), F32),
            pltpu.VMEM((nz, zblk, rank), F32),
            pltpu.VMEM((lz, yblk, rank), BF),
            pltpu.VMEM((nz, yblk, rank), BF),
            pltpu.VMEM((lx, zblk, rank), F32),
            pltpu.VMEM((nx, zblk, rank), F32),
            pltpu.VMEM((zblk, rank), F32),
            pltpu.VMEM((yblk, rank), F32),
            pltpu.VMEM((yblk, rank), BF),
            pltpu.VMEM((vecs, rank), BF),
            pltpu.SemaphoreType.DMA((7,)),
            pltpu.SemaphoreType.DMA((4,)),
            pltpu.SemaphoreType.DMA((9,)),
            pltpu.SemaphoreType.DMA((9,)),
        ]
        anywhere = pl.BlockSpec(memory_space=pl.ANY)
        out = pl.pallas_call(
            functools.partial(kernel, dims),
            out_shape=jax.ShapeDtypeStruct((leaf, vecs), BF),
            in_specs=[pl.BlockSpec(memory_space=pltpu.HBM)] * 5,
            out_specs=anywhere,
            scratch_shapes=scratch,
            compiler_params=pltpu.CompilerParams(
                collective_id=0, has_side_effects=True, vmem_limit_bytes=48 * 1024 * 1024,
            ),
        )(*(pltpu.with_memory_space_constraint(whole[0, 0], pltpu.HBM) for whole in (vectors, blocks, basis, transfer, coupling)))
        return out[None, None]

    return jax.shard_map(
        body,
        mesh=mesh,
        in_specs=(
            P("grp", "sub", None, None),
            P("grp", "sub", None, None),
            P("grp", "sub", None, None),
            P("grp", "sub", None, None, None),
            P("grp", "sub", None, None, None),
        ),
        out_specs=P("grp", "sub", None, None),
        check_vma=False,
    )
```

```python
import functools

import jax
import jax.numpy as jnp
from jax import lax
from jax.experimental import pallas as pl
from jax.experimental.pallas import tpu as pltpu
from jax.sharding import PartitionSpec as P

MESH = pl.DeviceIdType.MESH
BF = jnp.bfloat16
F32 = jnp.float32


def dot(left, right):
    return jnp.dot(left, right, preferred_element_type=F32)


def dot_nt(left, right):
    return lax.dot_general(left, right, (((1,), (1,)), ((), ())), preferred_element_type=F32)


def dot_tn(left, right):
    return lax.dot_general(left, right, (((0,), (0,)), ((), ())), preferred_element_type=F32)


def split(value):
    high = value.astype(BF)
    return high, (value - high.astype(F32)).astype(BF)


def flip(index, offset):
    out = index
    for bit in range(offset.bit_length()):
        if offset >> bit & 1:
            out = out + (1 << bit) * (1 - 2 * ((index // (1 << bit)) % 2))
    return out


def level_of(offset):
    return offset.bit_length() - 1


def wait_bytes(ref, sem):
    pltpu.make_async_copy(ref, ref, sem).wait()


def up_weight(product):
    high, low = split(product)
    return jnp.concatenate([high, high, low], axis=0)


def up_exact(matrix):
    return jnp.concatenate([matrix, matrix, jnp.zeros_like(matrix)], axis=0)


def wide(value):
    high, low = split(value)
    return jnp.concatenate([high, low, high], axis=1)


def times_exact(product, matrix):
    high, low = split(product)
    return dot(high, matrix) + dot(low, matrix)


def kernel(dims, x_hbm, d_hbm, u_hbm, t_hbm, b_hbm, o_hbm,
           xv, dv, uv, ut, tv, bv, near, ov,
           rt, bt, wy, vy, vyl, wz, wzl, wxl, vz, vzl, vx,
           h_send, h_recv, cy_send, cy_recv,
           cz_send, cz_recv, zs_send, zs_recv, x_send, x_recv,
           far_z_send, far_z, far_y_send, far_y,
           load_sem, store_sem, send_sem, recv_sem):
    lz, lx = dims
    ly = 3
    ny, nz, nx = 1 << ly, 1 << lz, 1 << lx
    leaf, vecs = x_hbm.shape
    rank = u_hbm.shape[1]
    yblk = vecs // ny
    zblk = yblk // nz
    sub, grp = lax.axis_index("sub"), lax.axis_index("grp")
    y, z = sub % ny, sub // ny

    def y_peer(j):
        return {"sub": z * ny + flip(y, j)}

    def z_peer(j):
        return {"sub": flip(z, j) * ny + y}

    def x_peer(j):
        return {"grp": flip(grp, j)}

    def rows(index, size):
        return pl.ds(pl.multiple_of(index * size, size), size)

    def send(src, dst, group, peer):
        pltpu.make_async_remote_copy(
            src_ref=src, dst_ref=dst, send_sem=send_sem.at[group], recv_sem=recv_sem.at[group],
            device_id=peer, device_id_type=MESH,
        ).start()

    head = leaf // 2
    loads = {}
    for i, (name, src, dst) in enumerate((
        ("u", u_hbm, uv),
        ("x0", x_hbm.at[pl.ds(0, head)], xv.at[pl.ds(0, head)]),
        ("x1", x_hbm.at[pl.ds(head, head)], xv.at[pl.ds(head, head)]),
        ("t", t_hbm, tv),
        ("d", d_hbm, dv),
        ("b", b_hbm, bv),
    )):
        loads[name] = pltpu.make_async_copy(src, dst, load_sem.at[i])
        loads[name].start()

    barrier = pltpu.get_barrier_semaphore()
    peers = [y_peer(j) for j in range(1, ny)] + [z_peer(j) for j in range(1, nz)] + [x_peer(j) for j in range(1, nx)]
    for peer in peers:
        pl.semaphore_signal(barrier, inc=1, device_id=peer, device_id_type=MESH)
    pl.semaphore_wait(barrier, len(peers))

    pair = y // 2
    outward = 2 * (y % 2) - 1

    def spread(src, dst, group):
        for k in range(1, 4):
            target = (y + k * outward + ny) % ny
            other = target // 2
            slot = (pair + other) % 2 + 2 * ((pair // 2 + other // 2) % 2)
            send(src.at[1], dst.at[slot], group, {"sub": z * ny + target})
        send(src.at[2], dst.at[4], group, y_peer(6))

    spread(t_hbm, rt, 1)

    def climb(base, levels):
        product = tv[base].astype(F32)
        chain = [product]
        for level in range(1, levels):
            product = times_exact(product, tv[base + level])
            chain.append(product)
        return chain

    def down(products, base, levels, doubled):
        parts = [bv[base]] * doubled
        for i in range(1, levels):
            high, low = split(times_exact(products[i - 1], bv[base + i]))
            parts += [high, high, low]
        return jnp.concatenate(parts, axis=1)

    def near_part(part, parts):
        size = vecs // parts
        at = pl.ds(part * size, size)
        near[:, at] = dot(dv[...], xv[:, at])

    loads["u"].wait()
    ut[...] = uv[...].T
    loads["x0"].wait()
    hat_t = dot(ut[:, :head], xv[:head, :])
    loads["x1"].wait()
    hat = (hat_t + dot(ut[:, head:], xv[head:, :])).T
    hat_high, hat_low = split(hat)
    loads["t"].wait()
    cy = dot(jnp.concatenate([hat_high, hat_low], axis=1), jnp.concatenate([tv[0], tv[0]], axis=0))
    cy_send[...] = cy.astype(BF)
    for j in range(1, ny):
        send(cy_send.at[rows(flip(y, j), yblk)], cy_recv.at[j], 0, y_peer(j))
    h_send[...] = hat_high

    tz = climb(ly, lz)
    wz[...] = up_weight(tz[lz - 1])
    rt[0] = tv[1]
    rt[5] = tv[2]
    loads["d"].wait()
    near_part(0, 2)
    wait_bytes(rt.at[pl.ds(1, 4)], recv_sem.at[1])
    lifts = []
    for quad in range(2):
        both = jnp.concatenate([rt[2 * quad], rt[2 * quad + 1]], axis=0)
        product = dot(both, rt[5 - quad])
        lifts += [product[:rank], product[rank:]]
    wy[...] = jnp.concatenate([up_weight(lift) for lift in lifts], axis=0)
    for r in range(4):
        high, low = split(lifts[r])
        vyl[r * rank:(r + 1) * rank, :] = jnp.concatenate([high, high, low], axis=1)

    wait_bytes(cy_recv.at[pl.ds(1, ny - 1)], recv_sem.at[0])
    blocks = [cy_send[rows(y, yblk), :]] + [cy_recv[j] for j in range(1, ny)]
    sums = [blocks[2 * r].astype(F32) + blocks[2 * r + 1].astype(F32) for r in range(4)]
    mid = dot(jnp.concatenate([wide(part) for part in sums], axis=1), wy[...])
    mid_w = wide(mid)
    cz_send[...] = dot(mid_w, wz[...])
    for j in range(1, nz):
        send(cz_send.at[rows(flip(z, j), zblk)], cz_recv.at[j], 3, z_peer(j))

    loads["b"].wait()
    spread(b_hbm, bt, 5)
    send(h_send, h_recv, 2, y_peer(1))
    zs_send[0] = mid.astype(BF)
    if lz > 1:
        wzl[...] = jnp.concatenate([up_exact(tv[ly])] + [up_weight(tz[i]) for i in range(1, lz - 1)], axis=1)
        zl = dot(mid_w, wzl[...])
        for i in range(lz - 1):
            zs_send[i + 1] = zl[:, i * rank:(i + 1) * rank].astype(BF)
    for j in range(1, nz):
        send(zs_send.at[level_of(j)], zs_recv.at[j], 4, z_peer(j))
    tx = climb(ly + lz, lx)
    if lx > 1:
        wxl[...] = jnp.concatenate([up_exact(tv[ly + lz])] + [up_weight(tx[i]) for i in range(1, lx - 1)], axis=1)

    wait_bytes(cz_recv.at[pl.ds(1, nz - 1)], recv_sem.at[3])
    top = cz_send[rows(z, zblk), :]
    for j in range(1, nz):
        top = top + cz_recv[j]
    x_send[0] = top
    if lx > 1:
        xl = dot(wide(top), wxl[...])
        for i in range(lx - 1):
            x_send[i + 1] = xl[:, i * rank:(i + 1) * rank]
    for j in range(1, nx):
        send(x_send.at[level_of(j)], x_recv.at[j], 6, x_peer(j))

    vx[...] = down(tx, ly + lz, lx, 2)
    quads = []
    for quad in range(2):
        left = jnp.concatenate([*split(sums[2 * quad]), *split(sums[2 * quad + 1])], axis=1)
        right = [rt[2 * quad]] * 2 + [rt[2 * quad + 1]] * 2
        quads.append(dot(left, jnp.concatenate(right, axis=0)))

    wait_bytes(x_recv.at[pl.ds(1, nx - 1)], recv_sem.at[6])
    parts = list(split(x_recv[1]))
    for level in range(1, lx):
        parts.append(wide(functools.reduce(jnp.add, [x_recv[j] for j in range(1 << level, 2 << level)])))
    far_z_send[...] = dot_nt(jnp.concatenate(parts, axis=1), vx[...])
    for j in range(1, nz):
        send(far_z_send, far_z.at[rows(z, zblk)], 7, z_peer(j))
    far_z[rows(z, zblk), :] = far_z_send[...]

    vz[...] = down(tz, ly, lz, 1)
    high, low = split(tz[lz - 1])
    vzl[...] = jnp.concatenate([high, high, low], axis=1)
    wait_bytes(zs_recv.at[pl.ds(1, nz - 1)], recv_sem.at[4])
    parts = [zs_recv[1]]
    for level in range(1, lz):
        parts.append(wide(functools.reduce(jnp.add, [zs_recv[j].astype(F32) for j in range(1 << level, 2 << level)])))
    mid_far = dot_nt(jnp.concatenate(parts, axis=1), vz[...])

    bt[0] = bv[1]
    bt[5] = bv[2]
    wait_bytes(bt.at[pl.ds(1, 4)], recv_sem.at[5])
    local = []
    for quad in range(2):
        both = jnp.concatenate([rt[2 * quad], rt[2 * quad + 1]], axis=0)
        high, low = split(dot(both, bt[5 - quad]))
        vy[...] = jnp.concatenate([high, high, low], axis=1)
        seen = dot_nt(wide(quads[1 - quad]), vy[...])
        for half in range(2):
            r = 2 * quad + half
            sibling = jnp.concatenate(split(sums[r ^ 1]), axis=1)
            local.append(seen[:, half * rank:(half + 1) * rank] + dot_nt(sibling, jnp.concatenate([bt[r]] * 2, axis=1)))
    local = jnp.concatenate(local, axis=1)

    wait_bytes(far_z.at[pl.ds(0, (nz - 1) * zblk)], recv_sem.at[7])
    mid_far = mid_far + dot_nt(wide(far_z[...]), vzl[...])
    pair_far = (local + dot_nt(wide(mid_far), vyl[...])).astype(BF)
    for r in range(4):
        far_y_send[r] = pair_far[:, r * rank:(r + 1) * rank]
    for j in range(1, ny):
        send(far_y_send.at[j // 2], far_y.at[rows(y, yblk)], 8, y_peer(j))
    far_y[rows(y, yblk), :] = far_y_send[0]

    near_part(1, 2)
    wait_bytes(h_recv, recv_sem.at[2])
    far = dot_nt(h_recv[...], bv[0])
    wait_bytes(far_y.at[pl.ds(0, (ny - 1) * yblk)], recv_sem.at[8])
    far_bf = (far + dot_nt(far_y[...], tv[0])).astype(BF)
    tile = leaf // 4
    stores = []
    for step in range(4):
        at = pl.ds(step * tile, tile)
        ov[at, :] = (near[at, :] + dot_nt(uv[at, :], far_bf)).astype(BF)
        store = pltpu.make_async_copy(ov.at[at], o_hbm.at[at], store_sem.at[step])
        store.start()
        stores.append(store)

    wait_bytes(cy_recv.at[pl.ds(1, ny - 1)], send_sem.at[0])
    wait_bytes(rt.at[pl.ds(1, 4)], send_sem.at[1])
    wait_bytes(h_send, send_sem.at[2])
    wait_bytes(cz_recv.at[pl.ds(1, nz - 1)], send_sem.at[3])
    wait_bytes(zs_recv.at[pl.ds(1, nz - 1)], send_sem.at[4])
    wait_bytes(bt.at[pl.ds(1, 4)], send_sem.at[5])
    wait_bytes(x_recv.at[pl.ds(1, nx - 1)], send_sem.at[6])
    wait_bytes(far_z.at[pl.ds(0, (nz - 1) * zblk)], send_sem.at[7])
    wait_bytes(far_y.at[pl.ds(0, (ny - 1) * yblk)], send_sem.at[8])
    for store in stores:
        store.wait()


def solution(mesh):
    ly = 3
    lz = mesh.shape["sub"].bit_length() - 1 - ly
    lx = mesh.shape["grp"].bit_length() - 1
    ny, nz, nx = 1 << ly, 1 << lz, 1 << lx

    def body(vectors, blocks, basis, transfer, coupling):
        leaf, vecs = vectors.shape[2:]
        rank = basis.shape[3]
        levels = transfer.shape[2]
        yblk, zblk = vecs // ny, vecs // ny // nz
        scratch = [
            pltpu.VMEM((leaf, vecs), BF),
            pltpu.VMEM((leaf, leaf), BF),
            pltpu.VMEM((leaf, rank), BF),
            pltpu.VMEM((rank, leaf), BF),
            pltpu.VMEM((levels, rank, rank), BF),
            pltpu.VMEM((levels, rank, rank), BF),
            pltpu.VMEM((leaf, vecs), F32),
            pltpu.VMEM((leaf, vecs), BF),
            pltpu.VMEM((6, rank, rank), BF),
            pltpu.VMEM((6, rank, rank), BF),
            pltpu.VMEM((12 * rank, rank), BF),
            pltpu.VMEM((2 * rank, 3 * rank), BF),
            pltpu.VMEM((4 * rank, 3 * rank), BF),
            pltpu.VMEM((3 * rank, rank), BF),
            pltpu.VMEM((3 * rank, max(1, lz - 1) * rank), BF),
            pltpu.VMEM((3 * rank, max(1, lx - 1) * rank), BF),
            pltpu.VMEM((rank, (3 * lz - 2) * rank), BF),
            pltpu.VMEM((rank, 3 * rank), BF),
            pltpu.VMEM((rank, (3 * lx - 1) * rank), BF),
            pltpu.VMEM((vecs, rank), BF),
            pltpu.VMEM((vecs, rank), BF),
            pltpu.VMEM((vecs, rank), BF),
            pltpu.VMEM((ny, yblk, rank), BF),
            pltpu.VMEM((yblk, rank), F32),
            pltpu.VMEM((nz, zblk, rank), F32),
            pltpu.VMEM((lz, yblk, rank), BF),
            pltpu.VMEM((nz, yblk, rank), BF),
            pltpu.VMEM((lx, zblk, rank), F32),
            pltpu.VMEM((nx, zblk, rank), F32),
            pltpu.VMEM((zblk, rank), F32),
            pltpu.VMEM((yblk, rank), F32),
            pltpu.VMEM((4, yblk, rank), BF),
            pltpu.VMEM((vecs, rank), BF),
            pltpu.SemaphoreType.DMA((6,)),
            pltpu.SemaphoreType.DMA((4,)),
            pltpu.SemaphoreType.DMA((9,)),
            pltpu.SemaphoreType.DMA((9,)),
        ]
        anywhere = pl.BlockSpec(memory_space=pl.ANY)
        out = pl.pallas_call(
            functools.partial(kernel, (lz, lx)),
            out_shape=jax.ShapeDtypeStruct((leaf, vecs), BF),
            in_specs=[pl.BlockSpec(memory_space=pltpu.HBM)] * 5,
            out_specs=anywhere,
            scratch_shapes=scratch,
            compiler_params=pltpu.CompilerParams(
                collective_id=0, has_side_effects=True, vmem_limit_bytes=48 * 1024 * 1024,
            ),
        )(*(pltpu.with_memory_space_constraint(whole[0, 0], pltpu.HBM) for whole in (vectors, blocks, basis, transfer, coupling)))
        return out[None, None]

    return jax.shard_map(
        body,
        mesh=mesh,
        in_specs=(
            P("grp", "sub", None, None),
            P("grp", "sub", None, None),
            P("grp", "sub", None, None),
            P("grp", "sub", None, None, None),
            P("grp", "sub", None, None, None),
        ),
        out_specs=P("grp", "sub", None, None),
        check_vma=False,
    )
```

```python
import functools

import jax
import jax.numpy as jnp
from jax import lax
from jax.experimental import pallas as pl
from jax.experimental.pallas import tpu as pltpu
from jax.sharding import PartitionSpec as P

MESH = pl.DeviceIdType.MESH
BF = jnp.bfloat16
F32 = jnp.float32


def dot(left, right):
    return jnp.dot(left, right, preferred_element_type=F32)


def dot_nt(left, right):
    return lax.dot_general(left, right, (((1,), (1,)), ((), ())), preferred_element_type=F32)


def dot_tn(left, right):
    return lax.dot_general(left, right, (((0,), (0,)), ((), ())), preferred_element_type=F32)


def split(value):
    high = value.astype(BF)
    return high, (value - high.astype(F32)).astype(BF)


def flip(index, offset):
    out = index
    for bit in range(offset.bit_length()):
        if offset >> bit & 1:
            out = out + (1 << bit) - (2 << bit) * lax.rem(lax.div(index, 1 << bit), 2)
    return out


def level_of(offset):
    return offset.bit_length() - 1


def wait_bytes(ref, sem):
    pltpu.make_async_copy(ref, ref, sem).wait()


def up_weight(product):
    high, low = split(product)
    return jnp.concatenate([high, high, low], axis=0)


def up_exact(matrix):
    return jnp.concatenate([matrix, matrix, jnp.zeros_like(matrix)], axis=0)


def wide(value):
    high, low = split(value)
    return jnp.concatenate([high, low, high], axis=1)


def times_exact(product, matrix):
    high, low = split(product)
    return dot(high, matrix) + dot(low, matrix)


def kernel(dims, x_hbm, d_hbm, u_hbm, t_hbm, b_hbm, o_hbm,
           xv, dv, uv, ut, tv, bv, near, ov,
           wy, wyl, wz, wzl, wxl, vy, vyl, vz, vzl, vx,
           h_send, h_recv, cy_send, cy_recv, cl_send, cl_recv, sl_send, sl_recv,
           cz_send, cz_recv, zs_send, zs_recv, x_send, x_recv,
           far_y_send, far_y,
           load_sem, store_sem, send_sem, recv_sem):
    ly, lz, lx = dims
    ny, nz, nx = 1 << ly, 1 << lz, 1 << lx
    leaf, vecs = x_hbm.shape
    yblk = vecs // ny
    sub, grp = lax.axis_index("sub"), lax.axis_index("grp")
    y, z = lax.rem(sub, ny), lax.div(sub, ny)

    def y_peer(j):
        return {"sub": z * ny + flip(y, j)}

    def z_peer(j):
        return {"sub": flip(z, j) * ny + y}

    def x_peer(j):
        return {"grp": flip(grp, j)}

    def rows(index, size):
        return pl.ds(pl.multiple_of(index * size, size), size)

    def send(src, dst, group, peer):
        pltpu.make_async_remote_copy(
            src_ref=src, dst_ref=dst, send_sem=send_sem.at[group], recv_sem=recv_sem.at[group],
            device_id=peer, device_id_type=MESH,
        ).start()

    head = leaf // 2
    loads = {}
    for i, (name, src, dst) in enumerate((
        ("t", t_hbm, tv),
        ("u", u_hbm, uv),
        ("x0", x_hbm.at[pl.ds(0, head)], xv.at[pl.ds(0, head)]),
        ("x1", x_hbm.at[pl.ds(head, head)], xv.at[pl.ds(head, head)]),
        ("b", b_hbm, bv),
        ("d", d_hbm, dv),
    )):
        loads[name] = pltpu.make_async_copy(src, dst, load_sem.at[i])
        loads[name].start()

    barrier = pltpu.get_barrier_semaphore()
    peers = [y_peer(j) for j in range(1, ny)] + [z_peer(j) for j in range(1, nz)] + [x_peer(j) for j in range(1, nx)]
    for peer in peers:
        pl.semaphore_signal(barrier, inc=1, device_id=peer, device_id_type=MESH)

    def climb(base, levels):
        product = tv[base].astype(F32)
        chain = [product]
        for level in range(1, levels):
            product = times_exact(product, tv[base + level])
            chain.append(product)
        return chain

    def down(products, base, levels):
        parts = [bv[base]]
        for i in range(1, levels):
            high, low = split(times_exact(products[i - 1], bv[base + i]))
            parts += [high, high, low] if base else [high, low]
        return jnp.concatenate(parts, axis=1)

    def near_part(part, parts):
        size = vecs // parts
        at = pl.ds(part * size, size)
        near[:, at] = dot(dv[...], xv[:, at])

    loads["t"].wait()
    ty = climb(0, ly)
    wy[...] = up_weight(ty[ly - 1])
    loads["u"].wait()
    ut[...] = uv[...].T

    loads["x0"].wait()
    hat_t = dot(ut[:, :head], xv[:head, :])
    loads["x1"].wait()
    hat = (hat_t + dot(ut[:, head:], xv[head:, :])).T
    hat_w = wide(hat)
    cy = dot(hat_w, wy[...])
    cy_send[...] = cy.astype(BF)
    pl.semaphore_wait(barrier, len(peers))
    for j in range(1, ny):
        send(cy_send.at[rows(flip(y, j), yblk)], cy_recv.at[j], 0, y_peer(j))

    wyl[...] = jnp.concatenate([up_exact(tv[0])] + [up_weight(ty[i]) for i in range(1, ly - 1)], axis=1)
    cl = dot(hat_w, wyl[...])
    for i in range(ly - 1):
        cl_send[i] = cl[:, i * 128:(i + 1) * 128].astype(BF)
    for j in range(1, ny):
        send(cl_send.at[:, rows(flip(y, j), yblk)], cl_recv.at[j], 1, y_peer(j))
    h_send[...] = hat.astype(BF)
    send(h_send, h_recv, 2, y_peer(1))
    tz = climb(ly, lz)
    wz[...] = up_weight(tz[lz - 1])

    if lz > 1:
        wzl[...] = jnp.concatenate([up_exact(tv[ly])] + [up_weight(tz[i]) for i in range(1, lz - 1)], axis=1)
    wait_bytes(cy_recv.at[pl.ds(1, ny - 1)], recv_sem.at[0])
    mid = cy_send[rows(y, yblk), :].astype(F32)
    for j in range(1, ny):
        mid = mid + cy_recv[j].astype(F32)
    mid_w = wide(mid)
    cz = dot(mid_w, wz[...])
    cz_send[...] = cz.astype(BF)
    for j in range(1, nz):
        send(cz_send, cz_recv.at[j], 3, z_peer(j))
    zs_send[0] = mid.astype(BF)
    if lz > 1:
        zl = dot(mid_w, wzl[...])
        for i in range(lz - 1):
            zs_send[i + 1] = zl[:, i * 128:(i + 1) * 128].astype(BF)
    for j in range(1, nz):
        send(zs_send.at[level_of(j)], zs_recv.at[j], 4, z_peer(j))

    wait_bytes(cl_recv.at[pl.ds(1, ny - 1)], recv_sem.at[1])
    for i in range(ly - 1):
        level = i + 1
        own = cl_send[i, rows(y, yblk), :].astype(F32)
        parts = [own] + [cl_recv[j, i].astype(F32) for j in range(1, ny)]
        sums = []
        for node in range(ny >> level):
            sums.append(functools.reduce(jnp.add, parts[node << level:(node + 1) << level]).astype(BF))
        for pair in range(ny // 2):
            sl_send[pair, i] = sums[(pair >> (level - 1)) ^ 1]
    for j in range(1, ny):
        send(sl_send.at[j // 2], sl_recv.at[:, rows(y, yblk)], 5, y_peer(j))
    sl_recv[:, rows(y, yblk), :] = sl_send[0]
    tx = climb(ly + lz, lx)
    if lx > 1:
        wxl[...] = jnp.concatenate([up_exact(tv[ly + lz])] + [up_weight(tx[i]) for i in range(1, lx - 1)], axis=1)
    loads["b"].wait()
    vx[...] = down(tx, ly + lz, lx)
    loads["d"].wait()
    near_part(0, 2)

    wait_bytes(cz_recv.at[pl.ds(1, nz - 1)], recv_sem.at[3])
    top = cz
    for j in range(1, nz):
        top = top + cz_recv[j].astype(F32)
    x_send[0] = top.astype(BF)
    if lx > 1:
        xl = dot(wide(top), wxl[...])
        for i in range(lx - 1):
            x_send[i + 1] = xl[:, i * 128:(i + 1) * 128].astype(BF)
    for j in range(1, nx):
        send(x_send.at[level_of(j)], x_recv.at[j], 6, x_peer(j))

    vz[...] = down(tz, ly, lz)
    high, low = split(tz[lz - 1])
    vzl[...] = jnp.concatenate([high, high, low], axis=1)
    wait_bytes(zs_recv.at[pl.ds(1, nz - 1)], recv_sem.at[4])
    parts = [zs_recv[1]]
    for level in range(1, lz):
        parts.append(wide(functools.reduce(jnp.add, [zs_recv[j].astype(F32) for j in range(1 << level, 2 << level)])))
    mid_far = dot_nt(jnp.concatenate(parts, axis=1), vz[...])

    wait_bytes(x_recv.at[pl.ds(1, nx - 1)], recv_sem.at[6])
    parts = [x_recv[1]]
    for level in range(1, lx):
        parts.append(wide(functools.reduce(jnp.add, [x_recv[j].astype(F32) for j in range(1 << level, 2 << level)])))
    top_far = dot_nt(jnp.concatenate(parts, axis=1), vx[...])
    mid_far = mid_far + dot_nt(wide(top_far), vzl[...])
    far_y_send[...] = mid_far.astype(BF)
    for j in range(1, ny):
        send(far_y_send, far_y.at[rows(y, yblk)], 7, y_peer(j))
    far_y[rows(y, yblk), :] = far_y_send[...]

    vy[...] = down(ty, 0, ly)
    high, low = split(ty[ly - 1])
    vyl[...] = jnp.concatenate([high, low], axis=1)
    wait_bytes(h_recv, recv_sem.at[2])
    wait_bytes(sl_recv.at[:, pl.ds(0, (ny - 1) * yblk)], recv_sem.at[5])
    parts = [h_recv[...]]
    for i in range(ly - 1):
        parts += [sl_recv[i]] * 2
    far = dot_nt(jnp.concatenate(parts, axis=1), vy[...])
    near_part(1, 2)
    wait_bytes(far_y.at[pl.ds(0, (ny - 1) * yblk)], recv_sem.at[7])
    last = far_y[...]
    far_bf = (far + dot_nt(jnp.concatenate([last, last], axis=1), vyl[...])).astype(BF)
    tile = leaf // 4
    stores = []
    for step in range(4):
        at = pl.ds(step * tile, tile)
        ov[at, :] = (near[at, :] + dot_nt(uv[at, :], far_bf)).astype(BF)
        store = pltpu.make_async_copy(ov.at[at], o_hbm.at[at], store_sem.at[step])
        store.start()
        stores.append(store)

    wait_bytes(cy_send.at[pl.ds(0, (ny - 1) * yblk)], send_sem.at[0])
    wait_bytes(cl_send.at[:, pl.ds(0, (ny - 1) * yblk)], send_sem.at[1])
    wait_bytes(h_send, send_sem.at[2])
    wait_bytes(cz_recv.at[pl.ds(1, nz - 1)], send_sem.at[3])
    wait_bytes(zs_recv.at[pl.ds(1, nz - 1)], send_sem.at[4])
    wait_bytes(sl_recv.at[:, pl.ds(0, (ny - 1) * yblk)], send_sem.at[5])
    wait_bytes(x_recv.at[pl.ds(1, nx - 1)], send_sem.at[6])
    wait_bytes(far_y.at[pl.ds(0, (ny - 1) * yblk)], send_sem.at[7])
    for store in stores:
        store.wait()


def solution(mesh):
    sub_levels = mesh.shape["sub"].bit_length() - 1
    ly = (sub_levels + 1) // 2
    lz = sub_levels - ly
    lx = mesh.shape["grp"].bit_length() - 1
    dims = (ly, lz, lx)
    ny, nz, nx = 1 << ly, 1 << lz, 1 << lx

    def body(vectors, blocks, basis, transfer, coupling):
        leaf, vecs = vectors.shape[2:]
        rank = basis.shape[3]
        levels = transfer.shape[2]
        yblk = vecs // ny
        scratch = [
            pltpu.VMEM((leaf, vecs), BF),
            pltpu.VMEM((leaf, leaf), BF),
            pltpu.VMEM((leaf, rank), BF),
            pltpu.VMEM((rank, leaf), BF),
            pltpu.VMEM((levels, rank, rank), BF),
            pltpu.VMEM((levels, rank, rank), BF),
            pltpu.VMEM((leaf, vecs), F32),
            pltpu.VMEM((leaf, vecs), BF),
            pltpu.VMEM((3 * rank, rank), BF),
            pltpu.VMEM((3 * rank, max(1, ly - 1) * rank), BF),
            pltpu.VMEM((3 * rank, rank), BF),
            pltpu.VMEM((3 * rank, max(1, lz - 1) * rank), BF),
            pltpu.VMEM((3 * rank, max(1, lx - 1) * rank), BF),
            pltpu.VMEM((rank, (2 * ly - 1) * rank), BF),
            pltpu.VMEM((rank, 2 * rank), BF),
            pltpu.VMEM((rank, (3 * lz - 2) * rank), BF),
            pltpu.VMEM((rank, 3 * rank), BF),
            pltpu.VMEM((rank, (3 * lx - 2) * rank), BF),
            pltpu.VMEM((vecs, rank), BF),
            pltpu.VMEM((vecs, rank), BF),
            pltpu.VMEM((vecs, rank), BF),
            pltpu.VMEM((ny, yblk, rank), BF),
            pltpu.VMEM((ly - 1, vecs, rank), BF),
            pltpu.VMEM((ny, ly - 1, yblk, rank), BF),
            pltpu.VMEM((ny // 2, ly - 1, yblk, rank), BF),
            pltpu.VMEM((ly - 1, vecs, rank), BF),
            pltpu.VMEM((yblk, rank), BF),
            pltpu.VMEM((nz, yblk, rank), BF),
            pltpu.VMEM((lz, yblk, rank), BF),
            pltpu.VMEM((nz, yblk, rank), BF),
            pltpu.VMEM((lx, yblk, rank), BF),
            pltpu.VMEM((nx, yblk, rank), BF),
            pltpu.VMEM((yblk, rank), BF),
            pltpu.VMEM((vecs, rank), BF),
            pltpu.SemaphoreType.DMA((6,)),
            pltpu.SemaphoreType.DMA((4,)),
            pltpu.SemaphoreType.DMA((8,)),
            pltpu.SemaphoreType.DMA((8,)),
        ]
        anywhere = pl.BlockSpec(memory_space=pl.ANY)
        out = pl.pallas_call(
            functools.partial(kernel, dims),
            out_shape=jax.ShapeDtypeStruct((leaf, vecs), BF),
            in_specs=[pl.BlockSpec(memory_space=pltpu.HBM)] * 5,
            out_specs=anywhere,
            scratch_shapes=scratch,
            compiler_params=pltpu.CompilerParams(
                collective_id=0, has_side_effects=True, vmem_limit_bytes=48 * 1024 * 1024,
            ),
        )(*(pltpu.with_memory_space_constraint(whole[0, 0], pltpu.HBM) for whole in (vectors, blocks, basis, transfer, coupling)))
        return out[None, None]

    return jax.shard_map(
        body,
        mesh=mesh,
        in_specs=(
            P("grp", "sub", None, None),
            P("grp", "sub", None, None),
            P("grp", "sub", None, None),
            P("grp", "sub", None, None, None),
            P("grp", "sub", None, None, None),
        ),
        out_specs=P("grp", "sub", None, None),
        check_vma=False,
    )
```

```python
import functools

import jax
import jax.numpy as jnp
from jax import lax
from jax.experimental import pallas as pl
from jax.experimental.pallas import tpu as pltpu
from jax.sharding import PartitionSpec as P

MESH = pl.DeviceIdType.MESH
BF = jnp.bfloat16
F32 = jnp.float32


def dot(left, right):
    return jnp.dot(left, right, preferred_element_type=F32)


def dot_nt(left, right):
    return lax.dot_general(left, right, (((1,), (1,)), ((), ())), preferred_element_type=F32)


def dot_tn(left, right):
    return lax.dot_general(left, right, (((0,), (0,)), ((), ())), preferred_element_type=F32)


def split(value):
    high = value.astype(BF)
    return high, (value - high.astype(F32)).astype(BF)


def flip(index, offset):
    out = index
    for bit in range(offset.bit_length()):
        if offset >> bit & 1:
            out = out + (1 << bit) - (2 << bit) * lax.rem(lax.div(index, 1 << bit), 2)
    return out


def level_of(offset):
    return offset.bit_length() - 1


def wait_bytes(ref, sem):
    pltpu.make_async_copy(ref, ref, sem).wait()


def up_weight(product):
    high, low = split(product)
    return jnp.concatenate([high, high, low], axis=0)


def up_exact(matrix):
    return jnp.concatenate([matrix, matrix, jnp.zeros_like(matrix)], axis=0)


def wide(value):
    high, low = split(value)
    return jnp.concatenate([high, low, high], axis=1)


def times_exact(product, matrix):
    high, low = split(product)
    return dot(high, matrix) + dot(low, matrix)


def leaf_kernel(dims, x_hbm, u_hbm, t_hbm, b_hbm,
                cy_out, cl_out, h_out, wz, wzl, wxl, vy, vyl, vz, vzl, vx,
                xv, uv, ut, tv, bv, wy, wyl, load_sem):
    ly, lz, lx = dims
    leaf = x_hbm.shape[0]
    head = leaf // 2
    loads = {}
    for i, (name, src, dst) in enumerate((
        ("t", t_hbm, tv),
        ("u", u_hbm, uv),
        ("x0", x_hbm.at[pl.ds(0, head)], xv.at[pl.ds(0, head)]),
        ("x1", x_hbm.at[pl.ds(head, head)], xv.at[pl.ds(head, head)]),
        ("b", b_hbm, bv),
    )):
        loads[name] = pltpu.make_async_copy(src, dst, load_sem.at[i])
        loads[name].start()

    def climb(base, levels):
        product = tv[base].astype(F32)
        chain = [product]
        for level in range(1, levels):
            product = times_exact(product, tv[base + level])
            chain.append(product)
        return chain

    def down(products, base, levels):
        parts = [bv[base]]
        for i in range(1, levels):
            high, low = split(times_exact(products[i - 1], bv[base + i]))
            parts += [high, high, low] if base else [high, low]
        return jnp.concatenate(parts, axis=1)

    loads["t"].wait()
    ty, tz, tx = climb(0, ly), climb(ly, lz), climb(ly + lz, lx)
    wy[...] = up_weight(ty[ly - 1])
    wyl[...] = jnp.concatenate([up_exact(tv[0])] + [up_weight(ty[i]) for i in range(1, ly - 1)], axis=1)
    wz[...] = up_weight(tz[lz - 1])
    if lz > 1:
        wzl[...] = jnp.concatenate([up_exact(tv[ly])] + [up_weight(tz[i]) for i in range(1, lz - 1)], axis=1)
    if lx > 1:
        wxl[...] = jnp.concatenate([up_exact(tv[ly + lz])] + [up_weight(tx[i]) for i in range(1, lx - 1)], axis=1)
    high, low = split(tz[lz - 1])
    vzl[...] = jnp.concatenate([high, high, low], axis=1)
    high, low = split(ty[ly - 1])
    vyl[...] = jnp.concatenate([high, low], axis=1)

    loads["u"].wait()
    ut[...] = uv[...].T
    loads["b"].wait()
    vx[...] = down(tx, ly + lz, lx)
    vz[...] = down(tz, ly, lz)
    vy[...] = down(ty, 0, ly)

    loads["x0"].wait()
    hat_t = dot(ut[:, :head], xv[:head, :])
    loads["x1"].wait()
    hat = (hat_t + dot(ut[:, head:], xv[head:, :])).T
    hat_w = wide(hat)
    cy_out[...] = dot(hat_w, wy[...]).astype(BF)
    cl = dot(hat_w, wyl[...])
    for i in range(ly - 1):
        cl_out[i] = cl[:, i * 128:(i + 1) * 128].astype(BF)
    h_out[...] = hat.astype(BF)


def kernel(dims, x_hbm, d_hbm, cy_send, cl_send, h_send, wz, wzl, wxl, vy, vyl, vz, vzl, vx, near, far_out,
           xv, dv,
           h_recv, cy_recv, cl_recv, sl_send, sl_recv,
           cz_send, cz_recv, zs_send, zs_recv, x_send, x_recv,
           far_y_send, far_y,
           load_sem, send_sem, recv_sem):
    ly, lz, lx = dims
    ny, nz, nx = 1 << ly, 1 << lz, 1 << lx
    leaf, vecs = x_hbm.shape
    yblk = vecs // ny
    sub, grp = lax.axis_index("sub"), lax.axis_index("grp")
    y, z = lax.rem(sub, ny), lax.div(sub, ny)

    def y_peer(j):
        return {"sub": z * ny + flip(y, j)}

    def z_peer(j):
        return {"sub": flip(z, j) * ny + y}

    def x_peer(j):
        return {"grp": flip(grp, j)}

    def rows(index, size):
        return pl.ds(pl.multiple_of(index * size, size), size)

    def send(src, dst, group, peer):
        pltpu.make_async_remote_copy(
            src_ref=src, dst_ref=dst, send_sem=send_sem.at[group], recv_sem=recv_sem.at[group],
            device_id=peer, device_id_type=MESH,
        ).start()

    def near_part(part, parts):
        size = vecs // parts
        at = pl.ds(part * size, size)
        near[:, at] = dot(dv[...], xv[:, at])

    barrier = pltpu.get_barrier_semaphore()
    peers = [y_peer(j) for j in range(1, ny)] + [z_peer(j) for j in range(1, nz)] + [x_peer(j) for j in range(1, nx)]
    for peer in peers:
        pl.semaphore_signal(barrier, inc=1, device_id=peer, device_id_type=MESH)
    loads = {}
    for i, (name, src, dst) in enumerate((("x", x_hbm, xv), ("d", d_hbm, dv))):
        loads[name] = pltpu.make_async_copy(src, dst, load_sem.at[i])
        loads[name].start()
    pl.semaphore_wait(barrier, len(peers))
    for j in range(1, ny):
        send(cy_send.at[rows(flip(y, j), yblk)], cy_recv.at[j], 0, y_peer(j))
    for j in range(1, ny):
        send(cl_send.at[:, rows(flip(y, j), yblk)], cl_recv.at[j], 1, y_peer(j))
    send(h_send, h_recv, 2, y_peer(1))

    wait_bytes(cy_recv.at[pl.ds(1, ny - 1)], recv_sem.at[0])
    mid = cy_send[rows(y, yblk), :].astype(F32)
    for j in range(1, ny):
        mid = mid + cy_recv[j].astype(F32)
    mid_w = wide(mid)
    cz = dot(mid_w, wz[...])
    cz_send[...] = cz.astype(BF)
    for j in range(1, nz):
        send(cz_send, cz_recv.at[j], 3, z_peer(j))
    zs_send[0] = mid.astype(BF)
    if lz > 1:
        zl = dot(mid_w, wzl[...])
        for i in range(lz - 1):
            zs_send[i + 1] = zl[:, i * 128:(i + 1) * 128].astype(BF)
    for j in range(1, nz):
        send(zs_send.at[level_of(j)], zs_recv.at[j], 4, z_peer(j))

    wait_bytes(cl_recv.at[pl.ds(1, ny - 1)], recv_sem.at[1])
    for i in range(ly - 1):
        level = i + 1
        own = cl_send[i, rows(y, yblk), :].astype(F32)
        parts = [own] + [cl_recv[j, i].astype(F32) for j in range(1, ny)]
        sums = []
        for node in range(ny >> level):
            sums.append(functools.reduce(jnp.add, parts[node << level:(node + 1) << level]).astype(BF))
        for pair in range(ny // 2):
            sl_send[pair, i] = sums[(pair >> (level - 1)) ^ 1]
    for j in range(1, ny):
        send(sl_send.at[j // 2], sl_recv.at[:, rows(y, yblk)], 5, y_peer(j))
    sl_recv[:, rows(y, yblk), :] = sl_send[0]
    loads["x"].wait()
    loads["d"].wait()
    near_part(0, 2)

    wait_bytes(cz_recv.at[pl.ds(1, nz - 1)], recv_sem.at[3])
    top = cz
    for j in range(1, nz):
        top = top + cz_recv[j].astype(F32)
    x_send[0] = top.astype(BF)
    if lx > 1:
        xl = dot(wide(top), wxl[...])
        for i in range(lx - 1):
            x_send[i + 1] = xl[:, i * 128:(i + 1) * 128].astype(BF)
    for j in range(1, nx):
        send(x_send.at[level_of(j)], x_recv.at[j], 6, x_peer(j))

    wait_bytes(zs_recv.at[pl.ds(1, nz - 1)], recv_sem.at[4])
    parts = [zs_recv[1]]
    for level in range(1, lz):
        parts.append(wide(functools.reduce(jnp.add, [zs_recv[j].astype(F32) for j in range(1 << level, 2 << level)])))
    mid_far = dot_nt(jnp.concatenate(parts, axis=1), vz[...])

    wait_bytes(x_recv.at[pl.ds(1, nx - 1)], recv_sem.at[6])
    parts = [x_recv[1]]
    for level in range(1, lx):
        parts.append(wide(functools.reduce(jnp.add, [x_recv[j].astype(F32) for j in range(1 << level, 2 << level)])))
    top_far = dot_nt(jnp.concatenate(parts, axis=1), vx[...])
    mid_far = mid_far + dot_nt(wide(top_far), vzl[...])
    far_y_send[...] = mid_far.astype(BF)
    for j in range(1, ny):
        send(far_y_send, far_y.at[rows(y, yblk)], 7, y_peer(j))
    far_y[rows(y, yblk), :] = far_y_send[...]

    wait_bytes(h_recv, recv_sem.at[2])
    wait_bytes(sl_recv.at[:, pl.ds(0, (ny - 1) * yblk)], recv_sem.at[5])
    parts = [h_recv[...]]
    for i in range(ly - 1):
        parts += [sl_recv[i]] * 2
    far = dot_nt(jnp.concatenate(parts, axis=1), vy[...])
    near_part(1, 2)
    wait_bytes(far_y.at[pl.ds(0, (ny - 1) * yblk)], recv_sem.at[7])
    last = far_y[...]
    far_out[...] = (far + dot_nt(jnp.concatenate([last, last], axis=1), vyl[...])).astype(BF)

    wait_bytes(cy_send.at[pl.ds(0, (ny - 1) * yblk)], send_sem.at[0])
    wait_bytes(cl_send.at[:, pl.ds(0, (ny - 1) * yblk)], send_sem.at[1])
    wait_bytes(h_send, send_sem.at[2])
    wait_bytes(cz_recv.at[pl.ds(1, nz - 1)], send_sem.at[3])
    wait_bytes(zs_recv.at[pl.ds(1, nz - 1)], send_sem.at[4])
    wait_bytes(sl_recv.at[:, pl.ds(0, (ny - 1) * yblk)], send_sem.at[5])
    wait_bytes(x_recv.at[pl.ds(1, nx - 1)], send_sem.at[6])
    wait_bytes(far_y.at[pl.ds(0, (ny - 1) * yblk)], send_sem.at[7])


def solution(mesh):
    sub_levels = mesh.shape["sub"].bit_length() - 1
    ly = (sub_levels + 1) // 2
    lz = sub_levels - ly
    lx = mesh.shape["grp"].bit_length() - 1
    dims = (ly, lz, lx)
    ny, nz, nx = 1 << ly, 1 << lz, 1 << lx
    vmem = pl.BlockSpec(memory_space=pltpu.VMEM)
    hbm = pl.BlockSpec(memory_space=pltpu.HBM)

    def body(vectors, blocks, basis, transfer, coupling):
        leaf, vecs = vectors.shape[2:]
        rank = basis.shape[3]
        levels = transfer.shape[2]
        yblk = vecs // ny
        x, d, u, t, b = (
            pltpu.with_memory_space_constraint(whole[0, 0], pltpu.HBM)
            for whole in (vectors, blocks, basis, transfer, coupling)
        )
        shapes = [
            (vecs, rank),
            (ly - 1, vecs, rank),
            (vecs, rank),
            (3 * rank, rank),
            (3 * rank, max(1, lz - 1) * rank),
            (3 * rank, max(1, lx - 1) * rank),
            (rank, (2 * ly - 1) * rank),
            (rank, 2 * rank),
            (rank, (3 * lz - 2) * rank),
            (rank, 3 * rank),
            (rank, (3 * lx - 2) * rank),
        ]
        own = pl.pallas_call(
            functools.partial(leaf_kernel, dims),
            out_shape=[jax.ShapeDtypeStruct(shape, BF) for shape in shapes],
            in_specs=[hbm] * 4,
            out_specs=[vmem] * len(shapes),
            scratch_shapes=[
                pltpu.VMEM((leaf, vecs), BF),
                pltpu.VMEM((leaf, rank), BF),
                pltpu.VMEM((rank, leaf), BF),
                pltpu.VMEM((levels, rank, rank), BF),
                pltpu.VMEM((levels, rank, rank), BF),
                pltpu.VMEM((3 * rank, rank), BF),
                pltpu.VMEM((3 * rank, max(1, ly - 1) * rank), BF),
                pltpu.SemaphoreType.DMA((5,)),
            ],
            compiler_params=pltpu.CompilerParams(vmem_limit_bytes=24 * 1024 * 1024),
        )(x, u, t, b)
        near, far = pl.pallas_call(
            functools.partial(kernel, dims),
            out_shape=[jax.ShapeDtypeStruct((leaf, vecs), F32), jax.ShapeDtypeStruct((vecs, rank), BF)],
            in_specs=[hbm] * 2 + [vmem] * len(shapes),
            out_specs=[vmem] * 2,
            scratch_shapes=[
                pltpu.VMEM((leaf, vecs), BF),
                pltpu.VMEM((leaf, leaf), BF),
                pltpu.VMEM((vecs, rank), BF),
                pltpu.VMEM((ny, yblk, rank), BF),
                pltpu.VMEM((ny, ly - 1, yblk, rank), BF),
                pltpu.VMEM((ny // 2, ly - 1, yblk, rank), BF),
                pltpu.VMEM((ly - 1, vecs, rank), BF),
                pltpu.VMEM((yblk, rank), BF),
                pltpu.VMEM((nz, yblk, rank), BF),
                pltpu.VMEM((lz, yblk, rank), BF),
                pltpu.VMEM((nz, yblk, rank), BF),
                pltpu.VMEM((lx, yblk, rank), BF),
                pltpu.VMEM((nx, yblk, rank), BF),
                pltpu.VMEM((yblk, rank), BF),
                pltpu.VMEM((vecs, rank), BF),
                pltpu.SemaphoreType.DMA((2,)),
                pltpu.SemaphoreType.DMA((8,)),
                pltpu.SemaphoreType.DMA((8,)),
            ],
            compiler_params=pltpu.CompilerParams(
                collective_id=0, has_side_effects=True, vmem_limit_bytes=24 * 1024 * 1024,
            ),
        )(x, d, *own)
        out = near + dot_nt(basis[0, 0], far)
        return out.astype(BF)[None, None]

    return jax.shard_map(
        body,
        mesh=mesh,
        in_specs=(
            P("grp", "sub", None, None),
            P("grp", "sub", None, None),
            P("grp", "sub", None, None),
            P("grp", "sub", None, None, None),
            P("grp", "sub", None, None, None),
        ),
        out_specs=P("grp", "sub", None, None),
        check_vma=False,
    )
```

```python
import functools

import jax
import jax.numpy as jnp
from jax import lax
from jax.experimental import pallas as pl
from jax.experimental.pallas import tpu as pltpu
from jax.sharding import PartitionSpec as P

MESH = pl.DeviceIdType.MESH
BF = jnp.bfloat16
F32 = jnp.float32


def dot(left, right):
    return jnp.dot(left, right, preferred_element_type=F32)


def dot_nt(left, right):
    return lax.dot_general(left, right, (((1,), (1,)), ((), ())), preferred_element_type=F32)


def dot_tn(left, right):
    return lax.dot_general(left, right, (((0,), (0,)), ((), ())), preferred_element_type=F32)


def split(value):
    high = value.astype(BF)
    return high, (value - high.astype(F32)).astype(BF)


def flip(index, offset):
    out = index
    for bit in range(offset.bit_length()):
        if offset >> bit & 1:
            out = out + (1 << bit) - (2 << bit) * lax.rem(lax.div(index, 1 << bit), 2)
    return out


def level_of(offset):
    return offset.bit_length() - 1


def far_first(count):
    return [j for j in (4, 5, 3, 7, 6, 2, 1) if j < count]


def wait_bytes(ref, sem):
    pltpu.make_async_copy(ref, ref, sem).wait()


def up_weight(product):
    high, low = split(product)
    return jnp.concatenate([high, high, low], axis=0)


def up_exact(matrix):
    return jnp.concatenate([matrix, matrix, jnp.zeros_like(matrix)], axis=0)


def wide(value):
    high, low = split(value)
    return jnp.concatenate([high, low, high], axis=1)


def times_exact(product, matrix):
    high, low = split(product)
    return dot(high, matrix) + dot(low, matrix)


def kernel(dims, x_hbm, d_hbm, u_hbm, t_hbm, b_hbm, near, far_out,
           xv, dv, uv, ut, tv, bv,
           rt, bt, wy, vy, vyl, wz, wzl, wxl, vz, vzl, vx,
           h_send, h_recv, cy_send, cy_recv,
           cz_send, cz_recv, zs_send, zs_recv, x_send, x_recv,
           far_y_send, far_y,
           load_sem, send_sem, recv_sem):
    lz, lx = dims
    ly = 3
    ny, nz, nx = 1 << ly, 1 << lz, 1 << lx
    leaf, vecs = x_hbm.shape
    rank = u_hbm.shape[1]
    yblk = vecs // ny
    sub, grp = lax.axis_index("sub"), lax.axis_index("grp")
    y, z = lax.rem(sub, ny), lax.div(sub, ny)

    def y_peer(j):
        return {"sub": z * ny + flip(y, j)}

    def z_peer(j):
        return {"sub": flip(z, j) * ny + y}

    def x_peer(j):
        return {"grp": flip(grp, j)}

    def rows(index, size):
        return pl.ds(pl.multiple_of(index * size, size), size)

    def send(src, dst, group, peer):
        pltpu.make_async_remote_copy(
            src_ref=src, dst_ref=dst, send_sem=send_sem.at[group], recv_sem=recv_sem.at[group],
            device_id=peer, device_id_type=MESH,
        ).start()

    barrier = pltpu.get_barrier_semaphore()
    peers = [z_peer(j) for j in far_first(nz)] + [x_peer(j) for j in far_first(nx)] + [y_peer(j) for j in far_first(ny)]
    for peer in peers:
        pl.semaphore_signal(barrier, inc=1, device_id=peer, device_id_type=MESH)

    head = leaf // 2
    loads = {}
    for i, (name, src, dst) in enumerate((
        ("u", u_hbm, uv),
        ("x0", x_hbm.at[pl.ds(0, head)], xv.at[pl.ds(0, head)]),
        ("x1", x_hbm.at[pl.ds(head, head)], xv.at[pl.ds(head, head)]),
        ("t", t_hbm, tv),
        ("d", d_hbm, dv),
        ("b", b_hbm, bv),
    )):
        loads[name] = pltpu.make_async_copy(src, dst, load_sem.at[i])
        loads[name].start()

    pl.semaphore_wait(barrier, len(peers))

    pair = lax.div(y, 2)
    outward = 2 * lax.rem(y, 2) - 1

    def spread(src, dst, group):
        for k in (3, 2, 1):
            target = lax.rem(y + k * outward + ny, ny)
            other = lax.div(target, 2)
            slot = lax.rem(pair + other, 2) + 2 * lax.rem(lax.div(pair, 2) + lax.div(other, 2), 2)
            send(src.at[1], dst.at[slot], group, {"sub": z * ny + target})
        send(src.at[2], dst.at[4], group, y_peer(6))

    spread(t_hbm, rt, 1)

    def climb(base, levels):
        product = tv[base].astype(F32)
        chain = [product]
        for level in range(1, levels):
            product = times_exact(product, tv[base + level])
            chain.append(product)
        return chain

    def down(products, base, levels):
        parts = [bv[base]]
        for i in range(1, levels):
            high, low = split(times_exact(products[i - 1], bv[base + i]))
            parts += [high, high, low]
        return jnp.concatenate(parts, axis=1)

    def near_part(part, parts):
        size = vecs // parts
        at = pl.ds(part * size, size)
        near[:, at] = dot(dv[...], xv[:, at])

    loads["u"].wait()
    ut[...] = uv[...].T
    loads["x0"].wait()
    hat_t = dot(ut[:, :head], xv[:head, :])
    loads["x1"].wait()
    hat = (hat_t + dot(ut[:, head:], xv[head:, :])).T
    hat_high, hat_low = split(hat)
    loads["t"].wait()
    cy = dot(jnp.concatenate([hat_high, hat_low], axis=1), jnp.concatenate([tv[0], tv[0]], axis=0))
    cy_send[...] = cy.astype(BF)
    for j in far_first(ny):
        send(cy_send.at[rows(flip(y, j), yblk)], cy_recv.at[j], 0, y_peer(j))
    h_send[...] = hat_high

    tz = climb(ly, lz)
    wz[...] = up_weight(tz[lz - 1])
    rt[0] = tv[1]
    rt[5] = tv[2]
    loads["d"].wait()
    near_part(0, 2)
    wait_bytes(rt.at[pl.ds(1, 4)], recv_sem.at[1])
    lifts = []
    for quad in range(2):
        both = jnp.concatenate([rt[2 * quad], rt[2 * quad + 1]], axis=0)
        product = dot(both, rt[5 - quad])
        lifts += [product[:rank], product[rank:]]
    wy[...] = jnp.concatenate([up_weight(lift) for lift in lifts], axis=0)
    for r in range(4):
        high, low = split(lifts[r])
        vyl[r * rank:(r + 1) * rank, :] = jnp.concatenate([high, high, low], axis=1)

    wait_bytes(cy_recv.at[pl.ds(1, ny - 1)], recv_sem.at[0])
    blocks = [cy_send[rows(y, yblk), :]] + [cy_recv[j] for j in range(1, ny)]
    sums = [blocks[2 * r].astype(F32) + blocks[2 * r + 1].astype(F32) for r in range(4)]
    mid = dot(jnp.concatenate([wide(part) for part in sums], axis=1), wy[...])
    mid_w = wide(mid)
    cz = dot(mid_w, wz[...])
    cz_send[...] = cz.astype(BF)
    for j in far_first(nz):
        send(cz_send, cz_recv.at[j], 3, z_peer(j))

    zs_send[0] = mid.astype(BF)
    if lz > 1:
        wzl[...] = jnp.concatenate([up_exact(tv[ly])] + [up_weight(tz[i]) for i in range(1, lz - 1)], axis=1)
        zl = dot(mid_w, wzl[...])
        for i in range(lz - 1):
            zs_send[i + 1] = zl[:, i * rank:(i + 1) * rank].astype(BF)
    for j in far_first(nz):
        send(zs_send.at[level_of(j)], zs_recv.at[j], 4, z_peer(j))
    spread(b_hbm, bt, 5)
    send(h_send, h_recv, 2, y_peer(1))
    tx = climb(ly + lz, lx)
    if lx > 1:
        wxl[...] = jnp.concatenate([up_exact(tv[ly + lz])] + [up_weight(tx[i]) for i in range(1, lx - 1)], axis=1)
    loads["b"].wait()
    vx[...] = down(tx, ly + lz, lx)
    quads = []
    for quad in range(2):
        left = jnp.concatenate([*split(sums[2 * quad]), *split(sums[2 * quad + 1])], axis=1)
        right = [rt[2 * quad]] * 2 + [rt[2 * quad + 1]] * 2
        quads.append(dot(left, jnp.concatenate(right, axis=0)))

    wait_bytes(cz_recv.at[pl.ds(1, nz - 1)], recv_sem.at[3])
    top = cz
    for j in range(1, nz):
        top = top + cz_recv[j].astype(F32)
    x_send[0] = top.astype(BF)
    if lx > 1:
        xl = dot(wide(top), wxl[...])
        for i in range(lx - 1):
            x_send[i + 1] = xl[:, i * rank:(i + 1) * rank].astype(BF)
    for j in far_first(nx):
        send(x_send.at[level_of(j)], x_recv.at[j], 6, x_peer(j))

    vz[...] = down(tz, ly, lz)
    high, low = split(tz[lz - 1])
    vzl[...] = jnp.concatenate([high, high, low], axis=1)
    wait_bytes(zs_recv.at[pl.ds(1, nz - 1)], recv_sem.at[4])
    parts = [zs_recv[1]]
    for level in range(1, lz):
        parts.append(wide(functools.reduce(jnp.add, [zs_recv[j].astype(F32) for j in range(1 << level, 2 << level)])))
    mid_far = dot_nt(jnp.concatenate(parts, axis=1), vz[...])

    bt[0] = bv[1]
    bt[5] = bv[2]
    wait_bytes(bt.at[pl.ds(1, 4)], recv_sem.at[5])
    local = []
    for quad in range(2):
        both = jnp.concatenate([rt[2 * quad], rt[2 * quad + 1]], axis=0)
        high, low = split(dot(both, bt[5 - quad]))
        vy[...] = jnp.concatenate([high, high, low], axis=1)
        seen = dot_nt(wide(quads[1 - quad]), vy[...])
        for half in range(2):
            r = 2 * quad + half
            sibling = jnp.concatenate(split(sums[r ^ 1]), axis=1)
            local.append(seen[:, half * rank:(half + 1) * rank] + dot_nt(sibling, jnp.concatenate([bt[r]] * 2, axis=1)))
    local = jnp.concatenate(local, axis=1)

    wait_bytes(x_recv.at[pl.ds(1, nx - 1)], recv_sem.at[6])
    parts = [x_recv[1]]
    for level in range(1, lx):
        parts.append(wide(functools.reduce(jnp.add, [x_recv[j].astype(F32) for j in range(1 << level, 2 << level)])))
    top_far = dot_nt(jnp.concatenate(parts, axis=1), vx[...])
    mid_far = mid_far + dot_nt(wide(top_far), vzl[...])
    pair_far = (local + dot_nt(wide(mid_far), vyl[...])).astype(BF)
    for r in range(4):
        far_y_send[r] = pair_far[:, r * rank:(r + 1) * rank]
    for j in far_first(ny):
        send(far_y_send.at[j // 2], far_y.at[rows(y, yblk)], 7, y_peer(j))
    far_y[rows(y, yblk), :] = far_y_send[0]

    near_part(1, 2)
    wait_bytes(h_recv, recv_sem.at[2])
    far = dot_nt(h_recv[...], bv[0])
    wait_bytes(far_y.at[pl.ds(0, (ny - 1) * yblk)], recv_sem.at[7])
    far_out[...] = (far + dot_nt(far_y[...], tv[0])).astype(BF)

    wait_bytes(cy_recv.at[pl.ds(1, ny - 1)], send_sem.at[0])
    wait_bytes(rt.at[pl.ds(1, 4)], send_sem.at[1])
    wait_bytes(h_send, send_sem.at[2])
    wait_bytes(cz_recv.at[pl.ds(1, nz - 1)], send_sem.at[3])
    wait_bytes(zs_recv.at[pl.ds(1, nz - 1)], send_sem.at[4])
    wait_bytes(bt.at[pl.ds(1, 4)], send_sem.at[5])
    wait_bytes(x_recv.at[pl.ds(1, nx - 1)], send_sem.at[6])
    wait_bytes(far_y.at[pl.ds(0, (ny - 1) * yblk)], send_sem.at[7])


def solution(mesh):
    ly = 3
    lz = mesh.shape["sub"].bit_length() - 1 - ly
    lx = mesh.shape["grp"].bit_length() - 1
    ny, nz, nx = 1 << ly, 1 << lz, 1 << lx

    def body(vectors, blocks, basis, transfer, coupling):
        leaf, vecs = vectors.shape[2:]
        rank = basis.shape[3]
        levels = transfer.shape[2]
        yblk = vecs // ny
        scratch = [
            pltpu.VMEM((leaf, vecs), BF),
            pltpu.VMEM((leaf, leaf), BF),
            pltpu.VMEM((leaf, rank), BF),
            pltpu.VMEM((rank, leaf), BF),
            pltpu.VMEM((levels, rank, rank), BF),
            pltpu.VMEM((levels, rank, rank), BF),
            pltpu.VMEM((6, rank, rank), BF),
            pltpu.VMEM((6, rank, rank), BF),
            pltpu.VMEM((12 * rank, rank), BF),
            pltpu.VMEM((2 * rank, 3 * rank), BF),
            pltpu.VMEM((4 * rank, 3 * rank), BF),
            pltpu.VMEM((3 * rank, rank), BF),
            pltpu.VMEM((3 * rank, max(1, lz - 1) * rank), BF),
            pltpu.VMEM((3 * rank, max(1, lx - 1) * rank), BF),
            pltpu.VMEM((rank, (3 * lz - 2) * rank), BF),
            pltpu.VMEM((rank, 3 * rank), BF),
            pltpu.VMEM((rank, (3 * lx - 2) * rank), BF),
            pltpu.VMEM((vecs, rank), BF),
            pltpu.VMEM((vecs, rank), BF),
            pltpu.VMEM((vecs, rank), BF),
            pltpu.VMEM((ny, yblk, rank), BF),
            pltpu.VMEM((yblk, rank), BF),
            pltpu.VMEM((nz, yblk, rank), BF),
            pltpu.VMEM((lz, yblk, rank), BF),
            pltpu.VMEM((nz, yblk, rank), BF),
            pltpu.VMEM((lx, yblk, rank), BF),
            pltpu.VMEM((nx, yblk, rank), BF),
            pltpu.VMEM((4, yblk, rank), BF),
            pltpu.VMEM((vecs, rank), BF),
            pltpu.SemaphoreType.DMA((6,)),
            pltpu.SemaphoreType.DMA((8,)),
            pltpu.SemaphoreType.DMA((8,)),
        ]
        near, far = pl.pallas_call(
            functools.partial(kernel, (lz, lx)),
            out_shape=[jax.ShapeDtypeStruct((leaf, vecs), F32), jax.ShapeDtypeStruct((vecs, rank), BF)],
            in_specs=[pl.BlockSpec(memory_space=pltpu.HBM)] * 5,
            out_specs=[pl.BlockSpec(memory_space=pltpu.VMEM)] * 2,
            scratch_shapes=scratch,
            compiler_params=pltpu.CompilerParams(
                collective_id=0, has_side_effects=True, vmem_limit_bytes=32 * 1024 * 1024,
            ),
        )(*(pltpu.with_memory_space_constraint(whole[0, 0], pltpu.HBM) for whole in (vectors, blocks, basis, transfer, coupling)))
        out = near + dot_nt(basis[0, 0], far)
        return out.astype(BF)[None, None]

    return jax.shard_map(
        body,
        mesh=mesh,
        in_specs=(
            P("grp", "sub", None, None),
            P("grp", "sub", None, None),
            P("grp", "sub", None, None),
            P("grp", "sub", None, None, None),
            P("grp", "sub", None, None, None),
        ),
        out_specs=P("grp", "sub", None, None),
        check_vma=False,
    )
```

```python
import functools

import jax
import jax.numpy as jnp
from jax import lax
from jax.experimental import pallas as pl
from jax.experimental.pallas import tpu as pltpu
from jax.sharding import PartitionSpec as P

MESH = pl.DeviceIdType.MESH
BF = jnp.bfloat16
F32 = jnp.float32


def dot(left, right):
    return jnp.dot(left, right, preferred_element_type=F32)


def dot_nt(left, right):
    return lax.dot_general(left, right, (((1,), (1,)), ((), ())), preferred_element_type=F32)


def dot_tn(left, right):
    return lax.dot_general(left, right, (((0,), (0,)), ((), ())), preferred_element_type=F32)


def split(value):
    high = value.astype(BF)
    return high, (value - high.astype(F32)).astype(BF)


def flip(index, offset):
    out = index
    for bit in range(offset.bit_length()):
        if offset >> bit & 1:
            out = out + (1 << bit) - (2 << bit) * lax.rem(lax.div(index, 1 << bit), 2)
    return out


def level_of(offset):
    return offset.bit_length() - 1


def far_first(count):
    return [j for j in (4, 5, 3, 7, 6, 2, 1) if j < count]


def wait_bytes(ref, sem):
    pltpu.make_async_copy(ref, ref, sem).wait()


def up_weight(product):
    high, low = split(product)
    return jnp.concatenate([high, high, low], axis=0)


def up_exact(matrix):
    return jnp.concatenate([matrix, matrix, jnp.zeros_like(matrix)], axis=0)


def wide(value):
    high, low = split(value)
    return jnp.concatenate([high, low, high], axis=1)


def times_exact(product, matrix):
    high, low = split(product)
    return dot(high, matrix) + dot(low, matrix)


def kernel(dims, x_hbm, d_hbm, u_hbm, t_hbm, b_hbm, near, far_out,
           xv, dv, uv, ut, tv, bv,
           rt, bt, wy, wx, wzl, vx, vz, vw, vg, r0t,
           h_send, h_recv, cy_send, cy_recv, cl_send, cl_recv,
           cz_send, cz_recv, zs_send, zs_recv, x_send, x_recv,
           far_y_send, far_y,
           load_sem, send_sem, recv_sem):
    lz, lx = dims
    ly = 3
    ny, nz, nx = 1 << ly, 1 << lz, 1 << lx
    leaf, vecs = x_hbm.shape
    rank = u_hbm.shape[1]
    yblk = vecs // ny
    sub, grp = lax.axis_index("sub"), lax.axis_index("grp")
    y, z = lax.rem(sub, ny), lax.div(sub, ny)

    def y_peer(j):
        return {"sub": z * ny + flip(y, j)}

    def z_peer(j):
        return {"sub": flip(z, j) * ny + y}

    def x_peer(j):
        return {"grp": flip(grp, j)}

    def rows(index, size):
        return pl.ds(pl.multiple_of(index * size, size), size)

    def send(src, dst, group, peer):
        pltpu.make_async_remote_copy(
            src_ref=src, dst_ref=dst, send_sem=send_sem.at[group], recv_sem=recv_sem.at[group],
            device_id=peer, device_id_type=MESH,
        ).start()

    barrier = pltpu.get_barrier_semaphore()
    peers = [y_peer(j) for j in far_first(ny)] + [z_peer(j) for j in far_first(nz)] + [x_peer(j) for j in far_first(nx)]
    for peer in peers:
        pl.semaphore_signal(barrier, inc=1, device_id=peer, device_id_type=MESH)

    head = leaf // 2
    loads = {}
    for i, (name, src, dst) in enumerate((
        ("u", u_hbm, uv),
        ("x0", x_hbm.at[pl.ds(0, head)], xv.at[pl.ds(0, head)]),
        ("x1", x_hbm.at[pl.ds(head, head)], xv.at[pl.ds(head, head)]),
        ("t", t_hbm, tv),
        ("d", d_hbm, dv),
        ("b", b_hbm, bv),
    )):
        loads[name] = pltpu.make_async_copy(src, dst, load_sem.at[i])
        loads[name].start()

    pair = lax.div(y, 2)
    outward = 2 * lax.rem(y, 2) - 1

    def spread(src, dst, group):
        for k in (3, 2, 1):
            target = lax.rem(y + k * outward + ny, ny)
            other = lax.div(target, 2)
            slot = lax.rem(pair + other, 2) + 2 * lax.rem(lax.div(pair, 2) + lax.div(other, 2), 2)
            send(src.at[1], dst.at[slot], group, {"sub": z * ny + target})
        send(src.at[2], dst.at[4], group, y_peer(6))

    def climb(base, levels):
        product = tv[base].astype(F32)
        chain = [product]
        for level in range(1, levels):
            product = times_exact(product, tv[base + level])
            chain.append(product)
        return chain

    def down(products, base, levels):
        parts = [bv[base].T]
        for i in range(1, levels):
            parts.append(up_weight(times_exact(products[i - 1], bv[base + i]).T))
        return jnp.concatenate(parts, axis=0)

    def near_part(part, parts):
        size = vecs // parts
        at = pl.ds(part * size, size)
        near[:, at] = dot(dv[...], xv[:, at])

    loads["t"].wait()
    ty = climb(0, ly)
    wy[...] = up_weight(ty[ly - 1])
    loads["u"].wait()
    ut[...] = uv[...].T
    loads["x0"].wait()
    hat_t = dot(ut[:, :head], xv[:head, :])
    loads["x1"].wait()
    hat = (hat_t + dot(ut[:, head:], xv[head:, :])).T
    hat_w = wide(hat)
    cy_send[...] = dot(hat_w, wy[...]).astype(BF)
    pl.semaphore_wait(barrier, len(peers))
    for j in far_first(ny):
        send(cy_send.at[rows(flip(y, j), yblk)], cy_recv.at[j], 0, y_peer(j))

    cl_send[...] = dot(hat_w[:, :2 * rank], jnp.concatenate([tv[0], tv[0]], axis=0)).astype(BF)
    h_send[...] = hat.astype(BF)
    tz = climb(ly, lz + lx - 1)
    wx[...] = jnp.concatenate([up_weight(product) for product in tz[lz - 1:]], axis=1)
    if lz > 1:
        wzl[...] = jnp.concatenate([up_exact(tv[ly])] + [up_weight(tz[i]) for i in range(1, lz - 1)], axis=1)
    loads["d"].wait()
    near_part(0, 2)
    for j in far_first(ny):
        send(cl_send.at[rows(flip(y, j), yblk)], cl_recv.at[j], 8, y_peer(j))
    spread(t_hbm, rt, 1)
    spread(b_hbm, bt, 5)

    wait_bytes(cy_recv.at[pl.ds(1, ny - 1)], recv_sem.at[0])
    mid = cy_send[rows(y, yblk), :].astype(F32)
    for j in range(1, ny):
        mid = mid + cy_recv[j].astype(F32)
    mid_w = wide(mid)
    share = dot(mid_w, wx[...])
    for i in range(lx):
        x_send[i] = share[:, i * rank:(i + 1) * rank].astype(BF)
    for j in far_first(nx):
        send(x_send.at[level_of(j)], x_recv.at[j], 6, x_peer(j))
    zs_send[0] = mid.astype(BF)
    if lz > 1:
        zl = dot(mid_w, wzl[...])
        for i in range(lz - 1):
            zs_send[i + 1] = zl[:, i * rank:(i + 1) * rank].astype(BF)
    for j in far_first(nz):
        send(zs_send.at[level_of(j)], zs_recv.at[j], 4, z_peer(j))
    send(h_send, h_recv, 2, y_peer(1))

    loads["b"].wait()
    vx[...] = down(climb(ly + lz, lx), ly + lz, lx)
    vz[...] = down(tz, ly, lz)

    wait_bytes(x_recv.at[pl.ds(1, nx - 1)], recv_sem.at[6])
    parts = [x_recv[1]]
    for level in range(1, lx):
        parts.append(wide(functools.reduce(jnp.add, [x_recv[j].astype(F32) for j in range(1 << level, 2 << level)])))
    top = dot(jnp.concatenate(parts, axis=1), vx[...])
    cz_send[...] = top.astype(BF)
    for j in far_first(nz):
        send(cz_send, cz_recv.at[j], 3, z_peer(j))

    rt[0] = tv[1]
    rt[5] = tv[2]
    bt[0] = bv[1]
    bt[5] = bv[2]
    r0t[...] = tv[0].T
    wait_bytes(rt.at[pl.ds(1, 4)], recv_sem.at[1])
    lifts = []
    for quad in range(2):
        both = jnp.concatenate([rt[2 * quad], rt[2 * quad + 1]], axis=0)
        lifts.append(dot(both, rt[5 - quad]))
    lifts = jnp.concatenate(lifts, axis=0)
    whole = dot(wide(lifts), wx[:, :rank])
    for r in range(4):
        at = slice(r * rank, (r + 1) * rank)
        vw[:, at] = up_weight(lifts[at].T)
        vg[:, at] = up_weight(whole[at].T)
    wait_bytes(zs_recv.at[pl.ds(1, nz - 1)], recv_sem.at[4])
    parts = [zs_recv[1]]
    for level in range(1, lz):
        parts.append(wide(functools.reduce(jnp.add, [zs_recv[j].astype(F32) for j in range(1 << level, 2 << level)])))
    mid_far = dot(jnp.concatenate(parts, axis=1), vz[...])

    wait_bytes(cl_recv.at[pl.ds(1, ny - 1)], recv_sem.at[8])
    given = [cl_send[rows(y, yblk), :]] + [cl_recv[j] for j in range(1, ny)]
    sums = [given[2 * r].astype(F32) + given[2 * r + 1].astype(F32) for r in range(4)]
    quads = []
    for quad in range(2):
        left = jnp.concatenate([*split(sums[2 * quad]), *split(sums[2 * quad + 1])], axis=1)
        right = [rt[2 * quad]] * 2 + [rt[2 * quad + 1]] * 2
        quads.append(dot(left, jnp.concatenate(right, axis=0)))
    wait_bytes(bt.at[pl.ds(1, 4)], recv_sem.at[5])
    local = []
    for quad in range(2):
        both = jnp.concatenate([rt[2 * quad], rt[2 * quad + 1]], axis=0)
        high, low = split(dot(both, bt[5 - quad]))
        seen = dot_nt(wide(quads[1 - quad]), jnp.concatenate([high, high, low], axis=1))
        for half in range(2):
            r = 2 * quad + half
            sibling = jnp.concatenate(split(sums[r ^ 1]), axis=1)
            local.append(seen[:, half * rank:(half + 1) * rank] + dot_nt(sibling, jnp.concatenate([bt[r]] * 2, axis=1)))
    local = jnp.concatenate(local, axis=1) + dot(wide(mid_far), vw[...])

    wait_bytes(cz_recv.at[pl.ds(1, nz - 1)], recv_sem.at[3])
    for j in range(1, nz):
        top = top + cz_recv[j].astype(F32)
    pair_far = (local + dot(wide(top), vg[...])).astype(BF)
    for r in range(4):
        far_y_send[r] = pair_far[:, r * rank:(r + 1) * rank]
    for j in far_first(ny):
        send(far_y_send.at[j // 2], far_y.at[rows(y, yblk)], 7, y_peer(j))
    far_y[rows(y, yblk), :] = far_y_send[0]

    near_part(1, 2)
    wait_bytes(h_recv, recv_sem.at[2])
    far = dot_nt(h_recv[...], bv[0])
    wait_bytes(far_y.at[pl.ds(0, (ny - 1) * yblk)], recv_sem.at[7])
    far_out[...] = (far + dot(far_y[...], r0t[...])).astype(BF)

    wait_bytes(cy_recv.at[pl.ds(1, ny - 1)], send_sem.at[0])
    wait_bytes(rt.at[pl.ds(1, 4)], send_sem.at[1])
    wait_bytes(h_send, send_sem.at[2])
    wait_bytes(cz_recv.at[pl.ds(1, nz - 1)], send_sem.at[3])
    wait_bytes(zs_recv.at[pl.ds(1, nz - 1)], send_sem.at[4])
    wait_bytes(bt.at[pl.ds(1, 4)], send_sem.at[5])
    wait_bytes(x_recv.at[pl.ds(1, nx - 1)], send_sem.at[6])
    wait_bytes(far_y.at[pl.ds(0, (ny - 1) * yblk)], send_sem.at[7])
    wait_bytes(cl_recv.at[pl.ds(1, ny - 1)], send_sem.at[8])


def solution(mesh):
    ly = 3
    lz = mesh.shape["sub"].bit_length() - 1 - ly
    lx = mesh.shape["grp"].bit_length() - 1
    ny, nz, nx = 1 << ly, 1 << lz, 1 << lx

    def body(vectors, blocks, basis, transfer, coupling):
        leaf, vecs = vectors.shape[2:]
        rank = basis.shape[3]
        levels = transfer.shape[2]
        yblk = vecs // ny
        scratch = [
            pltpu.VMEM((leaf, vecs), BF),
            pltpu.VMEM((leaf, leaf), BF),
            pltpu.VMEM((leaf, rank), BF),
            pltpu.VMEM((rank, leaf), BF),
            pltpu.VMEM((levels, rank, rank), BF),
            pltpu.VMEM((levels, rank, rank), BF),
            pltpu.VMEM((6, rank, rank), BF),
            pltpu.VMEM((6, rank, rank), BF),
            pltpu.VMEM((3 * rank, rank), BF),
            pltpu.VMEM((3 * rank, lx * rank), BF),
            pltpu.VMEM((3 * rank, max(1, lz - 1) * rank), BF),
            pltpu.VMEM(((3 * lx - 2) * rank, rank), BF),
            pltpu.VMEM(((3 * lz - 2) * rank, rank), BF),
            pltpu.VMEM((3 * rank, 4 * rank), BF),
            pltpu.VMEM((3 * rank, 4 * rank), BF),
            pltpu.VMEM((rank, rank), BF),
            pltpu.VMEM((vecs, rank), BF),
            pltpu.VMEM((vecs, rank), BF),
            pltpu.VMEM((vecs, rank), BF),
            pltpu.VMEM((ny, yblk, rank), BF),
            pltpu.VMEM((vecs, rank), BF),
            pltpu.VMEM((ny, yblk, rank), BF),
            pltpu.VMEM((yblk, rank), BF),
            pltpu.VMEM((nz, yblk, rank), BF),
            pltpu.VMEM((lz, yblk, rank), BF),
            pltpu.VMEM((nz, yblk, rank), BF),
            pltpu.VMEM((lx, yblk, rank), BF),
            pltpu.VMEM((nx, yblk, rank), BF),
            pltpu.VMEM((4, yblk, rank), BF),
            pltpu.VMEM((vecs, rank), BF),
            pltpu.SemaphoreType.DMA((6,)),
            pltpu.SemaphoreType.DMA((9,)),
            pltpu.SemaphoreType.DMA((9,)),
        ]
        near, far = pl.pallas_call(
            functools.partial(kernel, (lz, lx)),
            out_shape=[jax.ShapeDtypeStruct((leaf, vecs), F32), jax.ShapeDtypeStruct((vecs, rank), BF)],
            in_specs=[pl.BlockSpec(memory_space=pltpu.HBM)] * 5,
            out_specs=[pl.BlockSpec(memory_space=pltpu.VMEM)] * 2,
            scratch_shapes=scratch,
            compiler_params=pltpu.CompilerParams(
                collective_id=0, has_side_effects=True, vmem_limit_bytes=32 * 1024 * 1024,
            ),
        )(*(pltpu.with_memory_space_constraint(whole[0, 0], pltpu.HBM) for whole in (vectors, blocks, basis, transfer, coupling)))
        out = near + dot_nt(basis[0, 0], far)
        return out.astype(BF)[None, None]

    return jax.shard_map(
        body,
        mesh=mesh,
        in_specs=(
            P("grp", "sub", None, None),
            P("grp", "sub", None, None),
            P("grp", "sub", None, None),
            P("grp", "sub", None, None, None),
            P("grp", "sub", None, None, None),
        ),
        out_specs=P("grp", "sub", None, None),
        check_vma=False,
    )
```

```python
import functools

import jax
import jax.numpy as jnp
from jax import lax
from jax.experimental import pallas as pl
from jax.experimental.pallas import tpu as pltpu
from jax.sharding import PartitionSpec as P

MESH = pl.DeviceIdType.MESH
BF = jnp.bfloat16
F32 = jnp.float32


def dot(left, right):
    return jnp.dot(left, right, preferred_element_type=F32)


def dot_nt(left, right):
    return lax.dot_general(left, right, (((1,), (1,)), ((), ())), preferred_element_type=F32)


def dot_tn(left, right):
    return lax.dot_general(left, right, (((0,), (0,)), ((), ())), preferred_element_type=F32)


def split(value):
    high = value.astype(BF)
    return high, (value - high.astype(F32)).astype(BF)


def flip(index, offset):
    out = index
    for bit in range(offset.bit_length()):
        if offset >> bit & 1:
            out = out + (1 << bit) - (2 << bit) * lax.rem(lax.div(index, 1 << bit), 2)
    return out


def level_of(offset):
    return offset.bit_length() - 1


def far_first(count):
    return [j for j in (4, 5, 3, 7, 6, 2, 1) if j < count]


def wait_bytes(ref, sem):
    pltpu.make_async_copy(ref, ref, sem).wait()


def up_weight(product):
    high, low = split(product)
    return jnp.concatenate([high, high, low], axis=0)


def up_exact(matrix):
    return jnp.concatenate([matrix, matrix, jnp.zeros_like(matrix)], axis=0)


def wide(value):
    high, low = split(value)
    return jnp.concatenate([high, low, high], axis=1)


def times_exact(product, matrix):
    high, low = split(product)
    return dot(high, matrix) + dot(low, matrix)


def kernel(dims, x_hbm, d_hbm, u_hbm, t_hbm, b_hbm, near, lift_out, far_out,
           xv, dv, uv, ut, tv, bv,
           rt, bt, wy, wx, wzl, vx, vz, vw, vg,
           h_send, h_recv, cy_send, cy_recv, cl_send, cl_recv,
           cz_send, cz_recv, zs_send, zs_recv, x_send, x_recv,
           far_y_send, far_y,
           load_sem, send_sem, recv_sem):
    lz, lx = dims
    ly = 3
    ny, nz, nx = 1 << ly, 1 << lz, 1 << lx
    leaf, vecs = x_hbm.shape
    rank = u_hbm.shape[1]
    yblk = vecs // ny
    sub, grp = lax.axis_index("sub"), lax.axis_index("grp")
    y, z = lax.rem(sub, ny), lax.div(sub, ny)

    def y_peer(j):
        return {"sub": z * ny + flip(y, j)}

    def z_peer(j):
        return {"sub": flip(z, j) * ny + y}

    def x_peer(j):
        return {"grp": flip(grp, j)}

    def rows(index, size):
        return pl.ds(pl.multiple_of(index * size, size), size)

    def send(src, dst, group, peer):
        pltpu.make_async_remote_copy(
            src_ref=src, dst_ref=dst, send_sem=send_sem.at[group], recv_sem=recv_sem.at[group],
            device_id=peer, device_id_type=MESH,
        ).start()

    barrier = pltpu.get_barrier_semaphore()
    peers = []
    for j in far_first(8):
        peers += [peer(j) for peer, count in ((y_peer, ny), (z_peer, nz), (x_peer, nx)) if j < count]
    for peer in peers:
        pl.semaphore_signal(barrier, inc=1, device_id=peer, device_id_type=MESH)

    head = leaf // 2
    loads = {}
    for i, (name, src, dst) in enumerate((
        ("u", u_hbm, uv),
        ("x0", x_hbm.at[pl.ds(0, head)], xv.at[pl.ds(0, head)]),
        ("x1", x_hbm.at[pl.ds(head, head)], xv.at[pl.ds(head, head)]),
        ("t", t_hbm, tv),
        ("d", d_hbm, dv),
        ("b", b_hbm, bv),
    )):
        loads[name] = pltpu.make_async_copy(src, dst, load_sem.at[i])
        loads[name].start()

    pair = lax.div(y, 2)
    outward = 2 * lax.rem(y, 2) - 1

    def spread(src, dst, group):
        for k in (3, 2, 1):
            target = lax.rem(y + k * outward + ny, ny)
            other = lax.div(target, 2)
            slot = lax.rem(pair + other, 2) + 2 * lax.rem(lax.div(pair, 2) + lax.div(other, 2), 2)
            send(src.at[1], dst.at[slot], group, {"sub": z * ny + target})
        send(src.at[2], dst.at[4], group, y_peer(6))

    def climb(base, levels):
        product = tv[base].astype(F32)
        chain = [product]
        for level in range(1, levels):
            product = times_exact(product, tv[base + level])
            chain.append(product)
        return chain

    def down(products, base, levels):
        parts = [bv[base].T]
        for i in range(1, levels):
            parts.append(up_weight(times_exact(products[i - 1], bv[base + i]).T))
        return jnp.concatenate(parts, axis=0)

    def near_part(part, parts):
        size = vecs // parts
        at = pl.ds(part * size, size)
        near[:, at] = dot(dv[...], xv[:, at])

    loads["t"].wait()
    ty = climb(0, ly)
    wy[...] = up_weight(ty[ly - 1])
    loads["u"].wait()
    ut[...] = uv[...].T
    loads["x0"].wait()
    hat_t = dot(ut[:, :head], xv[:head, :])
    loads["x1"].wait()
    hat = (hat_t + dot(ut[:, head:], xv[head:, :])).T
    hat_w = wide(hat)
    cy_send[...] = dot(hat_w, wy[...]).astype(BF)
    pl.semaphore_wait(barrier, len(peers))
    for j in far_first(ny):
        send(cy_send.at[rows(flip(y, j), yblk)], cy_recv.at[j], 0, y_peer(j))

    cl_send[...] = dot(hat_w[:, :2 * rank], jnp.concatenate([tv[0], tv[0]], axis=0)).astype(BF)
    h_send[...] = hat.astype(BF)
    tz = climb(ly, lz + lx - 1)
    wx[...] = jnp.concatenate([up_weight(product) for product in tz[lz - 1:]], axis=1)
    if lz > 1:
        wzl[...] = jnp.concatenate([up_exact(tv[ly])] + [up_weight(tz[i]) for i in range(1, lz - 1)], axis=1)
    lift_out[...] = jnp.concatenate(split(dot(uv[...], tv[0])), axis=1)
    loads["d"].wait()
    near_part(0, 2)
    for j in far_first(ny):
        send(cl_send.at[rows(flip(y, j), yblk)], cl_recv.at[j], 8, y_peer(j))
    spread(t_hbm, rt, 1)
    spread(b_hbm, bt, 5)

    wait_bytes(cy_recv.at[pl.ds(1, ny - 1)], recv_sem.at[0])
    mid = cy_send[rows(y, yblk), :].astype(F32)
    for j in range(1, ny):
        mid = mid + cy_recv[j].astype(F32)
    mid_w = wide(mid)
    share = dot(mid_w, wx[...])
    for i in range(lx):
        x_send[i] = share[:, i * rank:(i + 1) * rank].astype(BF)
    for j in far_first(nx):
        send(x_send.at[level_of(j)], x_recv.at[j], 6, x_peer(j))
    zs_send[0] = mid.astype(BF)
    if lz > 1:
        zl = dot(mid_w, wzl[...])
        for i in range(lz - 1):
            zs_send[i + 1] = zl[:, i * rank:(i + 1) * rank].astype(BF)
    for j in far_first(nz):
        send(zs_send.at[level_of(j)], zs_recv.at[j], 4, z_peer(j))
    send(h_send, h_recv, 2, y_peer(1))

    loads["b"].wait()
    vx[...] = down(climb(ly + lz, lx), ly + lz, lx)
    vz[...] = down(tz, ly, lz)

    wait_bytes(x_recv.at[pl.ds(1, nx - 1)], recv_sem.at[6])
    parts = [x_recv[1]]
    for level in range(1, lx):
        parts.append(wide(functools.reduce(jnp.add, [x_recv[j].astype(F32) for j in range(1 << level, 2 << level)])))
    top = dot(jnp.concatenate(parts, axis=1), vx[...])
    cz_send[...] = top.astype(BF)
    for j in far_first(nz):
        send(cz_send, cz_recv.at[j], 3, z_peer(j))

    rt[0] = tv[1]
    rt[5] = tv[2]
    bt[0] = bv[1]
    bt[5] = bv[2]
    wait_bytes(rt.at[pl.ds(1, 4)], recv_sem.at[1])
    lifts = []
    for quad in range(2):
        both = jnp.concatenate([rt[2 * quad], rt[2 * quad + 1]], axis=0)
        lifts.append(dot(both, rt[5 - quad]))
    lifts = jnp.concatenate(lifts, axis=0)
    whole = dot(wide(lifts), wx[:, :rank])
    for r in range(4):
        at = slice(r * rank, (r + 1) * rank)
        vw[:, at] = up_weight(lifts[at].T)
        vg[:, at] = up_weight(whole[at].T)
    wait_bytes(zs_recv.at[pl.ds(1, nz - 1)], recv_sem.at[4])
    parts = [zs_recv[1]]
    for level in range(1, lz):
        parts.append(wide(functools.reduce(jnp.add, [zs_recv[j].astype(F32) for j in range(1 << level, 2 << level)])))
    mid_far = dot(jnp.concatenate(parts, axis=1), vz[...])

    wait_bytes(cl_recv.at[pl.ds(1, ny - 1)], recv_sem.at[8])
    given = [cl_send[rows(y, yblk), :]] + [cl_recv[j] for j in range(1, ny)]
    sums = [given[2 * r].astype(F32) + given[2 * r + 1].astype(F32) for r in range(4)]
    quads = []
    for quad in range(2):
        left = jnp.concatenate([*split(sums[2 * quad]), *split(sums[2 * quad + 1])], axis=1)
        right = [rt[2 * quad]] * 2 + [rt[2 * quad + 1]] * 2
        quads.append(dot(left, jnp.concatenate(right, axis=0)))
    wait_bytes(bt.at[pl.ds(1, 4)], recv_sem.at[5])
    local = []
    for quad in range(2):
        both = jnp.concatenate([rt[2 * quad], rt[2 * quad + 1]], axis=0)
        high, low = split(dot(both, bt[5 - quad]))
        seen = dot_nt(wide(quads[1 - quad]), jnp.concatenate([high, high, low], axis=1))
        for half in range(2):
            r = 2 * quad + half
            sibling = jnp.concatenate(split(sums[r ^ 1]), axis=1)
            local.append(seen[:, half * rank:(half + 1) * rank] + dot_nt(sibling, jnp.concatenate([bt[r]] * 2, axis=1)))
    local = jnp.concatenate(local, axis=1) + dot(wide(mid_far), vw[...])

    wait_bytes(cz_recv.at[pl.ds(1, nz - 1)], recv_sem.at[3])
    for j in range(1, nz):
        top = top + cz_recv[j].astype(F32)
    pair_far = (local + dot(wide(top), vg[...])).astype(BF)
    for r in range(4):
        far_y_send[r] = pair_far[:, r * rank:(r + 1) * rank]
    for j in far_first(ny):
        send(far_y_send.at[j // 2], far_y.at[rows(y, yblk)], 7, y_peer(j))
    far_y[rows(y, yblk), :] = far_y_send[0]

    wait_bytes(h_recv, recv_sem.at[2])
    far = dot_nt(h_recv[...], bv[0]).astype(BF)
    near_part(1, 2)
    near[...] += dot_nt(uv[...], far)
    wait_bytes(far_y.at[pl.ds(0, (ny - 1) * yblk)], recv_sem.at[7])
    far_out[...] = far_y[...]

    wait_bytes(cy_recv.at[pl.ds(1, ny - 1)], send_sem.at[0])
    wait_bytes(rt.at[pl.ds(1, 4)], send_sem.at[1])
    wait_bytes(h_send, send_sem.at[2])
    wait_bytes(cz_recv.at[pl.ds(1, nz - 1)], send_sem.at[3])
    wait_bytes(zs_recv.at[pl.ds(1, nz - 1)], send_sem.at[4])
    wait_bytes(bt.at[pl.ds(1, 4)], send_sem.at[5])
    wait_bytes(x_recv.at[pl.ds(1, nx - 1)], send_sem.at[6])
    wait_bytes(far_y.at[pl.ds(0, (ny - 1) * yblk)], send_sem.at[7])
    wait_bytes(cl_recv.at[pl.ds(1, ny - 1)], send_sem.at[8])


def last_kernel(near, lift, far, o_hbm, far_t, ov, store_sem):
    leaf = near.shape[0]
    chunks = store_sem.shape[0]
    tile = leaf // chunks
    far_t[...] = jnp.concatenate([far[...].T] * 2, axis=0)
    stores = []
    for step in range(chunks):
        at = pl.ds(step * tile, tile)
        ov[at, :] = (near[at, :] + dot(lift[at, :], far_t[...])).astype(BF)
        store = pltpu.make_async_copy(ov.at[at], o_hbm.at[at], store_sem.at[step])
        store.start()
        stores.append(store)
    for store in stores:
        store.wait()


def solution(mesh):
    ly = 3
    lz = mesh.shape["sub"].bit_length() - 1 - ly
    lx = mesh.shape["grp"].bit_length() - 1
    ny, nz, nx = 1 << ly, 1 << lz, 1 << lx

    def body(vectors, blocks, basis, transfer, coupling):
        leaf, vecs = vectors.shape[2:]
        rank = basis.shape[3]
        levels = transfer.shape[2]
        yblk = vecs // ny
        scratch = [
            pltpu.VMEM((leaf, vecs), BF),
            pltpu.VMEM((leaf, leaf), BF),
            pltpu.VMEM((leaf, rank), BF),
            pltpu.VMEM((rank, leaf), BF),
            pltpu.VMEM((levels, rank, rank), BF),
            pltpu.VMEM((levels, rank, rank), BF),
            pltpu.VMEM((6, rank, rank), BF),
            pltpu.VMEM((6, rank, rank), BF),
            pltpu.VMEM((3 * rank, rank), BF),
            pltpu.VMEM((3 * rank, lx * rank), BF),
            pltpu.VMEM((3 * rank, max(1, lz - 1) * rank), BF),
            pltpu.VMEM(((3 * lx - 2) * rank, rank), BF),
            pltpu.VMEM(((3 * lz - 2) * rank, rank), BF),
            pltpu.VMEM((3 * rank, 4 * rank), BF),
            pltpu.VMEM((3 * rank, 4 * rank), BF),
            pltpu.VMEM((vecs, rank), BF),
            pltpu.VMEM((vecs, rank), BF),
            pltpu.VMEM((vecs, rank), BF),
            pltpu.VMEM((ny, yblk, rank), BF),
            pltpu.VMEM((vecs, rank), BF),
            pltpu.VMEM((ny, yblk, rank), BF),
            pltpu.VMEM((yblk, rank), BF),
            pltpu.VMEM((nz, yblk, rank), BF),
            pltpu.VMEM((lz, yblk, rank), BF),
            pltpu.VMEM((nz, yblk, rank), BF),
            pltpu.VMEM((lx, yblk, rank), BF),
            pltpu.VMEM((nx, yblk, rank), BF),
            pltpu.VMEM((4, yblk, rank), BF),
            pltpu.VMEM((vecs, rank), BF),
            pltpu.SemaphoreType.DMA((6,)),
            pltpu.SemaphoreType.DMA((9,)),
            pltpu.SemaphoreType.DMA((9,)),
        ]
        vmem = pl.BlockSpec(memory_space=pltpu.VMEM)
        near, lift, far = pl.pallas_call(
            functools.partial(kernel, (lz, lx)),
            out_shape=[
                jax.ShapeDtypeStruct((leaf, vecs), F32),
                jax.ShapeDtypeStruct((leaf, 2 * rank), BF),
                jax.ShapeDtypeStruct((vecs, rank), BF),
            ],
            in_specs=[pl.BlockSpec(memory_space=pltpu.HBM)] * 5,
            out_specs=[vmem] * 3,
            scratch_shapes=scratch,
            compiler_params=pltpu.CompilerParams(
                collective_id=0, has_side_effects=True, vmem_limit_bytes=32 * 1024 * 1024,
            ),
        )(*(pltpu.with_memory_space_constraint(whole[0, 0], pltpu.HBM) for whole in (vectors, blocks, basis, transfer, coupling)))
        out = pl.pallas_call(
            last_kernel,
            out_shape=jax.ShapeDtypeStruct((leaf, vecs), BF),
            in_specs=[vmem] * 3,
            out_specs=pl.BlockSpec(memory_space=pltpu.HBM),
            scratch_shapes=[
                pltpu.VMEM((2 * rank, vecs), BF),
                pltpu.VMEM((leaf, vecs), BF),
                pltpu.SemaphoreType.DMA((4,)),
            ],
            compiler_params=pltpu.CompilerParams(vmem_limit_bytes=24 * 1024 * 1024),
        )(near, lift, far)
        return out[None, None]

    return jax.shard_map(
        body,
        mesh=mesh,
        in_specs=(
            P("grp", "sub", None, None),
            P("grp", "sub", None, None),
            P("grp", "sub", None, None),
            P("grp", "sub", None, None, None),
            P("grp", "sub", None, None, None),
        ),
        out_specs=P("grp", "sub", None, None),
        check_vma=False,
    )
```

```python
import functools

import jax
import jax.numpy as jnp
from jax import lax
from jax.experimental import pallas as pl
from jax.experimental.pallas import tpu as pltpu
from jax.sharding import PartitionSpec as P

MESH = pl.DeviceIdType.MESH
BF = jnp.bfloat16
F32 = jnp.float32


def dot(left, right):
    return jnp.dot(left, right, preferred_element_type=F32)


def dot_nt(left, right):
    return lax.dot_general(left, right, (((1,), (1,)), ((), ())), preferred_element_type=F32)


def dot_tn(left, right):
    return lax.dot_general(left, right, (((0,), (0,)), ((), ())), preferred_element_type=F32)


def split(value):
    high = value.astype(BF)
    return high, (value - high.astype(F32)).astype(BF)


def flip(index, offset):
    out = index
    for bit in range(offset.bit_length()):
        if offset >> bit & 1:
            out = out + (1 << bit) - (2 << bit) * lax.rem(lax.div(index, 1 << bit), 2)
    return out


def level_of(offset):
    return offset.bit_length() - 1


def far_first(count):
    return [j for j in (4, 5, 3, 7, 6, 2, 1) if j < count]


def wait_bytes(ref, sem):
    pltpu.make_async_copy(ref, ref, sem).wait()


def up_weight(product):
    high, low = split(product)
    return jnp.concatenate([high, high, low], axis=0)


def up_exact(matrix):
    return jnp.concatenate([matrix, matrix, jnp.zeros_like(matrix)], axis=0)


def wide(value):
    high, low = split(value)
    return jnp.concatenate([high, low, high], axis=1)


def times_exact(product, matrix):
    high, low = split(product)
    return dot(high, matrix) + dot(low, matrix)


def kernel(dims, x_hbm, d_hbm, u_hbm, t_hbm, b_hbm, near, lift_out, far_out,
           xv, dv, uv, ut, tv, bv,
           rt, bt, wy, wx, wzl, vx, vz, vw, vg,
           h_send, h_recv, cy_send, cy_recv, cl_send, cl_recv,
           cz_send, cz_recv, zs_send, zs_recv, x_send, x_recv,
           far_y_send, far_y,
           load_sem, y_sem, z_sem, send_sem, recv_sem):
    lz, lx = dims
    ly = 3
    ny, nz, nx = 1 << ly, 1 << lz, 1 << lx
    leaf, vecs = x_hbm.shape
    rank = u_hbm.shape[1]
    yblk = vecs // ny
    sub, grp = lax.axis_index("sub"), lax.axis_index("grp")
    y, z = lax.rem(sub, ny), lax.div(sub, ny)

    def y_peer(j):
        return {"sub": z * ny + flip(y, j)}

    def z_peer(j):
        return {"sub": flip(z, j) * ny + y}

    def x_peer(j):
        return {"grp": flip(grp, j)}

    def rows(index, size):
        return pl.ds(pl.multiple_of(index * size, size), size)

    def send(src, dst, group, peer):
        pltpu.make_async_remote_copy(
            src_ref=src, dst_ref=dst, send_sem=send_sem.at[group], recv_sem=recv_sem.at[group],
            device_id=peer, device_id_type=MESH,
        ).start()

    order = sorted(range(ny), key=lambda place: min(place, ny - place))
    rank_y = sum(jnp.where(y == place, k, 0) for k, place in enumerate(order))
    barrier = pltpu.get_barrier_semaphore()

    def greet(sem, peer):
        pl.semaphore_signal(sem, inc=1, device_id=peer, device_id_type=MESH)

    for k, place in reversed(list(enumerate(order))):
        @pl.when(rank_y < k)
        def _():
            greet(barrier, {"sub": z * ny + place})
    for place in reversed(range(nz)):
        @pl.when(z < place)
        def _():
            greet(barrier, {"sub": place * ny + y})
    for j in far_first(nx):
        greet(barrier, x_peer(j))

    head = leaf // 2
    loads = {}
    for i, (name, src, dst) in enumerate((
        ("u", u_hbm, uv),
        ("x0", x_hbm.at[pl.ds(0, head)], xv.at[pl.ds(0, head)]),
        ("x1", x_hbm.at[pl.ds(head, head)], xv.at[pl.ds(head, head)]),
        ("t", t_hbm, tv),
        ("d", d_hbm, dv),
        ("b", b_hbm, bv),
    )):
        loads[name] = pltpu.make_async_copy(src, dst, load_sem.at[i])
        loads[name].start()

    pl.semaphore_wait(barrier, nx - 1 + z + rank_y)
    for k, place in enumerate(order):
        @pl.when(rank_y > k)
        def _():
            greet(y_sem.at[y], {"sub": z * ny + place})
    for place in range(nz):
        @pl.when(z > place)
        def _():
            greet(z_sem, {"sub": place * ny + y})

    pair = lax.div(y, 2)
    outward = 2 * lax.rem(y, 2) - 1

    def spread(src, dst, group):
        for k in (3, 2, 1):
            target = lax.rem(y + k * outward + ny, ny)
            other = lax.div(target, 2)
            slot = lax.rem(pair + other, 2) + 2 * lax.rem(lax.div(pair, 2) + lax.div(other, 2), 2)
            send(src.at[1], dst.at[slot], group, {"sub": z * ny + target})
        send(src.at[2], dst.at[4], group, y_peer(6))

    def climb(base, levels):
        product = tv[base].astype(F32)
        chain = [product]
        for level in range(1, levels):
            product = times_exact(product, tv[base + level])
            chain.append(product)
        return chain

    def down(products, base, levels):
        parts = [bv[base].T]
        for i in range(1, levels):
            parts.append(up_weight(times_exact(products[i - 1], bv[base + i]).T))
        return jnp.concatenate(parts, axis=0)

    def near_part(part, parts):
        size = vecs // parts
        at = pl.ds(part * size, size)
        near[:, at] = dot(dv[...], xv[:, at])

    loads["t"].wait()
    ty = climb(0, ly)
    wy[...] = up_weight(ty[ly - 1])
    loads["u"].wait()
    ut[...] = uv[...].T
    loads["x0"].wait()
    hat_t = dot(ut[:, :head], xv[:head, :])
    loads["x1"].wait()
    hat = (hat_t + dot(ut[:, head:], xv[head:, :])).T
    hat_w = wide(hat)
    cy_send[...] = dot(hat_w, wy[...]).astype(BF)

    def scatter(place):
        send(cy_send.at[pl.ds(place * yblk, yblk)], cy_recv.at[flip(y, place)], 0, {"sub": z * ny + place})

    for k, place in enumerate(order):
        @pl.when(rank_y > k)
        def _():
            scatter(place)

    cl_send[...] = dot(hat_w[:, :2 * rank], jnp.concatenate([tv[0], tv[0]], axis=0)).astype(BF)
    h_send[...] = hat.astype(BF)
    tz = climb(ly, lz + lx - 1)
    wx[...] = jnp.concatenate([up_weight(product) for product in tz[lz - 1:]], axis=1)
    if lz > 1:
        wzl[...] = jnp.concatenate([up_exact(tv[ly])] + [up_weight(tz[i]) for i in range(1, lz - 1)], axis=1)
    lift_out[...] = jnp.concatenate(split(dot(uv[...], tv[0])), axis=1)
    loads["d"].wait()
    near_part(0, 2)
    for k, place in enumerate(order):
        @pl.when(rank_y < k)
        def _():
            pl.semaphore_wait(y_sem.at[place], 1)
            scatter(place)
    for j in far_first(ny):
        send(cl_send.at[rows(flip(y, j), yblk)], cl_recv.at[j], 8, y_peer(j))
    spread(t_hbm, rt, 1)
    spread(b_hbm, bt, 5)

    wait_bytes(cy_recv.at[pl.ds(1, ny - 1)], recv_sem.at[0])
    mid = cy_send[rows(y, yblk), :].astype(F32)
    for j in range(1, ny):
        mid = mid + cy_recv[j].astype(F32)
    mid_w = wide(mid)
    share = dot(mid_w, wx[...])
    for i in range(lx):
        x_send[i] = share[:, i * rank:(i + 1) * rank].astype(BF)
    for j in far_first(nx):
        send(x_send.at[level_of(j)], x_recv.at[j], 6, x_peer(j))
    zs_send[0] = mid.astype(BF)
    if lz > 1:
        zl = dot(mid_w, wzl[...])
        for i in range(lz - 1):
            zs_send[i + 1] = zl[:, i * rank:(i + 1) * rank].astype(BF)

    @pl.when(z < nz - 1)
    def _():
        pl.semaphore_wait(z_sem, nz - 1 - z)

    for j in far_first(nz):
        send(zs_send.at[level_of(j)], zs_recv.at[j], 4, z_peer(j))
    send(h_send, h_recv, 2, y_peer(1))

    loads["b"].wait()
    vx[...] = down(climb(ly + lz, lx), ly + lz, lx)
    vz[...] = down(tz, ly, lz)

    wait_bytes(x_recv.at[pl.ds(1, nx - 1)], recv_sem.at[6])
    parts = [x_recv[1]]
    for level in range(1, lx):
        parts.append(wide(functools.reduce(jnp.add, [x_recv[j].astype(F32) for j in range(1 << level, 2 << level)])))
    top = dot(jnp.concatenate(parts, axis=1), vx[...])
    cz_send[...] = top.astype(BF)
    for j in far_first(nz):
        send(cz_send, cz_recv.at[j], 3, z_peer(j))

    rt[0] = tv[1]
    rt[5] = tv[2]
    bt[0] = bv[1]
    bt[5] = bv[2]
    wait_bytes(rt.at[pl.ds(1, 4)], recv_sem.at[1])
    lifts = []
    for quad in range(2):
        both = jnp.concatenate([rt[2 * quad], rt[2 * quad + 1]], axis=0)
        lifts.append(dot(both, rt[5 - quad]))
    lifts = jnp.concatenate(lifts, axis=0)
    whole = dot(wide(lifts), wx[:, :rank])
    for r in range(4):
        at = slice(r * rank, (r + 1) * rank)
        vw[:, at] = up_weight(lifts[at].T)
        vg[:, at] = up_weight(whole[at].T)
    wait_bytes(zs_recv.at[pl.ds(1, nz - 1)], recv_sem.at[4])
    parts = [zs_recv[1]]
    for level in range(1, lz):
        parts.append(wide(functools.reduce(jnp.add, [zs_recv[j].astype(F32) for j in range(1 << level, 2 << level)])))
    mid_far = dot(jnp.concatenate(parts, axis=1), vz[...])

    wait_bytes(cl_recv.at[pl.ds(1, ny - 1)], recv_sem.at[8])
    given = [cl_send[rows(y, yblk), :]] + [cl_recv[j] for j in range(1, ny)]
    sums = [given[2 * r].astype(F32) + given[2 * r + 1].astype(F32) for r in range(4)]
    quads = []
    for quad in range(2):
        left = jnp.concatenate([*split(sums[2 * quad]), *split(sums[2 * quad + 1])], axis=1)
        right = [rt[2 * quad]] * 2 + [rt[2 * quad + 1]] * 2
        quads.append(dot(left, jnp.concatenate(right, axis=0)))
    wait_bytes(bt.at[pl.ds(1, 4)], recv_sem.at[5])
    local = []
    for quad in range(2):
        both = jnp.concatenate([rt[2 * quad], rt[2 * quad + 1]], axis=0)
        high, low = split(dot(both, bt[5 - quad]))
        seen = dot_nt(wide(quads[1 - quad]), jnp.concatenate([high, high, low], axis=1))
        for half in range(2):
            r = 2 * quad + half
            sibling = jnp.concatenate(split(sums[r ^ 1]), axis=1)
            local.append(seen[:, half * rank:(half + 1) * rank] + dot_nt(sibling, jnp.concatenate([bt[r]] * 2, axis=1)))
    local = jnp.concatenate(local, axis=1) + dot(wide(mid_far), vw[...])

    wait_bytes(cz_recv.at[pl.ds(1, nz - 1)], recv_sem.at[3])
    for j in range(1, nz):
        top = top + cz_recv[j].astype(F32)
    pair_far = (local + dot(wide(top), vg[...])).astype(BF)
    for r in range(4):
        far_y_send[r] = pair_far[:, r * rank:(r + 1) * rank]
    for j in far_first(ny):
        send(far_y_send.at[j // 2], far_y.at[rows(y, yblk)], 7, y_peer(j))
    far_y[rows(y, yblk), :] = far_y_send[0]

    wait_bytes(h_recv, recv_sem.at[2])
    far = dot_nt(h_recv[...], bv[0]).astype(BF)
    near_part(1, 2)
    near[...] += dot_nt(uv[...], far)
    wait_bytes(far_y.at[pl.ds(0, (ny - 1) * yblk)], recv_sem.at[7])
    far_out[...] = far_y[...]

    wait_bytes(cy_recv.at[pl.ds(1, ny - 1)], send_sem.at[0])
    wait_bytes(rt.at[pl.ds(1, 4)], send_sem.at[1])
    wait_bytes(h_send, send_sem.at[2])
    wait_bytes(cz_recv.at[pl.ds(1, nz - 1)], send_sem.at[3])
    wait_bytes(zs_recv.at[pl.ds(1, nz - 1)], send_sem.at[4])
    wait_bytes(bt.at[pl.ds(1, 4)], send_sem.at[5])
    wait_bytes(x_recv.at[pl.ds(1, nx - 1)], send_sem.at[6])
    wait_bytes(far_y.at[pl.ds(0, (ny - 1) * yblk)], send_sem.at[7])
    wait_bytes(cl_recv.at[pl.ds(1, ny - 1)], send_sem.at[8])


def last_kernel(near, lift, far, o_hbm, far_t, ov, store_sem):
    leaf = near.shape[0]
    chunks = store_sem.shape[0]
    tile = leaf // chunks
    far_t[...] = jnp.concatenate([far[...].T] * 2, axis=0)
    stores = []
    for step in range(chunks):
        at = pl.ds(step * tile, tile)
        ov[at, :] = (near[at, :] + dot(lift[at, :], far_t[...])).astype(BF)
        store = pltpu.make_async_copy(ov.at[at], o_hbm.at[at], store_sem.at[step])
        store.start()
        stores.append(store)
    for store in stores:
        store.wait()


def solution(mesh):
    ly = 3
    lz = mesh.shape["sub"].bit_length() - 1 - ly
    lx = mesh.shape["grp"].bit_length() - 1
    ny, nz, nx = 1 << ly, 1 << lz, 1 << lx

    def body(vectors, blocks, basis, transfer, coupling):
        leaf, vecs = vectors.shape[2:]
        rank = basis.shape[3]
        levels = transfer.shape[2]
        yblk = vecs // ny
        scratch = [
            pltpu.VMEM((leaf, vecs), BF),
            pltpu.VMEM((leaf, leaf), BF),
            pltpu.VMEM((leaf, rank), BF),
            pltpu.VMEM((rank, leaf), BF),
            pltpu.VMEM((levels, rank, rank), BF),
            pltpu.VMEM((levels, rank, rank), BF),
            pltpu.VMEM((6, rank, rank), BF),
            pltpu.VMEM((6, rank, rank), BF),
            pltpu.VMEM((3 * rank, rank), BF),
            pltpu.VMEM((3 * rank, lx * rank), BF),
            pltpu.VMEM((3 * rank, max(1, lz - 1) * rank), BF),
            pltpu.VMEM(((3 * lx - 2) * rank, rank), BF),
            pltpu.VMEM(((3 * lz - 2) * rank, rank), BF),
            pltpu.VMEM((3 * rank, 4 * rank), BF),
            pltpu.VMEM((3 * rank, 4 * rank), BF),
            pltpu.VMEM((vecs, rank), BF),
            pltpu.VMEM((vecs, rank), BF),
            pltpu.VMEM((vecs, rank), BF),
            pltpu.VMEM((ny, yblk, rank), BF),
            pltpu.VMEM((vecs, rank), BF),
            pltpu.VMEM((ny, yblk, rank), BF),
            pltpu.VMEM((yblk, rank), BF),
            pltpu.VMEM((nz, yblk, rank), BF),
            pltpu.VMEM((lz, yblk, rank), BF),
            pltpu.VMEM((nz, yblk, rank), BF),
            pltpu.VMEM((lx, yblk, rank), BF),
            pltpu.VMEM((nx, yblk, rank), BF),
            pltpu.VMEM((4, yblk, rank), BF),
            pltpu.VMEM((vecs, rank), BF),
            pltpu.SemaphoreType.DMA((6,)),
            pltpu.SemaphoreType.REGULAR((ny,)),
            pltpu.SemaphoreType.REGULAR,
            pltpu.SemaphoreType.DMA((9,)),
            pltpu.SemaphoreType.DMA((9,)),
        ]
        vmem = pl.BlockSpec(memory_space=pltpu.VMEM)
        near, lift, far = pl.pallas_call(
            functools.partial(kernel, (lz, lx)),
            out_shape=[
                jax.ShapeDtypeStruct((leaf, vecs), F32),
                jax.ShapeDtypeStruct((leaf, 2 * rank), BF),
                jax.ShapeDtypeStruct((vecs, rank), BF),
            ],
            in_specs=[pl.BlockSpec(memory_space=pltpu.HBM)] * 5,
            out_specs=[vmem] * 3,
            scratch_shapes=scratch,
            compiler_params=pltpu.CompilerParams(
                collective_id=0, has_side_effects=True, vmem_limit_bytes=32 * 1024 * 1024,
            ),
        )(*(pltpu.with_memory_space_constraint(whole[0, 0], pltpu.HBM) for whole in (vectors, blocks, basis, transfer, coupling)))
        out = pl.pallas_call(
            last_kernel,
            out_shape=jax.ShapeDtypeStruct((leaf, vecs), BF),
            in_specs=[vmem] * 3,
            out_specs=pl.BlockSpec(memory_space=pltpu.HBM),
            scratch_shapes=[
                pltpu.VMEM((2 * rank, vecs), BF),
                pltpu.VMEM((leaf, vecs), BF),
                pltpu.SemaphoreType.DMA((4,)),
            ],
            compiler_params=pltpu.CompilerParams(vmem_limit_bytes=24 * 1024 * 1024),
        )(near, lift, far)
        return out[None, None]

    return jax.shard_map(
        body,
        mesh=mesh,
        in_specs=(
            P("grp", "sub", None, None),
            P("grp", "sub", None, None),
            P("grp", "sub", None, None),
            P("grp", "sub", None, None, None),
            P("grp", "sub", None, None, None),
        ),
        out_specs=P("grp", "sub", None, None),
        check_vma=False,
    )
```

```python
import functools

import jax
import jax.numpy as jnp
from jax import lax
from jax.experimental import pallas as pl
from jax.experimental.pallas import tpu as pltpu
from jax.sharding import PartitionSpec as P

MESH = pl.DeviceIdType.MESH
BF = jnp.bfloat16
F32 = jnp.float32


def dot(left, right):
    return jnp.dot(left, right, preferred_element_type=F32)


def dot_nt(left, right):
    return lax.dot_general(left, right, (((1,), (1,)), ((), ())), preferred_element_type=F32)


def dot_tn(left, right):
    return lax.dot_general(left, right, (((0,), (0,)), ((), ())), preferred_element_type=F32)


def split(value):
    high = value.astype(BF)
    return high, (value - high.astype(F32)).astype(BF)


def flip(index, offset):
    out = index
    for bit in range(offset.bit_length()):
        if offset >> bit & 1:
            out = out + (1 << bit) - (2 << bit) * lax.rem(lax.div(index, 1 << bit), 2)
    return out


def level_of(offset):
    return offset.bit_length() - 1


def far_first(count):
    return [j for j in (4, 5, 3, 7, 6, 2, 1) if j < count]


def early(count, cores):
    ring = sorted(range(count), key=lambda place: min(place, count - place))
    return [place * cores + core for place in ring for core in reversed(range(cores))]


def wait_bytes(ref, sem):
    pltpu.make_async_copy(ref, ref, sem).wait()


def up_weight(product):
    high, low = split(product)
    return jnp.concatenate([high, high, low], axis=0)


def up_exact(matrix):
    return jnp.concatenate([matrix, matrix, jnp.zeros_like(matrix)], axis=0)


def wide(value):
    high, low = split(value)
    return jnp.concatenate([high, low, high], axis=1)


def times_exact(product, matrix):
    high, low = split(product)
    return dot(high, matrix) + dot(low, matrix)


def kernel(dims, x_hbm, d_hbm, u_hbm, t_hbm, b_hbm, near, lift_out, far_out,
           xv, dv, uv, ut, tv, bv,
           rt, bt, wy, wx, wzl, vx, vz, vw, vg,
           h_send, h_recv, cy_send, cy_recv, cl_send, cl_recv,
           cz_send, cz_recv, zs_send, zs_recv, x_send, x_recv,
           far_y_send, far_y,
           load_sem, z_sem, send_sem, recv_sem):
    lz, lx = dims
    ly = 3
    ny, nz, nx = 1 << ly, 1 << lz, 1 << lx
    leaf, vecs = x_hbm.shape
    rank = u_hbm.shape[1]
    yblk = vecs // ny
    sub, grp = lax.axis_index("sub"), lax.axis_index("grp")
    y, z = lax.rem(sub, ny), lax.div(sub, ny)

    def y_peer(j):
        return {"sub": z * ny + flip(y, j)}

    def z_peer(j):
        return {"sub": flip(z, j) * ny + y}

    def x_peer(j):
        return {"grp": flip(grp, j)}

    def rows(index, size):
        return pl.ds(pl.multiple_of(index * size, size), size)

    def send(src, dst, group, peer):
        pltpu.make_async_remote_copy(
            src_ref=src, dst_ref=dst, send_sem=send_sem.at[group], recv_sem=recv_sem.at[group],
            device_id=peer, device_id_type=MESH,
        ).start()

    barrier = pltpu.get_barrier_semaphore()

    def greet(sem, peer):
        pl.semaphore_signal(sem, inc=1, device_id=peer, device_id_type=MESH)

    for j in far_first(ny):
        greet(barrier, y_peer(j))
    for place in reversed(range(nz)):
        @pl.when(z < place)
        def _():
            greet(barrier, {"sub": place * ny + y})
    for j in far_first(nx):
        greet(barrier, x_peer(j))

    head = leaf // 2
    loads = {}
    for i, (name, src, dst) in enumerate((
        ("u", u_hbm, uv),
        ("x0", x_hbm.at[pl.ds(0, head)], xv.at[pl.ds(0, head)]),
        ("x1", x_hbm.at[pl.ds(head, head)], xv.at[pl.ds(head, head)]),
        ("t", t_hbm, tv),
        ("d", d_hbm, dv),
        ("b", b_hbm, bv),
    )):
        loads[name] = pltpu.make_async_copy(src, dst, load_sem.at[i])
        loads[name].start()

    pair = lax.div(y, 2)
    outward = 2 * lax.rem(y, 2) - 1

    def spread(src, dst, group):
        for k in (3, 2, 1):
            target = lax.rem(y + k * outward + ny, ny)
            other = lax.div(target, 2)
            slot = lax.rem(pair + other, 2) + 2 * lax.rem(lax.div(pair, 2) + lax.div(other, 2), 2)
            send(src.at[1], dst.at[slot], group, {"sub": z * ny + target})
        send(src.at[2], dst.at[4], group, y_peer(6))

    def climb(base, levels):
        product = tv[base].astype(F32)
        chain = [product]
        for level in range(1, levels):
            product = times_exact(product, tv[base + level])
            chain.append(product)
        return chain

    def down(products, base, levels):
        parts = [bv[base].T]
        for i in range(1, levels):
            parts.append(up_weight(times_exact(products[i - 1], bv[base + i]).T))
        return jnp.concatenate(parts, axis=0)

    def near_part(part, parts):
        size = vecs // parts
        at = pl.ds(part * size, size)
        near[:, at] = dot(dv[...], xv[:, at])

    loads["t"].wait()
    ty = climb(0, ly)
    wy[...] = up_weight(ty[ly - 1])
    loads["u"].wait()
    ut[...] = uv[...].T
    loads["x0"].wait()
    hat_t = dot(ut[:, :head], xv[:head, :])
    loads["x1"].wait()
    hat = (hat_t + dot(ut[:, head:], xv[head:, :])).T
    hat_w = wide(hat)
    cy_send[...] = dot(hat_w, wy[...]).astype(BF)
    pl.semaphore_wait(barrier, ny - 1 + nx - 1 + z)
    for place in range(nz):
        @pl.when(z > place)
        def _():
            greet(z_sem, {"sub": place * ny + y})
    for j in far_first(ny):
        send(cy_send.at[rows(flip(y, j), yblk)], cy_recv.at[j], 0, y_peer(j))

    cl_send[...] = dot(hat_w[:, :2 * rank], jnp.concatenate([tv[0], tv[0]], axis=0)).astype(BF)
    h_send[...] = hat.astype(BF)
    tz = climb(ly, lz + lx - 1)
    wx[...] = jnp.concatenate([up_weight(product) for product in tz[lz - 1:]], axis=1)
    if lz > 1:
        wzl[...] = jnp.concatenate([up_exact(tv[ly])] + [up_weight(tz[i]) for i in range(1, lz - 1)], axis=1)
    lift_out[...] = jnp.concatenate(split(dot(uv[...], tv[0])), axis=1)
    loads["d"].wait()
    near_part(0, 2)
    loads["b"].wait()
    vx[...] = down(climb(ly + lz, lx), ly + lz, lx)

    wait_bytes(cy_recv.at[pl.ds(1, ny - 1)], recv_sem.at[0])
    mid = cy_send[rows(y, yblk), :].astype(F32)
    for j in range(1, ny):
        mid = mid + cy_recv[j].astype(F32)
    mid_w = wide(mid)
    share = dot(mid_w, wx[...])
    for i in range(lx):
        x_send[i] = share[:, i * rank:(i + 1) * rank].astype(BF)
    for place in early(nx // 2, 2):
        @pl.when(grp != place)
        def _():
            apart = flip(grp, place)
            level = sum(jnp.where(apart >= 1 << i, 1, 0) for i in range(1, lx))
            send(x_send.at[level], x_recv.at[apart], 6, {"grp": place})
    zs_send[0] = mid.astype(BF)
    if lz > 1:
        zl = dot(mid_w, wzl[...])
        for i in range(lz - 1):
            zs_send[i + 1] = zl[:, i * rank:(i + 1) * rank].astype(BF)

    @pl.when(z < nz - 1)
    def _():
        pl.semaphore_wait(z_sem, nz - 1 - z)

    for j in far_first(nz):
        send(zs_send.at[level_of(j)], zs_recv.at[j], 4, z_peer(j))
    for j in far_first(ny):
        send(cl_send.at[rows(flip(y, j), yblk)], cl_recv.at[j], 8, y_peer(j))
    spread(t_hbm, rt, 1)
    spread(b_hbm, bt, 5)
    send(h_send, h_recv, 2, y_peer(1))

    wait_bytes(x_recv.at[pl.ds(1, nx - 1)], recv_sem.at[6])
    parts = [x_recv[1]]
    for level in range(1, lx):
        parts.append(wide(functools.reduce(jnp.add, [x_recv[j].astype(F32) for j in range(1 << level, 2 << level)])))
    top = dot(jnp.concatenate(parts, axis=1), vx[...])
    cz_send[...] = top.astype(BF)
    for place in range(nz):
        @pl.when(z != place)
        def _():
            send(cz_send, cz_recv.at[flip(z, place)], 3, {"sub": place * ny + y})

    vz[...] = down(tz, ly, lz)

    rt[0] = tv[1]
    rt[5] = tv[2]
    bt[0] = bv[1]
    bt[5] = bv[2]
    wait_bytes(rt.at[pl.ds(1, 4)], recv_sem.at[1])
    lifts = []
    for quad in range(2):
        both = jnp.concatenate([rt[2 * quad], rt[2 * quad + 1]], axis=0)
        lifts.append(dot(both, rt[5 - quad]))
    lifts = jnp.concatenate(lifts, axis=0)
    whole = dot(wide(lifts), wx[:, :rank])
    for r in range(4):
        at = slice(r * rank, (r + 1) * rank)
        vw[:, at] = up_weight(lifts[at].T)
        vg[:, at] = up_weight(whole[at].T)
    wait_bytes(zs_recv.at[pl.ds(1, nz - 1)], recv_sem.at[4])
    parts = [zs_recv[1]]
    for level in range(1, lz):
        parts.append(wide(functools.reduce(jnp.add, [zs_recv[j].astype(F32) for j in range(1 << level, 2 << level)])))
    mid_far = dot(jnp.concatenate(parts, axis=1), vz[...])

    wait_bytes(cl_recv.at[pl.ds(1, ny - 1)], recv_sem.at[8])
    given = [cl_send[rows(y, yblk), :]] + [cl_recv[j] for j in range(1, ny)]
    sums = [given[2 * r].astype(F32) + given[2 * r + 1].astype(F32) for r in range(4)]
    quads = []
    for quad in range(2):
        left = jnp.concatenate([*split(sums[2 * quad]), *split(sums[2 * quad + 1])], axis=1)
        right = [rt[2 * quad]] * 2 + [rt[2 * quad + 1]] * 2
        quads.append(dot(left, jnp.concatenate(right, axis=0)))
    wait_bytes(bt.at[pl.ds(1, 4)], recv_sem.at[5])
    local = []
    for quad in range(2):
        both = jnp.concatenate([rt[2 * quad], rt[2 * quad + 1]], axis=0)
        high, low = split(dot(both, bt[5 - quad]))
        seen = dot_nt(wide(quads[1 - quad]), jnp.concatenate([high, high, low], axis=1))
        for half in range(2):
            r = 2 * quad + half
            sibling = jnp.concatenate(split(sums[r ^ 1]), axis=1)
            local.append(seen[:, half * rank:(half + 1) * rank] + dot_nt(sibling, jnp.concatenate([bt[r]] * 2, axis=1)))
    local = jnp.concatenate(local, axis=1) + dot(wide(mid_far), vw[...])

    wait_bytes(cz_recv.at[pl.ds(1, nz - 1)], recv_sem.at[3])
    for j in range(1, nz):
        top = top + cz_recv[j].astype(F32)
    pair_far = (local + dot(wide(top), vg[...])).astype(BF)
    for r in range(4):
        far_y_send[r] = pair_far[:, r * rank:(r + 1) * rank]
    for place in early(ny, 1):
        @pl.when(y != place)
        def _():
            send(far_y_send.at[lax.div(flip(y, place), 2)], far_y.at[rows(y, yblk)], 7, {"sub": z * ny + place})
    far_y[rows(y, yblk), :] = far_y_send[0]

    wait_bytes(h_recv, recv_sem.at[2])
    far = dot_nt(h_recv[...], bv[0]).astype(BF)
    near_part(1, 2)
    near[...] += dot_nt(uv[...], far)
    wait_bytes(far_y.at[pl.ds(0, (ny - 1) * yblk)], recv_sem.at[7])
    far_out[...] = far_y[...]

    wait_bytes(cy_recv.at[pl.ds(1, ny - 1)], send_sem.at[0])
    wait_bytes(rt.at[pl.ds(1, 4)], send_sem.at[1])
    wait_bytes(h_send, send_sem.at[2])
    wait_bytes(cz_recv.at[pl.ds(1, nz - 1)], send_sem.at[3])
    wait_bytes(zs_recv.at[pl.ds(1, nz - 1)], send_sem.at[4])
    wait_bytes(bt.at[pl.ds(1, 4)], send_sem.at[5])
    wait_bytes(x_recv.at[pl.ds(1, nx - 1)], send_sem.at[6])
    wait_bytes(far_y.at[pl.ds(0, (ny - 1) * yblk)], send_sem.at[7])
    wait_bytes(cl_recv.at[pl.ds(1, ny - 1)], send_sem.at[8])


def last_kernel(near, lift, far, o_hbm, far_t, ov, store_sem):
    leaf = near.shape[0]
    chunks = store_sem.shape[0]
    tile = leaf // chunks
    far_t[...] = jnp.concatenate([far[...].T] * 2, axis=0)
    stores = []
    for step in range(chunks):
        at = pl.ds(step * tile, tile)
        ov[at, :] = (near[at, :] + dot(lift[at, :], far_t[...])).astype(BF)
        store = pltpu.make_async_copy(ov.at[at], o_hbm.at[at], store_sem.at[step])
        store.start()
        stores.append(store)
    for store in stores:
        store.wait()


def solution(mesh):
    ly = 3
    lz = mesh.shape["sub"].bit_length() - 1 - ly
    lx = mesh.shape["grp"].bit_length() - 1
    ny, nz, nx = 1 << ly, 1 << lz, 1 << lx

    def body(vectors, blocks, basis, transfer, coupling):
        leaf, vecs = vectors.shape[2:]
        rank = basis.shape[3]
        levels = transfer.shape[2]
        yblk = vecs // ny
        scratch = [
            pltpu.VMEM((leaf, vecs), BF),
            pltpu.VMEM((leaf, leaf), BF),
            pltpu.VMEM((leaf, rank), BF),
            pltpu.VMEM((rank, leaf), BF),
            pltpu.VMEM((levels, rank, rank), BF),
            pltpu.VMEM((levels, rank, rank), BF),
            pltpu.VMEM((6, rank, rank), BF),
            pltpu.VMEM((6, rank, rank), BF),
            pltpu.VMEM((3 * rank, rank), BF),
            pltpu.VMEM((3 * rank, lx * rank), BF),
            pltpu.VMEM((3 * rank, max(1, lz - 1) * rank), BF),
            pltpu.VMEM(((3 * lx - 2) * rank, rank), BF),
            pltpu.VMEM(((3 * lz - 2) * rank, rank), BF),
            pltpu.VMEM((3 * rank, 4 * rank), BF),
            pltpu.VMEM((3 * rank, 4 * rank), BF),
            pltpu.VMEM((vecs, rank), BF),
            pltpu.VMEM((vecs, rank), BF),
            pltpu.VMEM((vecs, rank), BF),
            pltpu.VMEM((ny, yblk, rank), BF),
            pltpu.VMEM((vecs, rank), BF),
            pltpu.VMEM((ny, yblk, rank), BF),
            pltpu.VMEM((yblk, rank), BF),
            pltpu.VMEM((nz, yblk, rank), BF),
            pltpu.VMEM((lz, yblk, rank), BF),
            pltpu.VMEM((nz, yblk, rank), BF),
            pltpu.VMEM((lx, yblk, rank), BF),
            pltpu.VMEM((nx, yblk, rank), BF),
            pltpu.VMEM((4, yblk, rank), BF),
            pltpu.VMEM((vecs, rank), BF),
            pltpu.SemaphoreType.DMA((6,)),
            pltpu.SemaphoreType.REGULAR,
            pltpu.SemaphoreType.DMA((9,)),
            pltpu.SemaphoreType.DMA((9,)),
        ]
        vmem = pl.BlockSpec(memory_space=pltpu.VMEM)
        near, lift, far = pl.pallas_call(
            functools.partial(kernel, (lz, lx)),
            out_shape=[
                jax.ShapeDtypeStruct((leaf, vecs), F32),
                jax.ShapeDtypeStruct((leaf, 2 * rank), BF),
                jax.ShapeDtypeStruct((vecs, rank), BF),
            ],
            in_specs=[pl.BlockSpec(memory_space=pltpu.HBM)] * 5,
            out_specs=[vmem] * 3,
            scratch_shapes=scratch,
            compiler_params=pltpu.CompilerParams(
                collective_id=0, has_side_effects=True, vmem_limit_bytes=32 * 1024 * 1024,
            ),
        )(*(pltpu.with_memory_space_constraint(whole[0, 0], pltpu.HBM) for whole in (vectors, blocks, basis, transfer, coupling)))
        out = pl.pallas_call(
            last_kernel,
            out_shape=jax.ShapeDtypeStruct((leaf, vecs), BF),
            in_specs=[vmem] * 3,
            out_specs=pl.BlockSpec(memory_space=pltpu.HBM),
            scratch_shapes=[
                pltpu.VMEM((2 * rank, vecs), BF),
                pltpu.VMEM((leaf, vecs), BF),
                pltpu.SemaphoreType.DMA((4,)),
            ],
            compiler_params=pltpu.CompilerParams(vmem_limit_bytes=24 * 1024 * 1024),
        )(near, lift, far)
        return out[None, None]

    return jax.shard_map(
        body,
        mesh=mesh,
        in_specs=(
            P("grp", "sub", None, None),
            P("grp", "sub", None, None),
            P("grp", "sub", None, None),
            P("grp", "sub", None, None, None),
            P("grp", "sub", None, None, None),
        ),
        out_specs=P("grp", "sub", None, None),
        check_vma=False,
    )
```

```python
import functools

import jax
import jax.numpy as jnp
from jax import lax
from jax.experimental import pallas as pl
from jax.experimental.pallas import tpu as pltpu
from jax.sharding import PartitionSpec as P

MESH = pl.DeviceIdType.MESH
BF = jnp.bfloat16
F32 = jnp.float32
CHUNKS = 2


def dot(left, right):
    return jnp.dot(left, right, preferred_element_type=F32)


def dot_nt(left, right):
    return lax.dot_general(left, right, (((1,), (1,)), ((), ())), preferred_element_type=F32)


def dot_tn(left, right):
    return lax.dot_general(left, right, (((0,), (0,)), ((), ())), preferred_element_type=F32)


def split(value):
    high = value.astype(BF)
    return high, (value - high.astype(F32)).astype(BF)


def flip(index, offset):
    out = index
    for bit in range(offset.bit_length()):
        if offset >> bit & 1:
            out = out + (1 << bit) - (2 << bit) * lax.rem(lax.div(index, 1 << bit), 2)
    return out


def level_of(offset):
    return offset.bit_length() - 1


def far_first(count):
    return [j for j in (4, 5, 3, 7, 6, 2, 1) if j < count]


def early(count, cores):
    ring = sorted(range(count), key=lambda place: min(place, count - place))
    return [place * cores + core for place in ring for core in reversed(range(cores))]


def wait_bytes(ref, sem):
    pltpu.make_async_copy(ref, ref, sem).wait()


def up_weight(product):
    high, low = split(product)
    return jnp.concatenate([high, high, low], axis=0)


def up_exact(matrix):
    return jnp.concatenate([matrix, matrix, jnp.zeros_like(matrix)], axis=0)


def wide(value):
    high, low = split(value)
    return jnp.concatenate([high, low, high], axis=1)


def times_exact(product, matrix):
    high, low = split(product)
    return dot(high, matrix) + dot(low, matrix)


def kernel(dims, x_hbm, d_hbm, u_hbm, t_hbm, b_hbm, near, lift_out, far_out,
           xv, dv, uv, ut, tv, bv,
           rt, bt, wy, wx, wzl, vx, vz, vw, vg,
           h_send, h_recv, cy_send, cy_recv, cl_send, cl_recv,
           cz_send, cz_recv, zs_send, zs_recv, x_send, x_recv,
           far_y_send, far_y,
           load_sem, z_sem, send_sem, recv_sem):
    lz, lx = dims
    ly = 3
    ny, nz, nx = 1 << ly, 1 << lz, 1 << lx
    leaf, vecs = x_hbm.shape
    rank = u_hbm.shape[1]
    yblk = vecs // ny
    half = yblk // CHUNKS
    sub, grp = lax.axis_index("sub"), lax.axis_index("grp")
    y, z = lax.rem(sub, ny), lax.div(sub, ny)

    def y_peer(j):
        return {"sub": z * ny + flip(y, j)}

    def z_peer(j):
        return {"sub": flip(z, j) * ny + y}

    def x_peer(j):
        return {"grp": flip(grp, j)}

    def rows(index, size):
        return pl.ds(pl.multiple_of(index * size, size), size)

    def part(index, c):
        return pl.ds(pl.multiple_of(index * yblk + c * half, half), half)

    def send(src, dst, group, peer):
        pltpu.make_async_remote_copy(
            src_ref=src, dst_ref=dst, send_sem=send_sem.at[group], recv_sem=recv_sem.at[group],
            device_id=peer, device_id_type=MESH,
        ).start()

    head = leaf // 2
    loads = {}
    for i, (name, src, dst) in enumerate((
        ("t", t_hbm.at[pl.ds(0, ly)], tv.at[pl.ds(0, ly)]),
        ("u", u_hbm, uv),
        ("x0", x_hbm.at[pl.ds(0, head)], xv.at[pl.ds(0, head)]),
        ("x1", x_hbm.at[pl.ds(head, head)], xv.at[pl.ds(head, head)]),
        ("t1", t_hbm.at[pl.ds(ly, lz + lx)], tv.at[pl.ds(ly, lz + lx)]),
        ("b", b_hbm, bv),
        ("d", d_hbm, dv),
    )):
        loads[name] = pltpu.make_async_copy(src, dst, load_sem.at[i])
    for name in ("t", "u", "x0", "x1"):
        loads[name].start()

    barrier = pltpu.get_barrier_semaphore()

    def greet(sem, peer):
        pl.semaphore_signal(sem, inc=1, device_id=peer, device_id_type=MESH)

    for j in far_first(ny):
        greet(barrier, y_peer(j))
    for place in reversed(range(nz)):
        @pl.when(z < place)
        def _():
            greet(barrier, {"sub": place * ny + y})
    for j in far_first(nx):
        greet(barrier, x_peer(j))

    pair = lax.div(y, 2)
    outward = 2 * lax.rem(y, 2) - 1

    def spread(src, dst, group):
        for k in (3, 2, 1):
            target = lax.rem(y + k * outward + ny, ny)
            other = lax.div(target, 2)
            slot = lax.rem(pair + other, 2) + 2 * lax.rem(lax.div(pair, 2) + lax.div(other, 2), 2)
            send(src.at[1], dst.at[slot], group, {"sub": z * ny + target})
        send(src.at[2], dst.at[4], group, y_peer(6))

    def climb(base, levels):
        product = tv[base].astype(F32)
        chain = [product]
        for level in range(1, levels):
            product = times_exact(product, tv[base + level])
            chain.append(product)
        return chain

    def down(products, base, levels):
        parts = [bv[base].T]
        for i in range(1, levels):
            parts.append(up_weight(times_exact(products[i - 1], bv[base + i]).T))
        return jnp.concatenate(parts, axis=0)

    def near_part(part, parts):
        size = vecs // parts
        at = pl.ds(part * size, size)
        near[:, at] = dot(dv[...], xv[:, at])

    loads["t"].wait()
    ty = climb(0, ly)
    wy[...] = up_weight(ty[ly - 1])
    loads["u"].wait()
    ut[...] = uv[...].T
    loads["x0"].wait()
    hat_t = dot(ut[:, :head], xv[:head, :])
    loads["x1"].wait()
    for name in ("t1", "b", "d"):
        loads[name].start()
    hat = (hat_t + dot(ut[:, head:], xv[head:, :])).T
    hat_w = wide(hat)
    cy_send[...] = dot(hat_w, wy[...]).astype(BF)
    pl.semaphore_wait(barrier, ny - 1 + nx - 1 + z)
    for c in range(CHUNKS):
        for j in far_first(ny):
            send(cy_send.at[part(flip(y, j), c)], cy_recv.at[c, j], 5 + c, y_peer(j))
    for place in range(nz):
        @pl.when(z > place)
        def _():
            greet(z_sem, {"sub": place * ny + y})

    cl_send[...] = dot(hat_w[:, :2 * rank], jnp.concatenate([tv[0], tv[0]], axis=0)).astype(BF)
    h_send[...] = hat.astype(BF)
    loads["t1"].wait()
    tz = climb(ly, lz + lx - 1)
    wx[...] = jnp.concatenate([up_weight(product) for product in tz[lz - 1:]], axis=1)
    if lz > 1:
        wzl[...] = jnp.concatenate([up_exact(tv[ly])] + [up_weight(tz[i]) for i in range(1, lz - 1)], axis=1)
    lift_out[...] = jnp.concatenate(split(dot(uv[...], tv[0])), axis=1)
    loads["d"].wait()
    near_part(0, 2)
    loads["b"].wait()
    vx[...] = down(climb(ly + lz, lx), ly + lz, lx)

    mids = []
    for c in range(CHUNKS):
        wait_bytes(cy_recv.at[c, pl.ds(1, ny - 1)], recv_sem.at[5 + c])
        mid = cy_send[part(y, c), :].astype(F32)
        for j in range(1, ny):
            mid = mid + cy_recv[c, j].astype(F32)
        mids.append(wide(mid))
        share = dot(mids[c], wx[...])
        for i in range(lx):
            x_send[c, i] = share[:, i * rank:(i + 1) * rank].astype(BF)
        for place in early(nx // 2, 2):
            @pl.when(grp != place)
            def _():
                apart = flip(grp, place)
                level = sum(jnp.where(apart >= 1 << i, 1, 0) for i in range(1, lx))
                send(x_send.at[c, level], x_recv.at[c, apart], 7 + c, {"grp": place})

    mid_w = jnp.concatenate(mids, axis=0)
    zs_send[0] = mid_w[:, :rank]
    if lz > 1:
        zl = dot(mid_w, wzl[...])
        for i in range(lz - 1):
            zs_send[i + 1] = zl[:, i * rank:(i + 1) * rank].astype(BF)

    @pl.when(z < nz - 1)
    def _():
        pl.semaphore_wait(z_sem, nz - 1 - z)

    for j in far_first(nz):
        send(zs_send.at[level_of(j)], zs_recv.at[j], 4, z_peer(j))

    tops = []
    for c in range(CHUNKS):
        wait_bytes(x_recv.at[c, pl.ds(1, nx - 1)], recv_sem.at[7 + c])
        parts = [x_recv[c, 1]]
        for level in range(1, lx):
            parts.append(wide(functools.reduce(jnp.add, [x_recv[c, j].astype(F32) for j in range(1 << level, 2 << level)])))
        top = dot(jnp.concatenate(parts, axis=1), vx[...])
        tops.append(top)
        cz_send[c] = top.astype(BF)
        for place in range(nz):
            @pl.when(z != place)
            def _():
                send(cz_send.at[c], cz_recv.at[c, flip(z, place)], 9 + c, {"sub": place * ny + y})

    for j in far_first(ny):
        send(cl_send.at[rows(flip(y, j), yblk)], cl_recv.at[j], 0, y_peer(j))
    spread(t_hbm, rt, 1)
    spread(b_hbm, bt, 3)
    send(h_send, h_recv, 2, y_peer(1))
    vz[...] = down(tz, ly, lz)

    rt[0] = tv[1]
    rt[5] = tv[2]
    bt[0] = bv[1]
    bt[5] = bv[2]
    wait_bytes(rt.at[pl.ds(1, 4)], recv_sem.at[1])
    lifts = []
    for quad in range(2):
        both = jnp.concatenate([rt[2 * quad], rt[2 * quad + 1]], axis=0)
        lifts.append(dot(both, rt[5 - quad]))
    lifts = jnp.concatenate(lifts, axis=0)
    whole = dot(wide(lifts), wx[:, :rank])
    for r in range(4):
        at = slice(r * rank, (r + 1) * rank)
        vw[:, at] = up_weight(lifts[at].T)
        vg[:, at] = up_weight(whole[at].T)
    wait_bytes(zs_recv.at[pl.ds(1, nz - 1)], recv_sem.at[4])
    parts = [zs_recv[1]]
    for level in range(1, lz):
        parts.append(wide(functools.reduce(jnp.add, [zs_recv[j].astype(F32) for j in range(1 << level, 2 << level)])))
    mid_far = dot(jnp.concatenate(parts, axis=1), vz[...])

    wait_bytes(cl_recv.at[pl.ds(1, ny - 1)], recv_sem.at[0])
    given = [cl_send[rows(y, yblk), :]] + [cl_recv[j] for j in range(1, ny)]
    sums = [given[2 * r].astype(F32) + given[2 * r + 1].astype(F32) for r in range(4)]
    quads = []
    for quad in range(2):
        left = jnp.concatenate([*split(sums[2 * quad]), *split(sums[2 * quad + 1])], axis=1)
        right = [rt[2 * quad]] * 2 + [rt[2 * quad + 1]] * 2
        quads.append(dot(left, jnp.concatenate(right, axis=0)))
    wait_bytes(bt.at[pl.ds(1, 4)], recv_sem.at[3])
    local = []
    for quad in range(2):
        both = jnp.concatenate([rt[2 * quad], rt[2 * quad + 1]], axis=0)
        high, low = split(dot(both, bt[5 - quad]))
        seen = dot_nt(wide(quads[1 - quad]), jnp.concatenate([high, high, low], axis=1))
        for side in range(2):
            r = 2 * quad + side
            sibling = jnp.concatenate(split(sums[r ^ 1]), axis=1)
            local.append(seen[:, side * rank:(side + 1) * rank] + dot_nt(sibling, jnp.concatenate([bt[r]] * 2, axis=1)))
    local = jnp.concatenate(local, axis=1) + dot(wide(mid_far), vw[...])

    for c in range(CHUNKS):
        wait_bytes(cz_recv.at[c, pl.ds(1, nz - 1)], recv_sem.at[9 + c])
        top = tops[c]
        for j in range(1, nz):
            top = top + cz_recv[c, j].astype(F32)
        at = pl.ds(c * half, half)
        pair_far = (local[c * half:(c + 1) * half] + dot(wide(top), vg[...])).astype(BF)
        for r in range(4):
            far_y_send[r, at, :] = pair_far[:, r * rank:(r + 1) * rank]
        for place in early(ny, 1):
            @pl.when(y != place)
            def _():
                send(far_y_send.at[lax.div(flip(y, place), 2), at], far_y.at[part(y, c)], 11 + c, {"sub": z * ny + place})
        far_y[part(y, c), :] = far_y_send[0, at, :]

    wait_bytes(h_recv, recv_sem.at[2])
    far = dot_nt(h_recv[...], bv[0]).astype(BF)
    near_part(1, 2)
    near[...] += dot_nt(uv[...], far)
    for c in range(CHUNKS):
        wait_bytes(far_y.at[pl.ds(0, (ny - 1) * half)], recv_sem.at[11 + c])
    far_out[...] = far_y[...]

    wait_bytes(cl_recv.at[pl.ds(1, ny - 1)], send_sem.at[0])
    wait_bytes(rt.at[pl.ds(1, 4)], send_sem.at[1])
    wait_bytes(h_send, send_sem.at[2])
    wait_bytes(bt.at[pl.ds(1, 4)], send_sem.at[3])
    wait_bytes(zs_recv.at[pl.ds(1, nz - 1)], send_sem.at[4])
    for c in range(CHUNKS):
        wait_bytes(cy_recv.at[c, pl.ds(1, ny - 1)], send_sem.at[5 + c])
        wait_bytes(x_recv.at[c, pl.ds(1, nx - 1)], send_sem.at[7 + c])
        wait_bytes(cz_recv.at[c, pl.ds(1, nz - 1)], send_sem.at[9 + c])
        wait_bytes(far_y.at[pl.ds(0, (ny - 1) * half)], send_sem.at[11 + c])


def last_kernel(near, lift, far, o_hbm, far_t, ov, store_sem):
    leaf = near.shape[0]
    chunks = store_sem.shape[0]
    tile = leaf // chunks
    far_t[...] = jnp.concatenate([far[...].T] * 2, axis=0)
    stores = []
    for step in range(chunks):
        at = pl.ds(step * tile, tile)
        ov[at, :] = (near[at, :] + dot(lift[at, :], far_t[...])).astype(BF)
        store = pltpu.make_async_copy(ov.at[at], o_hbm.at[at], store_sem.at[step])
        store.start()
        stores.append(store)
    for store in stores:
        store.wait()


def solution(mesh):
    ly = 3
    lz = mesh.shape["sub"].bit_length() - 1 - ly
    lx = mesh.shape["grp"].bit_length() - 1
    ny, nz, nx = 1 << ly, 1 << lz, 1 << lx

    def body(vectors, blocks, basis, transfer, coupling):
        leaf, vecs = vectors.shape[2:]
        rank = basis.shape[3]
        levels = transfer.shape[2]
        yblk = vecs // ny
        scratch = [
            pltpu.VMEM((leaf, vecs), BF),
            pltpu.VMEM((leaf, leaf), BF),
            pltpu.VMEM((leaf, rank), BF),
            pltpu.VMEM((rank, leaf), BF),
            pltpu.VMEM((levels, rank, rank), BF),
            pltpu.VMEM((levels, rank, rank), BF),
            pltpu.VMEM((6, rank, rank), BF),
            pltpu.VMEM((6, rank, rank), BF),
            pltpu.VMEM((3 * rank, rank), BF),
            pltpu.VMEM((3 * rank, lx * rank), BF),
            pltpu.VMEM((3 * rank, max(1, lz - 1) * rank), BF),
            pltpu.VMEM(((3 * lx - 2) * rank, rank), BF),
            pltpu.VMEM(((3 * lz - 2) * rank, rank), BF),
            pltpu.VMEM((3 * rank, 4 * rank), BF),
            pltpu.VMEM((3 * rank, 4 * rank), BF),
            pltpu.VMEM((vecs, rank), BF),
            pltpu.VMEM((vecs, rank), BF),
            pltpu.VMEM((vecs, rank), BF),
            pltpu.VMEM((CHUNKS, ny, yblk // CHUNKS, rank), BF),
            pltpu.VMEM((vecs, rank), BF),
            pltpu.VMEM((ny, yblk, rank), BF),
            pltpu.VMEM((CHUNKS, yblk // CHUNKS, rank), BF),
            pltpu.VMEM((CHUNKS, nz, yblk // CHUNKS, rank), BF),
            pltpu.VMEM((lz, yblk, rank), BF),
            pltpu.VMEM((nz, yblk, rank), BF),
            pltpu.VMEM((CHUNKS, lx, yblk // CHUNKS, rank), BF),
            pltpu.VMEM((CHUNKS, nx, yblk // CHUNKS, rank), BF),
            pltpu.VMEM((4, yblk, rank), BF),
            pltpu.VMEM((vecs, rank), BF),
            pltpu.SemaphoreType.DMA((7,)),
            pltpu.SemaphoreType.REGULAR,
            pltpu.SemaphoreType.DMA((13,)),
            pltpu.SemaphoreType.DMA((13,)),
        ]
        vmem = pl.BlockSpec(memory_space=pltpu.VMEM)
        near, lift, far = pl.pallas_call(
            functools.partial(kernel, (lz, lx)),
            out_shape=[
                jax.ShapeDtypeStruct((leaf, vecs), F32),
                jax.ShapeDtypeStruct((leaf, 2 * rank), BF),
                jax.ShapeDtypeStruct((vecs, rank), BF),
            ],
            in_specs=[pl.BlockSpec(memory_space=pltpu.HBM)] * 5,
            out_specs=[vmem] * 3,
            scratch_shapes=scratch,
            compiler_params=pltpu.CompilerParams(
                collective_id=0, has_side_effects=True, vmem_limit_bytes=32 * 1024 * 1024,
            ),
        )(*(pltpu.with_memory_space_constraint(whole[0, 0], pltpu.HBM) for whole in (vectors, blocks, basis, transfer, coupling)))
        out = pl.pallas_call(
            last_kernel,
            out_shape=jax.ShapeDtypeStruct((leaf, vecs), BF),
            in_specs=[vmem] * 3,
            out_specs=pl.BlockSpec(memory_space=pltpu.HBM),
            scratch_shapes=[
                pltpu.VMEM((2 * rank, vecs), BF),
                pltpu.VMEM((leaf, vecs), BF),
                pltpu.SemaphoreType.DMA((4,)),
            ],
            compiler_params=pltpu.CompilerParams(vmem_limit_bytes=24 * 1024 * 1024),
        )(near, lift, far)
        return out[None, None]

    return jax.shard_map(
        body,
        mesh=mesh,
        in_specs=(
            P("grp", "sub", None, None),
            P("grp", "sub", None, None),
            P("grp", "sub", None, None),
            P("grp", "sub", None, None, None),
            P("grp", "sub", None, None, None),
        ),
        out_specs=P("grp", "sub", None, None),
        check_vma=False,
    )
```

```python
import functools

import jax
import jax.numpy as jnp
from jax import lax
from jax.experimental import pallas as pl
from jax.experimental.pallas import tpu as pltpu
from jax.sharding import PartitionSpec as P

MESH = pl.DeviceIdType.MESH
BF = jnp.bfloat16
F32 = jnp.float32
CHUNKS = 1


def dot(left, right):
    return jnp.dot(left, right, preferred_element_type=F32)


def dot_nt(left, right):
    return lax.dot_general(left, right, (((1,), (1,)), ((), ())), preferred_element_type=F32)


def dot_tn(left, right):
    return lax.dot_general(left, right, (((0,), (0,)), ((), ())), preferred_element_type=F32)


def split(value):
    high = value.astype(BF)
    return high, (value - high.astype(F32)).astype(BF)


def flip(index, offset):
    out = index
    for bit in range(offset.bit_length()):
        if offset >> bit & 1:
            out = out + (1 << bit) - (2 << bit) * lax.rem(lax.div(index, 1 << bit), 2)
    return out


def level_of(offset):
    return offset.bit_length() - 1


def far_first(count):
    return [j for j in (4, 5, 3, 7, 6, 2, 1) if j < count]


def early(count, cores):
    ring = sorted(range(count), key=lambda place: min(place, count - place))
    return [place * cores + core for place in ring for core in reversed(range(cores))]


def wait_bytes(ref, sem):
    pltpu.make_async_copy(ref, ref, sem).wait()


def up_weight(product):
    high, low = split(product)
    return jnp.concatenate([high, high, low], axis=0)


def up_exact(matrix):
    return jnp.concatenate([matrix, matrix, jnp.zeros_like(matrix)], axis=0)


def wide(value):
    high, low = split(value)
    return jnp.concatenate([high, low, high], axis=1)


def times_exact(product, matrix):
    high, low = split(product)
    return dot(high, matrix) + dot(low, matrix)


def kernel(dims, x_hbm, d_hbm, u_hbm, t_hbm, b_hbm, near, lift_out, far_out,
           xv, dv, uv, ut, tv, bv,
           rt, bt, wy, wx, wzl, vx, vz, vw, vg,
           h_send, h_recv, cy_send, cy_recv, cl_send, cl_recv,
           cz_send, cz_recv, zs_send, zs_recv, x_send, x_recv,
           far_y_send, far_y,
           load_sem, z_sem, send_sem, recv_sem):
    lz, lx = dims
    ly = 3
    ny, nz, nx = 1 << ly, 1 << lz, 1 << lx
    leaf, vecs = x_hbm.shape
    rank = u_hbm.shape[1]
    yblk = vecs // ny
    half = yblk // CHUNKS
    sub, grp = lax.axis_index("sub"), lax.axis_index("grp")
    y, z = lax.rem(sub, ny), lax.div(sub, ny)

    def y_peer(j):
        return {"sub": z * ny + flip(y, j)}

    def z_peer(j):
        return {"sub": flip(z, j) * ny + y}

    def x_peer(j):
        return {"grp": flip(grp, j)}

    def rows(index, size):
        return pl.ds(pl.multiple_of(index * size, size), size)

    def part(index, c):
        return pl.ds(pl.multiple_of(index * yblk + c * half, half), half)

    def send(src, dst, group, peer):
        pltpu.make_async_remote_copy(
            src_ref=src, dst_ref=dst, send_sem=send_sem.at[group], recv_sem=recv_sem.at[group],
            device_id=peer, device_id_type=MESH,
        ).start()

    head = leaf // 2
    loads = {}
    for i, (name, src, dst) in enumerate((
        ("t", t_hbm.at[pl.ds(0, ly)], tv.at[pl.ds(0, ly)]),
        ("u", u_hbm, uv),
        ("x0", x_hbm.at[pl.ds(0, head)], xv.at[pl.ds(0, head)]),
        ("x1", x_hbm.at[pl.ds(head, head)], xv.at[pl.ds(head, head)]),
        ("t1", t_hbm.at[pl.ds(ly, lz + lx)], tv.at[pl.ds(ly, lz + lx)]),
        ("b", b_hbm, bv),
        ("d", d_hbm, dv),
    )):
        loads[name] = pltpu.make_async_copy(src, dst, load_sem.at[i])
    for name in ("t", "u", "x0", "x1"):
        loads[name].start()

    barrier = pltpu.get_barrier_semaphore()

    def greet(sem, peer):
        pl.semaphore_signal(sem, inc=1, device_id=peer, device_id_type=MESH)

    for j in far_first(ny):
        greet(barrier, y_peer(j))
    for place in reversed(range(nz)):
        @pl.when(z < place)
        def _():
            greet(barrier, {"sub": place * ny + y})
    for j in far_first(nx):
        greet(barrier, x_peer(j))

    pair = lax.div(y, 2)
    outward = 2 * lax.rem(y, 2) - 1

    def spread(src, dst, group):
        for k in (3, 2, 1):
            target = lax.rem(y + k * outward + ny, ny)
            other = lax.div(target, 2)
            slot = lax.rem(pair + other, 2) + 2 * lax.rem(lax.div(pair, 2) + lax.div(other, 2), 2)
            send(src.at[1], dst.at[slot], group, {"sub": z * ny + target})
        send(src.at[2], dst.at[4], group, y_peer(6))

    def climb(base, levels):
        product = tv[base].astype(F32)
        chain = [product]
        for level in range(1, levels):
            product = times_exact(product, tv[base + level])
            chain.append(product)
        return chain

    def down(products, base, levels):
        parts = [bv[base].T]
        for i in range(1, levels):
            parts.append(up_weight(times_exact(products[i - 1], bv[base + i]).T))
        return jnp.concatenate(parts, axis=0)

    def near_part(part, parts):
        size = vecs // parts
        at = pl.ds(part * size, size)
        near[:, at] = dot(dv[...], xv[:, at])

    loads["t"].wait()
    ty = climb(0, ly)
    wy[...] = up_weight(ty[ly - 1])
    loads["u"].wait()
    ut[...] = uv[...].T
    loads["x0"].wait()
    hat_t = dot(ut[:, :head], xv[:head, :])
    loads["x1"].wait()
    for name in ("t1", "b", "d"):
        loads[name].start()
    hat = (hat_t + dot(ut[:, head:], xv[head:, :])).T
    hat_w = wide(hat)
    cy_send[...] = dot(hat_w, wy[...]).astype(BF)
    pl.semaphore_wait(barrier, ny - 1 + nx - 1 + z)
    for c in range(CHUNKS):
        for j in far_first(ny):
            send(cy_send.at[part(flip(y, j), c)], cy_recv.at[c, j], 5 + c, y_peer(j))
    for place in range(nz):
        @pl.when(z > place)
        def _():
            greet(z_sem, {"sub": place * ny + y})

    cl_send[...] = dot(hat_w[:, :2 * rank], jnp.concatenate([tv[0], tv[0]], axis=0)).astype(BF)
    h_send[...] = hat.astype(BF)
    loads["t1"].wait()
    tz = climb(ly, lz + lx - 1)
    wx[...] = jnp.concatenate([up_weight(product) for product in tz[lz - 1:]], axis=1)
    if lz > 1:
        wzl[...] = jnp.concatenate([up_exact(tv[ly])] + [up_weight(tz[i]) for i in range(1, lz - 1)], axis=1)
    lift_out[...] = jnp.concatenate(split(dot(uv[...], tv[0])), axis=1)
    loads["d"].wait()
    near_part(0, 2)
    loads["b"].wait()
    vx[...] = down(climb(ly + lz, lx), ly + lz, lx)

    mids = []
    for c in range(CHUNKS):
        wait_bytes(cy_recv.at[c, pl.ds(1, ny - 1)], recv_sem.at[5 + c])
        mid = cy_send[part(y, c), :].astype(F32)
        for j in range(1, ny):
            mid = mid + cy_recv[c, j].astype(F32)
        mids.append(wide(mid))
        share = dot(mids[c], wx[...])
        for i in range(lx):
            x_send[c, i] = share[:, i * rank:(i + 1) * rank].astype(BF)
        for place in early(nx // 2, 2):
            @pl.when(grp != place)
            def _():
                apart = flip(grp, place)
                level = sum(jnp.where(apart >= 1 << i, 1, 0) for i in range(1, lx))
                send(x_send.at[c, level], x_recv.at[c, apart], 7 + c, {"grp": place})

    mid_w = jnp.concatenate(mids, axis=0)
    zs_send[0] = mid_w[:, :rank]
    if lz > 1:
        zl = dot(mid_w, wzl[...])
        for i in range(lz - 1):
            zs_send[i + 1] = zl[:, i * rank:(i + 1) * rank].astype(BF)

    @pl.when(z < nz - 1)
    def _():
        pl.semaphore_wait(z_sem, nz - 1 - z)

    for j in far_first(nz):
        send(zs_send.at[level_of(j)], zs_recv.at[j], 4, z_peer(j))
    for j in far_first(ny):
        send(cl_send.at[rows(flip(y, j), yblk)], cl_recv.at[j], 0, y_peer(j))

    tops = []
    for c in range(CHUNKS):
        wait_bytes(x_recv.at[c, pl.ds(1, nx - 1)], recv_sem.at[7 + c])
        parts = [x_recv[c, 1]]
        for level in range(1, lx):
            parts.append(wide(functools.reduce(jnp.add, [x_recv[c, j].astype(F32) for j in range(1 << level, 2 << level)])))
        top = dot(jnp.concatenate(parts, axis=1), vx[...])
        tops.append(top)
        cz_send[c] = top.astype(BF)
        for place in range(nz):
            @pl.when(z != place)
            def _():
                send(cz_send.at[c], cz_recv.at[c, flip(z, place)], 9 + c, {"sub": place * ny + y})

    spread(t_hbm, rt, 1)
    spread(b_hbm, bt, 3)
    send(h_send, h_recv, 2, y_peer(1))
    vz[...] = down(tz, ly, lz)

    rt[0] = tv[1]
    rt[5] = tv[2]
    bt[0] = bv[1]
    bt[5] = bv[2]
    wait_bytes(rt.at[pl.ds(1, 4)], recv_sem.at[1])
    lifts = []
    for quad in range(2):
        both = jnp.concatenate([rt[2 * quad], rt[2 * quad + 1]], axis=0)
        lifts.append(dot(both, rt[5 - quad]))
    lifts = jnp.concatenate(lifts, axis=0)
    whole = dot(wide(lifts), wx[:, :rank])
    for r in range(4):
        at = slice(r * rank, (r + 1) * rank)
        vw[:, at] = up_weight(lifts[at].T)
        vg[:, at] = up_weight(whole[at].T)
    wait_bytes(zs_recv.at[pl.ds(1, nz - 1)], recv_sem.at[4])
    parts = [zs_recv[1]]
    for level in range(1, lz):
        parts.append(wide(functools.reduce(jnp.add, [zs_recv[j].astype(F32) for j in range(1 << level, 2 << level)])))
    mid_far = dot(jnp.concatenate(parts, axis=1), vz[...])

    wait_bytes(cl_recv.at[pl.ds(1, ny - 1)], recv_sem.at[0])
    given = [cl_send[rows(y, yblk), :]] + [cl_recv[j] for j in range(1, ny)]
    sums = [given[2 * r].astype(F32) + given[2 * r + 1].astype(F32) for r in range(4)]
    quads = []
    for quad in range(2):
        left = jnp.concatenate([*split(sums[2 * quad]), *split(sums[2 * quad + 1])], axis=1)
        right = [rt[2 * quad]] * 2 + [rt[2 * quad + 1]] * 2
        quads.append(dot(left, jnp.concatenate(right, axis=0)))
    wait_bytes(bt.at[pl.ds(1, 4)], recv_sem.at[3])
    local = []
    for quad in range(2):
        both = jnp.concatenate([rt[2 * quad], rt[2 * quad + 1]], axis=0)
        high, low = split(dot(both, bt[5 - quad]))
        seen = dot_nt(wide(quads[1 - quad]), jnp.concatenate([high, high, low], axis=1))
        for side in range(2):
            r = 2 * quad + side
            sibling = jnp.concatenate(split(sums[r ^ 1]), axis=1)
            local.append(seen[:, side * rank:(side + 1) * rank] + dot_nt(sibling, jnp.concatenate([bt[r]] * 2, axis=1)))
    local = jnp.concatenate(local, axis=1) + dot(wide(mid_far), vw[...])

    for c in range(CHUNKS):
        wait_bytes(cz_recv.at[c, pl.ds(1, nz - 1)], recv_sem.at[9 + c])
        top = tops[c]
        for j in range(1, nz):
            top = top + cz_recv[c, j].astype(F32)
        at = pl.ds(c * half, half)
        pair_far = (local[c * half:(c + 1) * half] + dot(wide(top), vg[...])).astype(BF)
        for r in range(4):
            far_y_send[r, at, :] = pair_far[:, r * rank:(r + 1) * rank]
        for place in early(ny, 1):
            @pl.when(y != place)
            def _():
                send(far_y_send.at[lax.div(flip(y, place), 2), at], far_y.at[part(y, c)], 11 + c, {"sub": z * ny + place})
        far_y[part(y, c), :] = far_y_send[0, at, :]

    wait_bytes(h_recv, recv_sem.at[2])
    far = dot_nt(h_recv[...], bv[0]).astype(BF)
    near_part(1, 2)
    near[...] += dot_nt(uv[...], far)
    for c in range(CHUNKS):
        wait_bytes(far_y.at[pl.ds(0, (ny - 1) * half)], recv_sem.at[11 + c])
    far_out[...] = far_y[...]

    wait_bytes(cl_recv.at[pl.ds(1, ny - 1)], send_sem.at[0])
    wait_bytes(rt.at[pl.ds(1, 4)], send_sem.at[1])
    wait_bytes(h_send, send_sem.at[2])
    wait_bytes(bt.at[pl.ds(1, 4)], send_sem.at[3])
    wait_bytes(zs_recv.at[pl.ds(1, nz - 1)], send_sem.at[4])
    for c in range(CHUNKS):
        wait_bytes(cy_recv.at[c, pl.ds(1, ny - 1)], send_sem.at[5 + c])
        wait_bytes(x_recv.at[c, pl.ds(1, nx - 1)], send_sem.at[7 + c])
        wait_bytes(cz_recv.at[c, pl.ds(1, nz - 1)], send_sem.at[9 + c])
        wait_bytes(far_y.at[pl.ds(0, (ny - 1) * half)], send_sem.at[11 + c])


def last_kernel(near, lift, far, o_hbm, far_t, ov, store_sem):
    leaf = near.shape[0]
    chunks = store_sem.shape[0]
    tile = leaf // chunks
    far_t[...] = jnp.concatenate([far[...].T] * 2, axis=0)
    stores = []
    for step in range(chunks):
        at = pl.ds(step * tile, tile)
        ov[at, :] = (near[at, :] + dot(lift[at, :], far_t[...])).astype(BF)
        store = pltpu.make_async_copy(ov.at[at], o_hbm.at[at], store_sem.at[step])
        store.start()
        stores.append(store)
    for store in stores:
        store.wait()


def solution(mesh):
    ly = 3
    lz = mesh.shape["sub"].bit_length() - 1 - ly
    lx = mesh.shape["grp"].bit_length() - 1
    ny, nz, nx = 1 << ly, 1 << lz, 1 << lx

    def body(vectors, blocks, basis, transfer, coupling):
        leaf, vecs = vectors.shape[2:]
        rank = basis.shape[3]
        levels = transfer.shape[2]
        yblk = vecs // ny
        scratch = [
            pltpu.VMEM((leaf, vecs), BF),
            pltpu.VMEM((leaf, leaf), BF),
            pltpu.VMEM((leaf, rank), BF),
            pltpu.VMEM((rank, leaf), BF),
            pltpu.VMEM((levels, rank, rank), BF),
            pltpu.VMEM((levels, rank, rank), BF),
            pltpu.VMEM((6, rank, rank), BF),
            pltpu.VMEM((6, rank, rank), BF),
            pltpu.VMEM((3 * rank, rank), BF),
            pltpu.VMEM((3 * rank, lx * rank), BF),
            pltpu.VMEM((3 * rank, max(1, lz - 1) * rank), BF),
            pltpu.VMEM(((3 * lx - 2) * rank, rank), BF),
            pltpu.VMEM(((3 * lz - 2) * rank, rank), BF),
            pltpu.VMEM((3 * rank, 4 * rank), BF),
            pltpu.VMEM((3 * rank, 4 * rank), BF),
            pltpu.VMEM((vecs, rank), BF),
            pltpu.VMEM((vecs, rank), BF),
            pltpu.VMEM((vecs, rank), BF),
            pltpu.VMEM((CHUNKS, ny, yblk // CHUNKS, rank), BF),
            pltpu.VMEM((vecs, rank), BF),
            pltpu.VMEM((ny, yblk, rank), BF),
            pltpu.VMEM((CHUNKS, yblk // CHUNKS, rank), BF),
            pltpu.VMEM((CHUNKS, nz, yblk // CHUNKS, rank), BF),
            pltpu.VMEM((lz, yblk, rank), BF),
            pltpu.VMEM((nz, yblk, rank), BF),
            pltpu.VMEM((CHUNKS, lx, yblk // CHUNKS, rank), BF),
            pltpu.VMEM((CHUNKS, nx, yblk // CHUNKS, rank), BF),
            pltpu.VMEM((4, yblk, rank), BF),
            pltpu.VMEM((vecs, rank), BF),
            pltpu.SemaphoreType.DMA((7,)),
            pltpu.SemaphoreType.REGULAR,
            pltpu.SemaphoreType.DMA((13,)),
            pltpu.SemaphoreType.DMA((13,)),
        ]
        vmem = pl.BlockSpec(memory_space=pltpu.VMEM)
        near, lift, far = pl.pallas_call(
            functools.partial(kernel, (lz, lx)),
            out_shape=[
                jax.ShapeDtypeStruct((leaf, vecs), F32),
                jax.ShapeDtypeStruct((leaf, 2 * rank), BF),
                jax.ShapeDtypeStruct((vecs, rank), BF),
            ],
            in_specs=[pl.BlockSpec(memory_space=pltpu.HBM)] * 5,
            out_specs=[vmem] * 3,
            scratch_shapes=scratch,
            compiler_params=pltpu.CompilerParams(
                collective_id=0, has_side_effects=True, vmem_limit_bytes=32 * 1024 * 1024,
            ),
        )(*(pltpu.with_memory_space_constraint(whole[0, 0], pltpu.HBM) for whole in (vectors, blocks, basis, transfer, coupling)))
        out = pl.pallas_call(
            last_kernel,
            out_shape=jax.ShapeDtypeStruct((leaf, vecs), BF),
            in_specs=[vmem] * 3,
            out_specs=pl.BlockSpec(memory_space=pltpu.HBM),
            scratch_shapes=[
                pltpu.VMEM((2 * rank, vecs), BF),
                pltpu.VMEM((leaf, vecs), BF),
                pltpu.SemaphoreType.DMA((4,)),
            ],
            compiler_params=pltpu.CompilerParams(vmem_limit_bytes=24 * 1024 * 1024),
        )(near, lift, far)
        return out[None, None]

    return jax.shard_map(
        body,
        mesh=mesh,
        in_specs=(
            P("grp", "sub", None, None),
            P("grp", "sub", None, None),
            P("grp", "sub", None, None),
            P("grp", "sub", None, None, None),
            P("grp", "sub", None, None, None),
        ),
        out_specs=P("grp", "sub", None, None),
        check_vma=False,
    )
```

```python
import functools

import jax
import jax.numpy as jnp
from jax import lax
from jax.experimental import pallas as pl
from jax.experimental.pallas import tpu as pltpu
from jax.sharding import PartitionSpec as P

MESH = pl.DeviceIdType.MESH
BF = jnp.bfloat16
F32 = jnp.float32
CHUNKS = 1


def dot(left, right):
    return jnp.dot(left, right, preferred_element_type=F32)


def dot_nt(left, right):
    return lax.dot_general(left, right, (((1,), (1,)), ((), ())), preferred_element_type=F32)


def dot_tn(left, right):
    return lax.dot_general(left, right, (((0,), (0,)), ((), ())), preferred_element_type=F32)


def split(value):
    high = value.astype(BF)
    return high, (value - high.astype(F32)).astype(BF)


def flip(index, offset):
    out = index
    for bit in range(offset.bit_length()):
        if offset >> bit & 1:
            out = out + (1 << bit) - (2 << bit) * lax.rem(lax.div(index, 1 << bit), 2)
    return out


def level_of(offset):
    return offset.bit_length() - 1


def far_first(count):
    return [j for j in (4, 5, 3, 7, 6, 2, 1) if j < count]


def later(index, k):
    return jnp.where(index > k, 0, 1)


def wait_bytes(ref, sem):
    pltpu.make_async_copy(ref, ref, sem).wait()


def up_weight(product):
    high, low = split(product)
    return jnp.concatenate([high, high, low], axis=0)


def up_exact(matrix):
    return jnp.concatenate([matrix, matrix, jnp.zeros_like(matrix)], axis=0)


def wide(value):
    high, low = split(value)
    return jnp.concatenate([high, low, high], axis=1)


def times_exact(product, matrix):
    high, low = split(product)
    return dot(high, matrix) + dot(low, matrix)


def kernel(dims, x_hbm, d_hbm, u_hbm, t_hbm, b_hbm, near, lift_out, far_out,
           xv, dv, uv, ut, tv, bv,
           rt, bt, wy, wx, wzl, vx, vz, vw, vg,
           h_send, h_recv, cy_send, cy_recv, cl_send, cl_recv,
           cz_send, cz_recv, zs_send, zs_recv, x_send, x_recv,
           far_y_send, far_y,
           load_sem, z_sem, send_sem, recv_sem):
    lz, lx = dims
    ly = 3
    ny, nz, nx = 1 << ly, 1 << lz, 1 << lx
    leaf, vecs = x_hbm.shape
    rank = u_hbm.shape[1]
    yblk = vecs // ny
    half = yblk // CHUNKS
    sub, grp = lax.axis_index("sub"), lax.axis_index("grp")
    y, z = lax.rem(sub, ny), lax.div(sub, ny)

    def y_peer(j):
        return {"sub": z * ny + flip(y, j)}

    def z_peer(j):
        return {"sub": flip(z, j) * ny + y}

    def x_peer(j):
        return {"grp": flip(grp, j)}

    def rows(index, size):
        return pl.ds(pl.multiple_of(index * size, size), size)

    def part(index, c):
        return pl.ds(pl.multiple_of(index * yblk + c * half, half), half)

    def send(src, dst, group, peer):
        pltpu.make_async_remote_copy(
            src_ref=src, dst_ref=dst, send_sem=send_sem.at[group], recv_sem=recv_sem.at[group],
            device_id=peer, device_id_type=MESH,
        ).start()

    head = leaf // 2
    loads = {}
    for i, (name, src, dst) in enumerate((
        ("t", t_hbm.at[pl.ds(0, ly)], tv.at[pl.ds(0, ly)]),
        ("u", u_hbm, uv),
        ("x0", x_hbm.at[pl.ds(0, head)], xv.at[pl.ds(0, head)]),
        ("x1", x_hbm.at[pl.ds(head, head)], xv.at[pl.ds(head, head)]),
        ("t1", t_hbm.at[pl.ds(ly, lz + lx)], tv.at[pl.ds(ly, lz + lx)]),
        ("b", b_hbm, bv),
        ("d", d_hbm, dv),
    )):
        loads[name] = pltpu.make_async_copy(src, dst, load_sem.at[i])
    for name in ("t", "u", "x0", "x1"):
        loads[name].start()

    order = sorted(range(ny), key=lambda place: min(place, ny - place))
    rank_y = sum(jnp.where(y == place, k, 0) for k, place in enumerate(order))
    barrier = pltpu.get_barrier_semaphore()

    def greet(sem, peer):
        pl.semaphore_signal(sem, inc=1, device_id=peer, device_id_type=MESH)

    for j in far_first(ny):
        greet(barrier, y_peer(j))
    for place in reversed(range(nz)):
        @pl.when(z < place)
        def _():
            greet(barrier, {"sub": place * ny + y})
    for j in far_first(nx):
        greet(barrier, x_peer(j))

    pair = lax.div(y, 2)
    outward = 2 * lax.rem(y, 2) - 1

    def spread(src, dst, group):
        for k in (3, 2, 1):
            target = lax.rem(y + k * outward + ny, ny)
            other = lax.div(target, 2)
            slot = lax.rem(pair + other, 2) + 2 * lax.rem(lax.div(pair, 2) + lax.div(other, 2), 2)
            send(src.at[1], dst.at[slot], group, {"sub": z * ny + target})
        send(src.at[2], dst.at[4], group, y_peer(6))

    def climb(base, levels):
        product = tv[base].astype(F32)
        chain = [product]
        for level in range(1, levels):
            product = times_exact(product, tv[base + level])
            chain.append(product)
        return chain

    def down(products, base, levels):
        parts = [bv[base].T]
        for i in range(1, levels):
            parts.append(up_weight(times_exact(products[i - 1], bv[base + i]).T))
        return jnp.concatenate(parts, axis=0)

    def near_part(part, parts):
        size = vecs // parts
        at = pl.ds(part * size, size)
        near[:, at] = dot(dv[...], xv[:, at])

    loads["t"].wait()
    ty = climb(0, ly)
    wy[...] = up_weight(ty[ly - 1])
    loads["u"].wait()
    ut[...] = uv[...].T
    loads["x0"].wait()
    hat_t = dot(ut[:, :head], xv[:head, :])
    loads["x1"].wait()
    for name in ("t1", "b", "d"):
        loads[name].start()
    hat = (hat_t + dot(ut[:, head:], xv[head:, :])).T
    hat_w = wide(hat)
    cy_send[...] = dot(hat_w, wy[...]).astype(BF)
    pl.semaphore_wait(barrier, ny - 1 + nx - 1 + z)
    for c in range(CHUNKS):
        for j in far_first(ny):
            send(cy_send.at[part(flip(y, j), c)], cy_recv.at[c, j], 5 + c, y_peer(j))
    for place in range(nz):
        @pl.when(z > place)
        def _():
            greet(z_sem, {"sub": place * ny + y})

    loads["t1"].wait()
    tz = climb(ly, lz + lx - 1)
    wx[...] = jnp.concatenate([up_weight(product) for product in tz[lz - 1:]], axis=1)
    loads["b"].wait()
    vx[...] = down(climb(ly + lz, lx), ly + lz, lx)

    mids = []
    for c in range(CHUNKS):
        wait_bytes(cy_recv.at[c, pl.ds(1, ny - 1)], recv_sem.at[5 + c])
        mid = cy_send[part(y, c), :].astype(F32)
        for j in range(1, ny):
            mid = mid + cy_recv[c, j].astype(F32)
        mids.append(wide(mid))
        share = dot(mids[c], wx[...])
        for i in range(lx):
            x_send[c, i] = share[:, i * rank:(i + 1) * rank].astype(BF)
        for j in (4, 5, 6, 7, 2, 3, 1):
            if j < nx:
                send(x_send.at[c, level_of(j)], x_recv.at[c, j], 7 + c, x_peer(j))

    mid_w = jnp.concatenate(mids, axis=0)
    zs_send[0] = mid_w[:, :rank]
    if lz > 1:
        wzl[...] = jnp.concatenate([up_exact(tv[ly])] + [up_weight(tz[i]) for i in range(1, lz - 1)], axis=1)
        zl = dot(mid_w, wzl[...])
        for i in range(lz - 1):
            zs_send[i + 1] = zl[:, i * rank:(i + 1) * rank].astype(BF)

    @pl.when(z < nz - 1)
    def _():
        pl.semaphore_wait(z_sem, nz - 1 - z)

    for j in far_first(nz):
        send(zs_send.at[level_of(j)], zs_recv.at[j], 4, z_peer(j))
    cl_send[...] = dot(hat_w[:, :2 * rank], jnp.concatenate([tv[0], tv[0]], axis=0)).astype(BF)
    h_send[...] = hat.astype(BF)
    for j in far_first(ny):
        send(cl_send.at[rows(flip(y, j), yblk)], cl_recv.at[j], 0, y_peer(j))

    for c in range(CHUNKS):
        wait_bytes(x_recv.at[c, pl.ds(1, nx - 1)], recv_sem.at[7 + c])
        parts = [x_recv[c, 1]]
        for level in range(1, lx):
            parts.append(wide(functools.reduce(jnp.add, [x_recv[c, j].astype(F32) for j in range(1 << level, 2 << level)])))
        top = dot(jnp.concatenate(parts, axis=1), vx[...])
        cz_send[c] = top.astype(BF)
        for k in range(nz - 1):
            send(cz_send.at[c], cz_recv.at[c, z], 9 + c, {"sub": (k + later(z, k)) * ny + y})
        cz_recv[c, z] = cz_send[c]

    spread(t_hbm, rt, 1)
    spread(b_hbm, bt, 3)
    send(h_send, h_recv, 2, y_peer(1))
    vz[...] = down(tz, ly, lz)

    lift_out[...] = jnp.concatenate(split(dot(uv[...], tv[0])), axis=1)
    loads["d"].wait()
    near_part(0, 2)
    rt[0] = tv[1]
    rt[5] = tv[2]
    bt[0] = bv[1]
    bt[5] = bv[2]
    wait_bytes(rt.at[pl.ds(1, 4)], recv_sem.at[1])
    lifts = []
    for quad in range(2):
        both = jnp.concatenate([rt[2 * quad], rt[2 * quad + 1]], axis=0)
        lifts.append(dot(both, rt[5 - quad]))
    lifts = jnp.concatenate(lifts, axis=0)
    whole = dot(wide(lifts), wx[:, :rank])
    for r in range(4):
        at = slice(r * rank, (r + 1) * rank)
        vw[:, at] = up_weight(lifts[at].T)
        vg[:, at] = up_weight(whole[at].T)
    wait_bytes(zs_recv.at[pl.ds(1, nz - 1)], recv_sem.at[4])
    parts = [zs_recv[1]]
    for level in range(1, lz):
        parts.append(wide(functools.reduce(jnp.add, [zs_recv[j].astype(F32) for j in range(1 << level, 2 << level)])))
    mid_far = dot(jnp.concatenate(parts, axis=1), vz[...])

    wait_bytes(cl_recv.at[pl.ds(1, ny - 1)], recv_sem.at[0])
    given = [cl_send[rows(y, yblk), :]] + [cl_recv[j] for j in range(1, ny)]
    sums = [given[2 * r].astype(F32) + given[2 * r + 1].astype(F32) for r in range(4)]
    quads = []
    for quad in range(2):
        left = jnp.concatenate([*split(sums[2 * quad]), *split(sums[2 * quad + 1])], axis=1)
        right = [rt[2 * quad]] * 2 + [rt[2 * quad + 1]] * 2
        quads.append(dot(left, jnp.concatenate(right, axis=0)))
    wait_bytes(bt.at[pl.ds(1, 4)], recv_sem.at[3])
    local = []
    for quad in range(2):
        both = jnp.concatenate([rt[2 * quad], rt[2 * quad + 1]], axis=0)
        high, low = split(dot(both, bt[5 - quad]))
        seen = dot_nt(wide(quads[1 - quad]), jnp.concatenate([high, high, low], axis=1))
        for side in range(2):
            r = 2 * quad + side
            sibling = jnp.concatenate(split(sums[r ^ 1]), axis=1)
            local.append(seen[:, side * rank:(side + 1) * rank] + dot_nt(sibling, jnp.concatenate([bt[r]] * 2, axis=1)))
    local = jnp.concatenate(local, axis=1) + dot(wide(mid_far), vw[...])

    for c in range(CHUNKS):
        wait_bytes(cz_recv.at[c, pl.ds(0, nz - 1)], recv_sem.at[9 + c])
        top = functools.reduce(jnp.add, [cz_recv[c, place].astype(F32) for place in range(nz)])
        at = pl.ds(c * half, half)
        pair_far = (local[c * half:(c + 1) * half] + dot(wide(top), vg[...])).astype(BF)
        for r in range(4):
            far_y_send[flip(pair, r), at, :] = pair_far[:, r * rank:(r + 1) * rank]
        for k in range(ny - 1):
            place = jnp.where(rank_y > k, order[k], order[k + 1])
            mate = jnp.where(rank_y > k, order[k] // 2, order[k + 1] // 2)
            send(far_y_send.at[mate, at], far_y.at[part(y, c)], 11 + c, {"sub": z * ny + place})
        far_y[part(y, c), :] = pair_far[:, :rank]

    wait_bytes(h_recv, recv_sem.at[2])
    far = dot_nt(h_recv[...], bv[0]).astype(BF)
    near_part(1, 2)
    near[...] += dot_nt(uv[...], far)
    for c in range(CHUNKS):
        wait_bytes(far_y.at[pl.ds(0, (ny - 1) * half)], recv_sem.at[11 + c])
    far_out[...] = far_y[...]

    wait_bytes(cl_recv.at[pl.ds(1, ny - 1)], send_sem.at[0])
    wait_bytes(rt.at[pl.ds(1, 4)], send_sem.at[1])
    wait_bytes(h_send, send_sem.at[2])
    wait_bytes(bt.at[pl.ds(1, 4)], send_sem.at[3])
    wait_bytes(zs_recv.at[pl.ds(1, nz - 1)], send_sem.at[4])
    for c in range(CHUNKS):
        wait_bytes(cy_recv.at[c, pl.ds(1, ny - 1)], send_sem.at[5 + c])
        wait_bytes(x_recv.at[c, pl.ds(1, nx - 1)], send_sem.at[7 + c])
        wait_bytes(cz_recv.at[c, pl.ds(1, nz - 1)], send_sem.at[9 + c])
        wait_bytes(far_y.at[pl.ds(0, (ny - 1) * half)], send_sem.at[11 + c])


def last_kernel(near, lift, far, o_hbm, far_t, ov, store_sem):
    leaf = near.shape[0]
    chunks = store_sem.shape[0]
    tile = leaf // chunks
    far_t[...] = jnp.concatenate([far[...].T] * 2, axis=0)
    stores = []
    for step in range(chunks):
        at = pl.ds(step * tile, tile)
        ov[at, :] = (near[at, :] + dot(lift[at, :], far_t[...])).astype(BF)
        store = pltpu.make_async_copy(ov.at[at], o_hbm.at[at], store_sem.at[step])
        store.start()
        stores.append(store)
    for store in stores:
        store.wait()


def solution(mesh):
    ly = 3
    lz = mesh.shape["sub"].bit_length() - 1 - ly
    lx = mesh.shape["grp"].bit_length() - 1
    ny, nz, nx = 1 << ly, 1 << lz, 1 << lx

    def body(vectors, blocks, basis, transfer, coupling):
        leaf, vecs = vectors.shape[2:]
        rank = basis.shape[3]
        levels = transfer.shape[2]
        yblk = vecs // ny
        scratch = [
            pltpu.VMEM((leaf, vecs), BF),
            pltpu.VMEM((leaf, leaf), BF),
            pltpu.VMEM((leaf, rank), BF),
            pltpu.VMEM((rank, leaf), BF),
            pltpu.VMEM((levels, rank, rank), BF),
            pltpu.VMEM((levels, rank, rank), BF),
            pltpu.VMEM((6, rank, rank), BF),
            pltpu.VMEM((6, rank, rank), BF),
            pltpu.VMEM((3 * rank, rank), BF),
            pltpu.VMEM((3 * rank, lx * rank), BF),
            pltpu.VMEM((3 * rank, max(1, lz - 1) * rank), BF),
            pltpu.VMEM(((3 * lx - 2) * rank, rank), BF),
            pltpu.VMEM(((3 * lz - 2) * rank, rank), BF),
            pltpu.VMEM((3 * rank, 4 * rank), BF),
            pltpu.VMEM((3 * rank, 4 * rank), BF),
            pltpu.VMEM((vecs, rank), BF),
            pltpu.VMEM((vecs, rank), BF),
            pltpu.VMEM((vecs, rank), BF),
            pltpu.VMEM((CHUNKS, ny, yblk // CHUNKS, rank), BF),
            pltpu.VMEM((vecs, rank), BF),
            pltpu.VMEM((ny, yblk, rank), BF),
            pltpu.VMEM((CHUNKS, yblk // CHUNKS, rank), BF),
            pltpu.VMEM((CHUNKS, nz, yblk // CHUNKS, rank), BF),
            pltpu.VMEM((lz, yblk, rank), BF),
            pltpu.VMEM((nz, yblk, rank), BF),
            pltpu.VMEM((CHUNKS, lx, yblk // CHUNKS, rank), BF),
            pltpu.VMEM((CHUNKS, nx, yblk // CHUNKS, rank), BF),
            pltpu.VMEM((4, yblk, rank), BF),
            pltpu.VMEM((vecs, rank), BF),
            pltpu.SemaphoreType.DMA((7,)),
            pltpu.SemaphoreType.REGULAR,
            pltpu.SemaphoreType.DMA((13,)),
            pltpu.SemaphoreType.DMA((13,)),
        ]
        vmem = pl.BlockSpec(memory_space=pltpu.VMEM)
        near, lift, far = pl.pallas_call(
            functools.partial(kernel, (lz, lx)),
            out_shape=[
                jax.ShapeDtypeStruct((leaf, vecs), F32),
                jax.ShapeDtypeStruct((leaf, 2 * rank), BF),
                jax.ShapeDtypeStruct((vecs, rank), BF),
            ],
            in_specs=[pl.BlockSpec(memory_space=pltpu.HBM)] * 5,
            out_specs=[vmem] * 3,
            scratch_shapes=scratch,
            compiler_params=pltpu.CompilerParams(
                collective_id=0, has_side_effects=True, vmem_limit_bytes=32 * 1024 * 1024,
            ),
        )(*(pltpu.with_memory_space_constraint(whole[0, 0], pltpu.HBM) for whole in (vectors, blocks, basis, transfer, coupling)))
        out = pl.pallas_call(
            last_kernel,
            out_shape=jax.ShapeDtypeStruct((leaf, vecs), BF),
            in_specs=[vmem] * 3,
            out_specs=pl.BlockSpec(memory_space=pltpu.HBM),
            scratch_shapes=[
                pltpu.VMEM((2 * rank, vecs), BF),
                pltpu.VMEM((leaf, vecs), BF),
                pltpu.SemaphoreType.DMA((4,)),
            ],
            compiler_params=pltpu.CompilerParams(vmem_limit_bytes=24 * 1024 * 1024),
        )(near, lift, far)
        return out[None, None]

    return jax.shard_map(
        body,
        mesh=mesh,
        in_specs=(
            P("grp", "sub", None, None),
            P("grp", "sub", None, None),
            P("grp", "sub", None, None),
            P("grp", "sub", None, None, None),
            P("grp", "sub", None, None, None),
        ),
        out_specs=P("grp", "sub", None, None),
        check_vma=False,
    )
```

```python
import functools

import jax
import jax.numpy as jnp
from jax import lax
from jax.experimental import pallas as pl
from jax.experimental.pallas import tpu as pltpu
from jax.sharding import PartitionSpec as P

MESH = pl.DeviceIdType.MESH
BF = jnp.bfloat16
F32 = jnp.float32
CHUNKS = 1


def dot(left, right):
    return jnp.dot(left, right, preferred_element_type=F32)


def dot_nt(left, right):
    return lax.dot_general(left, right, (((1,), (1,)), ((), ())), preferred_element_type=F32)


def dot_tn(left, right):
    return lax.dot_general(left, right, (((0,), (0,)), ((), ())), preferred_element_type=F32)


def split(value):
    high = value.astype(BF)
    return high, (value - high.astype(F32)).astype(BF)


def flip(index, offset):
    out = index
    for bit in range(offset.bit_length()):
        if offset >> bit & 1:
            out = out + (1 << bit) - (2 << bit) * lax.rem(lax.div(index, 1 << bit), 2)
    return out


def xor(left, right, bits):
    out = 0
    for bit in range(bits):
        out = out + (1 << bit) * lax.rem(lax.div(left, 1 << bit) + lax.div(right, 1 << bit), 2)
    return out


def level_of(offset):
    return offset.bit_length() - 1


def far_first(count):
    return [j for j in (4, 5, 3, 7, 6, 2, 1) if j < count]


def later(index, k):
    return jnp.where(index > k, 0, 1)


def wait_bytes(ref, sem):
    pltpu.make_async_copy(ref, ref, sem).wait()


def up_weight(product):
    high, low = split(product)
    return jnp.concatenate([high, high, low], axis=0)


def up_exact(matrix):
    return jnp.concatenate([matrix, matrix, jnp.zeros_like(matrix)], axis=0)


def wide(value):
    high, low = split(value)
    return jnp.concatenate([high, low, high], axis=1)


def times_exact(product, matrix):
    high, low = split(product)
    return dot(high, matrix) + dot(low, matrix)


def kernel(dims, x_hbm, d_hbm, u_hbm, t_hbm, b_hbm, near, lift_out, far_out,
           xv, dv, uv, ut, tv, bv,
           rt, bt, wy, wx, wzl, vx, vz, vw, vg,
           h_send, h_recv, cy_send, cy_recv, cl_send, cl_recv,
           cz_send, cz_recv, zs_send, zs_recv, x_send, x_recv,
           far_y_send, far_y,
           load_sem, z_sem, send_sem, recv_sem):
    lz, lx = dims
    ly = 3
    ny, nz, nx = 1 << ly, 1 << lz, 1 << lx
    leaf, vecs = x_hbm.shape
    rank = u_hbm.shape[1]
    yblk = vecs // ny
    half = yblk // CHUNKS
    sub, grp = lax.axis_index("sub"), lax.axis_index("grp")
    y, z = lax.rem(sub, ny), lax.div(sub, ny)

    def y_peer(j):
        return {"sub": z * ny + flip(y, j)}

    def z_peer(j):
        return {"sub": flip(z, j) * ny + y}

    def x_peer(j):
        return {"grp": flip(grp, j)}

    def rows(index, size):
        return pl.ds(pl.multiple_of(index * size, size), size)

    def part(index, c):
        return pl.ds(pl.multiple_of(index * yblk + c * half, half), half)

    def send(src, dst, group, peer):
        pltpu.make_async_remote_copy(
            src_ref=src, dst_ref=dst, send_sem=send_sem.at[group], recv_sem=recv_sem.at[group],
            device_id=peer, device_id_type=MESH,
        ).start()

    head = leaf // 2
    loads = {}
    for i, (name, src, dst) in enumerate((
        ("t", t_hbm.at[pl.ds(0, ly)], tv.at[pl.ds(0, ly)]),
        ("u", u_hbm, uv),
        ("x0", x_hbm.at[pl.ds(0, head)], xv.at[pl.ds(0, head)]),
        ("x1", x_hbm.at[pl.ds(head, head)], xv.at[pl.ds(head, head)]),
        ("t1", t_hbm.at[pl.ds(ly, lz + lx)], tv.at[pl.ds(ly, lz + lx)]),
        ("b", b_hbm, bv),
        ("d", d_hbm, dv),
    )):
        loads[name] = pltpu.make_async_copy(src, dst, load_sem.at[i])
    for name in ("t", "u", "x0", "x1"):
        loads[name].start()

    order = sorted(range(ny), key=lambda place: min(place, ny - place))
    rank_y = sum(jnp.where(y == place, k, 0) for k, place in enumerate(order))
    chips = sorted(range(1, nx // 2), key=lambda place: min(place, nx // 2 - place))
    places = [1, 0] + [2 * chip + core for chip in chips for core in range(2)]
    rank_x = sum(jnp.where(grp == place, k, 0) for k, place in enumerate(places))
    barrier = pltpu.get_barrier_semaphore()

    def greet(sem, peer):
        pl.semaphore_signal(sem, inc=1, device_id=peer, device_id_type=MESH)

    for j in far_first(ny):
        greet(barrier, y_peer(j))
    for place in reversed(range(nz)):
        @pl.when(z < place)
        def _():
            greet(barrier, {"sub": place * ny + y})
    for j in far_first(nx):
        greet(barrier, x_peer(j))

    pair = lax.div(y, 2)
    outward = 2 * lax.rem(y, 2) - 1

    def spread(src, dst, group):
        for k in (3, 2, 1):
            target = lax.rem(y + k * outward + ny, ny)
            other = lax.div(target, 2)
            slot = lax.rem(pair + other, 2) + 2 * lax.rem(lax.div(pair, 2) + lax.div(other, 2), 2)
            send(src.at[1], dst.at[slot], group, {"sub": z * ny + target})
        send(src.at[2], dst.at[4], group, y_peer(6))

    def climb(base, levels):
        product = tv[base].astype(F32)
        chain = [product]
        for level in range(1, levels):
            product = times_exact(product, tv[base + level])
            chain.append(product)
        return chain

    def down(products, base, levels):
        parts = [bv[base].T]
        for i in range(1, levels):
            parts.append(up_weight(times_exact(products[i - 1], bv[base + i]).T))
        return jnp.concatenate(parts, axis=0)

    def near_part(part, parts):
        size = vecs // parts
        at = pl.ds(part * size, size)
        near[:, at] = dot(dv[...], xv[:, at])

    loads["t"].wait()
    ty = climb(0, ly)
    wy[...] = up_weight(ty[ly - 1])
    loads["u"].wait()
    ut[...] = uv[...].T
    loads["x0"].wait()
    hat_t = dot(ut[:, :head], xv[:head, :])
    loads["x1"].wait()
    for name in ("t1", "b", "d"):
        loads[name].start()
    hat = (hat_t + dot(ut[:, head:], xv[head:, :])).T
    hat_w = wide(hat)
    cy_send[...] = dot(hat_w, wy[...]).astype(BF)
    pl.semaphore_wait(barrier, ny - 1 + nx - 1 + z)
    for c in range(CHUNKS):
        for j in far_first(ny):
            send(cy_send.at[part(flip(y, j), c)], cy_recv.at[c, j], 5 + c, y_peer(j))
    for place in range(nz):
        @pl.when(z > place)
        def _():
            greet(z_sem, {"sub": place * ny + y})

    loads["t1"].wait()
    tz = climb(ly, lz + lx - 1)
    wx[...] = jnp.concatenate([up_weight(product) for product in tz[lz - 1:]], axis=1)
    loads["b"].wait()
    vx[...] = down(climb(ly + lz, lx), ly + lz, lx)

    mids = []
    for c in range(CHUNKS):
        wait_bytes(cy_recv.at[c, pl.ds(1, ny - 1)], recv_sem.at[5 + c])
        mid = cy_send[part(y, c), :].astype(F32)
        for j in range(1, ny):
            mid = mid + cy_recv[c, j].astype(F32)
        mids.append(wide(mid))
        share = dot(mids[c], wx[...])
        for i in range(lx):
            x_send[c, i] = share[:, i * rank:(i + 1) * rank].astype(BF)
        for k in range(nx - 1):
            target = jnp.where(rank_x > k, places[k], places[k + 1])
            apart = xor(grp, target, lx)
            level = sum(jnp.where(apart >= 1 << i, 1, 0) for i in range(1, lx))
            send(x_send.at[c, level], x_recv.at[c, apart], 7 + c, {"grp": target})

    mid_w = jnp.concatenate(mids, axis=0)
    zs_send[0] = mid_w[:, :rank]
    if lz > 1:
        wzl[...] = jnp.concatenate([up_exact(tv[ly])] + [up_weight(tz[i]) for i in range(1, lz - 1)], axis=1)
        zl = dot(mid_w, wzl[...])
        for i in range(lz - 1):
            zs_send[i + 1] = zl[:, i * rank:(i + 1) * rank].astype(BF)

    @pl.when(z < nz - 1)
    def _():
        pl.semaphore_wait(z_sem, nz - 1 - z)

    for j in far_first(nz):
        send(zs_send.at[level_of(j)], zs_recv.at[j], 4, z_peer(j))
    cl_send[...] = dot(hat_w[:, :2 * rank], jnp.concatenate([tv[0], tv[0]], axis=0)).astype(BF)
    h_send[...] = hat.astype(BF)
    for j in far_first(ny):
        send(cl_send.at[rows(flip(y, j), yblk)], cl_recv.at[j], 0, y_peer(j))

    for c in range(CHUNKS):
        wait_bytes(x_recv.at[c, pl.ds(1, nx - 1)], recv_sem.at[7 + c])
        parts = [x_recv[c, 1]]
        for level in range(1, lx):
            parts.append(wide(functools.reduce(jnp.add, [x_recv[c, j].astype(F32) for j in range(1 << level, 2 << level)])))
        top = dot(jnp.concatenate(parts, axis=1), vx[...])
        cz_send[c] = top.astype(BF)
        for k in range(nz - 1):
            send(cz_send.at[c], cz_recv.at[c, z], 9 + c, {"sub": (k + later(z, k)) * ny + y})
        cz_recv[c, z] = cz_send[c]

    spread(t_hbm, rt, 1)
    spread(b_hbm, bt, 3)
    send(h_send, h_recv, 2, y_peer(1))
    vz[...] = down(tz, ly, lz)

    lift_out[...] = jnp.concatenate(split(dot(uv[...], tv[0])), axis=1)
    loads["d"].wait()
    near_part(0, 2)
    rt[0] = tv[1]
    rt[5] = tv[2]
    bt[0] = bv[1]
    bt[5] = bv[2]
    wait_bytes(rt.at[pl.ds(1, 4)], recv_sem.at[1])
    lifts = []
    for quad in range(2):
        both = jnp.concatenate([rt[2 * quad], rt[2 * quad + 1]], axis=0)
        lifts.append(dot(both, rt[5 - quad]))
    lifts = jnp.concatenate(lifts, axis=0)
    whole = dot(wide(lifts), wx[:, :rank])
    for r in range(4):
        at = slice(r * rank, (r + 1) * rank)
        vw[:, at] = up_weight(lifts[at].T)
        vg[:, at] = up_weight(whole[at].T)
    wait_bytes(zs_recv.at[pl.ds(1, nz - 1)], recv_sem.at[4])
    parts = [zs_recv[1]]
    for level in range(1, lz):
        parts.append(wide(functools.reduce(jnp.add, [zs_recv[j].astype(F32) for j in range(1 << level, 2 << level)])))
    mid_far = dot(jnp.concatenate(parts, axis=1), vz[...])

    wait_bytes(cl_recv.at[pl.ds(1, ny - 1)], recv_sem.at[0])
    given = [cl_send[rows(y, yblk), :]] + [cl_recv[j] for j in range(1, ny)]
    sums = [given[2 * r].astype(F32) + given[2 * r + 1].astype(F32) for r in range(4)]
    quads = []
    for quad in range(2):
        left = jnp.concatenate([*split(sums[2 * quad]), *split(sums[2 * quad + 1])], axis=1)
        right = [rt[2 * quad]] * 2 + [rt[2 * quad + 1]] * 2
        quads.append(dot(left, jnp.concatenate(right, axis=0)))
    wait_bytes(bt.at[pl.ds(1, 4)], recv_sem.at[3])
    local = []
    for quad in range(2):
        both = jnp.concatenate([rt[2 * quad], rt[2 * quad + 1]], axis=0)
        high, low = split(dot(both, bt[5 - quad]))
        seen = dot_nt(wide(quads[1 - quad]), jnp.concatenate([high, high, low], axis=1))
        for side in range(2):
            r = 2 * quad + side
            sibling = jnp.concatenate(split(sums[r ^ 1]), axis=1)
            local.append(seen[:, side * rank:(side + 1) * rank] + dot_nt(sibling, jnp.concatenate([bt[r]] * 2, axis=1)))
    local = jnp.concatenate(local, axis=1) + dot(wide(mid_far), vw[...])

    for c in range(CHUNKS):
        wait_bytes(cz_recv.at[c, pl.ds(0, nz - 1)], recv_sem.at[9 + c])
        top = functools.reduce(jnp.add, [cz_recv[c, place].astype(F32) for place in range(nz)])
        at = pl.ds(c * half, half)
        pair_far = (local[c * half:(c + 1) * half] + dot(wide(top), vg[...])).astype(BF)
        for r in range(4):
            far_y_send[flip(pair, r), at, :] = pair_far[:, r * rank:(r + 1) * rank]
        for k in range(ny - 1):
            place = jnp.where(rank_y > k, order[k], order[k + 1])
            mate = jnp.where(rank_y > k, order[k] // 2, order[k + 1] // 2)
            send(far_y_send.at[mate, at], far_y.at[part(y, c)], 11 + c, {"sub": z * ny + place})
        far_y[part(y, c), :] = pair_far[:, :rank]

    wait_bytes(h_recv, recv_sem.at[2])
    far = dot_nt(h_recv[...], bv[0]).astype(BF)
    near_part(1, 2)
    near[...] += dot_nt(uv[...], far)
    for c in range(CHUNKS):
        wait_bytes(far_y.at[pl.ds(0, (ny - 1) * half)], recv_sem.at[11 + c])
    far_out[...] = far_y[...]

    wait_bytes(cl_recv.at[pl.ds(1, ny - 1)], send_sem.at[0])
    wait_bytes(rt.at[pl.ds(1, 4)], send_sem.at[1])
    wait_bytes(h_send, send_sem.at[2])
    wait_bytes(bt.at[pl.ds(1, 4)], send_sem.at[3])
    wait_bytes(zs_recv.at[pl.ds(1, nz - 1)], send_sem.at[4])
    for c in range(CHUNKS):
        wait_bytes(cy_recv.at[c, pl.ds(1, ny - 1)], send_sem.at[5 + c])
        wait_bytes(x_recv.at[c, pl.ds(1, nx - 1)], send_sem.at[7 + c])
        wait_bytes(cz_recv.at[c, pl.ds(1, nz - 1)], send_sem.at[9 + c])
        wait_bytes(far_y.at[pl.ds(0, (ny - 1) * half)], send_sem.at[11 + c])


def last_kernel(near, lift, far, o_hbm, far_t, ov, store_sem):
    leaf = near.shape[0]
    chunks = store_sem.shape[0]
    tile = leaf // chunks
    far_t[...] = jnp.concatenate([far[...].T] * 2, axis=0)
    stores = []
    for step in range(chunks):
        at = pl.ds(step * tile, tile)
        ov[at, :] = (near[at, :] + dot(lift[at, :], far_t[...])).astype(BF)
        store = pltpu.make_async_copy(ov.at[at], o_hbm.at[at], store_sem.at[step])
        store.start()
        stores.append(store)
    for store in stores:
        store.wait()


def solution(mesh):
    ly = 3
    lz = mesh.shape["sub"].bit_length() - 1 - ly
    lx = mesh.shape["grp"].bit_length() - 1
    ny, nz, nx = 1 << ly, 1 << lz, 1 << lx

    def body(vectors, blocks, basis, transfer, coupling):
        leaf, vecs = vectors.shape[2:]
        rank = basis.shape[3]
        levels = transfer.shape[2]
        yblk = vecs // ny
        scratch = [
            pltpu.VMEM((leaf, vecs), BF),
            pltpu.VMEM((leaf, leaf), BF),
            pltpu.VMEM((leaf, rank), BF),
            pltpu.VMEM((rank, leaf), BF),
            pltpu.VMEM((levels, rank, rank), BF),
            pltpu.VMEM((levels, rank, rank), BF),
            pltpu.VMEM((6, rank, rank), BF),
            pltpu.VMEM((6, rank, rank), BF),
            pltpu.VMEM((3 * rank, rank), BF),
            pltpu.VMEM((3 * rank, lx * rank), BF),
            pltpu.VMEM((3 * rank, max(1, lz - 1) * rank), BF),
            pltpu.VMEM(((3 * lx - 2) * rank, rank), BF),
            pltpu.VMEM(((3 * lz - 2) * rank, rank), BF),
            pltpu.VMEM((3 * rank, 4 * rank), BF),
            pltpu.VMEM((3 * rank, 4 * rank), BF),
            pltpu.VMEM((vecs, rank), BF),
            pltpu.VMEM((vecs, rank), BF),
            pltpu.VMEM((vecs, rank), BF),
            pltpu.VMEM((CHUNKS, ny, yblk // CHUNKS, rank), BF),
            pltpu.VMEM((vecs, rank), BF),
            pltpu.VMEM((ny, yblk, rank), BF),
            pltpu.VMEM((CHUNKS, yblk // CHUNKS, rank), BF),
            pltpu.VMEM((CHUNKS, nz, yblk // CHUNKS, rank), BF),
            pltpu.VMEM((lz, yblk, rank), BF),
            pltpu.VMEM((nz, yblk, rank), BF),
            pltpu.VMEM((CHUNKS, lx, yblk // CHUNKS, rank), BF),
            pltpu.VMEM((CHUNKS, nx, yblk // CHUNKS, rank), BF),
            pltpu.VMEM((4, yblk, rank), BF),
            pltpu.VMEM((vecs, rank), BF),
            pltpu.SemaphoreType.DMA((7,)),
            pltpu.SemaphoreType.REGULAR,
            pltpu.SemaphoreType.DMA((13,)),
            pltpu.SemaphoreType.DMA((13,)),
        ]
        vmem = pl.BlockSpec(memory_space=pltpu.VMEM)
        near, lift, far = pl.pallas_call(
            functools.partial(kernel, (lz, lx)),
            out_shape=[
                jax.ShapeDtypeStruct((leaf, vecs), F32),
                jax.ShapeDtypeStruct((leaf, 2 * rank), BF),
                jax.ShapeDtypeStruct((vecs, rank), BF),
            ],
            in_specs=[pl.BlockSpec(memory_space=pltpu.HBM)] * 5,
            out_specs=[vmem] * 3,
            scratch_shapes=scratch,
            compiler_params=pltpu.CompilerParams(
                collective_id=0, has_side_effects=True, vmem_limit_bytes=32 * 1024 * 1024,
            ),
        )(*(pltpu.with_memory_space_constraint(whole[0, 0], pltpu.HBM) for whole in (vectors, blocks, basis, transfer, coupling)))
        out = pl.pallas_call(
            last_kernel,
            out_shape=jax.ShapeDtypeStruct((leaf, vecs), BF),
            in_specs=[vmem] * 3,
            out_specs=pl.BlockSpec(memory_space=pltpu.HBM),
            scratch_shapes=[
                pltpu.VMEM((2 * rank, vecs), BF),
                pltpu.VMEM((leaf, vecs), BF),
                pltpu.SemaphoreType.DMA((4,)),
            ],
            compiler_params=pltpu.CompilerParams(vmem_limit_bytes=24 * 1024 * 1024),
        )(near, lift, far)
        return out[None, None]

    return jax.shard_map(
        body,
        mesh=mesh,
        in_specs=(
            P("grp", "sub", None, None),
            P("grp", "sub", None, None),
            P("grp", "sub", None, None),
            P("grp", "sub", None, None, None),
            P("grp", "sub", None, None, None),
        ),
        out_specs=P("grp", "sub", None, None),
        check_vma=False,
    )
```

```python
import functools

import jax
import jax.numpy as jnp
from jax import lax
from jax.experimental import pallas as pl
from jax.experimental.pallas import tpu as pltpu
from jax.sharding import PartitionSpec as P

MESH = pl.DeviceIdType.MESH
BF = jnp.bfloat16
F32 = jnp.float32
CHUNKS = 1


def dot(left, right):
    return jnp.dot(left, right, preferred_element_type=F32)


def dot_nt(left, right):
    return lax.dot_general(left, right, (((1,), (1,)), ((), ())), preferred_element_type=F32)


def dot_tn(left, right):
    return lax.dot_general(left, right, (((0,), (0,)), ((), ())), preferred_element_type=F32)


def split(value):
    high = value.astype(BF)
    return high, (value - high.astype(F32)).astype(BF)


def flip(index, offset):
    out = index
    for bit in range(offset.bit_length()):
        if offset >> bit & 1:
            out = out + (1 << bit) - (2 << bit) * lax.rem(lax.div(index, 1 << bit), 2)
    return out


def xor(left, right, bits):
    out = 0
    for bit in range(bits):
        out = out + (1 << bit) * lax.rem(lax.div(left, 1 << bit) + lax.div(right, 1 << bit), 2)
    return out


def level_of(offset):
    return offset.bit_length() - 1


def far_first(count):
    return [j for j in (4, 5, 3, 7, 6, 2, 1) if j < count]


def later(index, k):
    return jnp.where(index > k, 0, 1)


def wait_bytes(ref, sem):
    pltpu.make_async_copy(ref, ref, sem).wait()


def up_weight(product):
    high, low = split(product)
    return jnp.concatenate([high, high, low], axis=0)


def up_exact(matrix):
    return jnp.concatenate([matrix, matrix, jnp.zeros_like(matrix)], axis=0)


def wide(value):
    high, low = split(value)
    return jnp.concatenate([high, low, high], axis=1)


def times_exact(product, matrix):
    high, low = split(product)
    return dot(high, matrix) + dot(low, matrix)


def kernel(dims, x_hbm, d_hbm, u_hbm, t_hbm, b_hbm, near, lift_out, far_out,
           xv, dv, uv, ut, tv, bv,
           rt, bt, wy, wx, wzl, vx, vz, vw, vg,
           h_send, h_recv, cy_send, cy_recv, cl_send, cl_recv,
           cz_send, cz_recv, zs_send, zs_recv, x_send, x_recv,
           far_y_send, far_y,
           load_sem, z_sem, send_sem, recv_sem):
    lz, lx = dims
    ly = 3
    ny, nz, nx = 1 << ly, 1 << lz, 1 << lx
    leaf, vecs = x_hbm.shape
    rank = u_hbm.shape[1]
    yblk = vecs // ny
    half = yblk // CHUNKS
    sub, grp = lax.axis_index("sub"), lax.axis_index("grp")
    y, z = lax.rem(sub, ny), lax.div(sub, ny)

    def y_peer(j):
        return {"sub": z * ny + flip(y, j)}

    def z_peer(j):
        return {"sub": flip(z, j) * ny + y}

    def x_peer(j):
        return {"grp": flip(grp, j)}

    def rows(index, size):
        return pl.ds(pl.multiple_of(index * size, size), size)

    def part(index, c):
        return pl.ds(pl.multiple_of(index * yblk + c * half, half), half)

    def send(src, dst, group, peer):
        pltpu.make_async_remote_copy(
            src_ref=src, dst_ref=dst, send_sem=send_sem.at[group], recv_sem=recv_sem.at[group],
            device_id=peer, device_id_type=MESH,
        ).start()

    head = leaf // 2
    loads = {}
    for i, (name, src, dst) in enumerate((
        ("t", t_hbm.at[pl.ds(0, ly)], tv.at[pl.ds(0, ly)]),
        ("u", u_hbm, uv),
        ("x0", x_hbm.at[pl.ds(0, head)], xv.at[pl.ds(0, head)]),
        ("x1", x_hbm.at[pl.ds(head, head)], xv.at[pl.ds(head, head)]),
        ("t1", t_hbm.at[pl.ds(ly, lz + lx)], tv.at[pl.ds(ly, lz + lx)]),
        ("b", b_hbm, bv),
        ("d", d_hbm, dv),
    )):
        loads[name] = pltpu.make_async_copy(src, dst, load_sem.at[i])
    for name in ("t", "u", "x0", "x1"):
        loads[name].start()

    order = sorted(range(ny), key=lambda place: min(place, ny - place))
    rank_y = sum(jnp.where(y == place, k, 0) for k, place in enumerate(order))
    chips = sorted(range(1, nx // 2), key=lambda place: min(place, nx // 2 - place))
    places = [1, 0] + [2 * chip + core for chip in chips for core in range(2)]
    rank_x = sum(jnp.where(grp == place, k, 0) for k, place in enumerate(places))
    barrier = pltpu.get_barrier_semaphore()

    def greet(sem, peer):
        pl.semaphore_signal(sem, inc=1, device_id=peer, device_id_type=MESH)

    for j in far_first(ny):
        greet(barrier, y_peer(j))
    for place in reversed(range(nz)):
        @pl.when(z < place)
        def _():
            greet(barrier, {"sub": place * ny + y})
    for j in far_first(nx):
        greet(barrier, x_peer(j))

    pair = lax.div(y, 2)
    outward = 2 * lax.rem(y, 2) - 1

    def spread(src, dst, group):
        for k in (3, 2, 1):
            target = lax.rem(y + k * outward + ny, ny)
            other = lax.div(target, 2)
            slot = lax.rem(pair + other, 2) + 2 * lax.rem(lax.div(pair, 2) + lax.div(other, 2), 2)
            send(src.at[1], dst.at[slot], group, {"sub": z * ny + target})
        send(src.at[2], dst.at[4], group, y_peer(6))

    def climb(base, levels):
        product = tv[base].astype(F32)
        chain = [product]
        for level in range(1, levels):
            product = times_exact(product, tv[base + level])
            chain.append(product)
        return chain

    def down(products, base, levels):
        parts = [bv[base].T]
        for i in range(1, levels):
            parts.append(up_weight(times_exact(products[i - 1], bv[base + i]).T))
        return jnp.concatenate(parts, axis=0)

    def near_part(part, parts):
        size = vecs // parts
        at = pl.ds(part * size, size)
        near[:, at] = dot(dv[...], xv[:, at])

    loads["t"].wait()
    ty = climb(0, ly)
    wy[...] = up_weight(ty[ly - 1])
    loads["u"].wait()
    ut[...] = uv[...].T
    loads["x0"].wait()
    hat_t = dot(ut[:, :head], xv[:head, :])
    loads["x1"].wait()
    for name in ("t1", "b", "d"):
        loads[name].start()
    hat = (hat_t + dot(ut[:, head:], xv[head:, :])).T
    hat_w = wide(hat)
    cy_send[...] = dot(hat_w, wy[...]).astype(BF)
    pl.semaphore_wait(barrier, ny - 1 + nx - 1 + z)
    for c in range(CHUNKS):
        for j in far_first(ny):
            send(cy_send.at[part(flip(y, j), c)], cy_recv.at[c, j], 5 + c, y_peer(j))
    for place in range(nz):
        @pl.when(z > place)
        def _():
            greet(z_sem, {"sub": place * ny + y})

    cl_send[...] = dot(hat_w[:, :2 * rank], jnp.concatenate([tv[0], tv[0]], axis=0)).astype(BF)
    h_send[...] = hat.astype(BF)
    loads["t1"].wait()
    tz = climb(ly, lz + lx - 1)
    wx[...] = jnp.concatenate([up_weight(product) for product in tz[lz - 1:]], axis=1)
    loads["b"].wait()
    vx[...] = down(climb(ly + lz, lx), ly + lz, lx)

    mids = []
    for c in range(CHUNKS):
        wait_bytes(cy_recv.at[c, pl.ds(1, ny - 1)], recv_sem.at[5 + c])
        mid = cy_send[part(y, c), :].astype(F32)
        for j in range(1, ny):
            mid = mid + cy_recv[c, j].astype(F32)
        mids.append(wide(mid))
        share = dot(mids[c], wx[...])
        for i in range(lx):
            x_send[c, i] = share[:, i * rank:(i + 1) * rank].astype(BF)
        for k in range(nx - 1):
            target = jnp.where(rank_x > k, places[k], places[k + 1])
            apart = xor(grp, target, lx)
            level = sum(jnp.where(apart >= 1 << i, 1, 0) for i in range(1, lx))
            send(x_send.at[c, level], x_recv.at[c, apart], 7 + c, {"grp": target})

    mid_w = jnp.concatenate(mids, axis=0)
    zs_send[0] = mid_w[:, :rank]
    if lz > 1:
        wzl[...] = jnp.concatenate([up_exact(tv[ly])] + [up_weight(tz[i]) for i in range(1, lz - 1)], axis=1)
        zl = dot(mid_w, wzl[...])
        for i in range(lz - 1):
            zs_send[i + 1] = zl[:, i * rank:(i + 1) * rank].astype(BF)

    @pl.when(z < nz - 1)
    def _():
        pl.semaphore_wait(z_sem, nz - 1 - z)

    for j in far_first(nz):
        send(zs_send.at[level_of(j)], zs_recv.at[j], 4, z_peer(j))
    for j in far_first(ny):
        send(cl_send.at[rows(flip(y, j), yblk)], cl_recv.at[j], 0, y_peer(j))
    spread(t_hbm, rt, 1)
    spread(b_hbm, bt, 3)
    send(h_send, h_recv, 2, y_peer(1))

    for c in range(CHUNKS):
        wait_bytes(x_recv.at[c, pl.ds(1, nx - 1)], recv_sem.at[7 + c])
        parts = [x_recv[c, 1]]
        for level in range(1, lx):
            parts.append(wide(functools.reduce(jnp.add, [x_recv[c, j].astype(F32) for j in range(1 << level, 2 << level)])))
        top = dot(jnp.concatenate(parts, axis=1), vx[...])
        cz_send[c] = top.astype(BF)
        for k in range(nz - 1):
            send(cz_send.at[c], cz_recv.at[c, z], 9 + c, {"sub": (k + later(z, k)) * ny + y})
        cz_recv[c, z] = cz_send[c]

    vz[...] = down(tz, ly, lz)

    lift_out[...] = jnp.concatenate(split(dot(uv[...], tv[0])), axis=1)
    loads["d"].wait()
    near_part(0, 2)
    rt[0] = tv[1]
    rt[5] = tv[2]
    bt[0] = bv[1]
    bt[5] = bv[2]
    wait_bytes(rt.at[pl.ds(1, 4)], recv_sem.at[1])
    lifts = []
    for quad in range(2):
        both = jnp.concatenate([rt[2 * quad], rt[2 * quad + 1]], axis=0)
        lifts.append(dot(both, rt[5 - quad]))
    lifts = jnp.concatenate(lifts, axis=0)
    whole = dot(wide(lifts), wx[:, :rank])
    for r in range(4):
        at = slice(r * rank, (r + 1) * rank)
        vw[:, at] = up_weight(lifts[at].T)
        vg[:, at] = up_weight(whole[at].T)
    wait_bytes(zs_recv.at[pl.ds(1, nz - 1)], recv_sem.at[4])
    parts = [zs_recv[1]]
    for level in range(1, lz):
        parts.append(wide(functools.reduce(jnp.add, [zs_recv[j].astype(F32) for j in range(1 << level, 2 << level)])))
    mid_far = dot(jnp.concatenate(parts, axis=1), vz[...])

    wait_bytes(cl_recv.at[pl.ds(1, ny - 1)], recv_sem.at[0])
    given = [cl_send[rows(y, yblk), :]] + [cl_recv[j] for j in range(1, ny)]
    sums = [given[2 * r].astype(F32) + given[2 * r + 1].astype(F32) for r in range(4)]
    quads = []
    for quad in range(2):
        left = jnp.concatenate([*split(sums[2 * quad]), *split(sums[2 * quad + 1])], axis=1)
        right = [rt[2 * quad]] * 2 + [rt[2 * quad + 1]] * 2
        quads.append(dot(left, jnp.concatenate(right, axis=0)))
    wait_bytes(bt.at[pl.ds(1, 4)], recv_sem.at[3])
    local = []
    for quad in range(2):
        both = jnp.concatenate([rt[2 * quad], rt[2 * quad + 1]], axis=0)
        high, low = split(dot(both, bt[5 - quad]))
        seen = dot_nt(wide(quads[1 - quad]), jnp.concatenate([high, high, low], axis=1))
        for side in range(2):
            r = 2 * quad + side
            sibling = jnp.concatenate(split(sums[r ^ 1]), axis=1)
            local.append(seen[:, side * rank:(side + 1) * rank] + dot_nt(sibling, jnp.concatenate([bt[r]] * 2, axis=1)))
    local = jnp.concatenate(local, axis=1) + dot(wide(mid_far), vw[...])

    for c in range(CHUNKS):
        wait_bytes(cz_recv.at[c, pl.ds(0, nz - 1)], recv_sem.at[9 + c])
        top = functools.reduce(jnp.add, [cz_recv[c, place].astype(F32) for place in range(nz)])
        at = pl.ds(c * half, half)
        pair_far = (local[c * half:(c + 1) * half] + dot(wide(top), vg[...])).astype(BF)
        for r in range(4):
            far_y_send[flip(pair, r), at, :] = pair_far[:, r * rank:(r + 1) * rank]
        for k in range(ny - 1):
            place = jnp.where(rank_y > k, order[k], order[k + 1])
            mate = jnp.where(rank_y > k, order[k] // 2, order[k + 1] // 2)
            send(far_y_send.at[mate, at], far_y.at[part(y, c)], 11 + c, {"sub": z * ny + place})
        far_y[part(y, c), :] = pair_far[:, :rank]

    wait_bytes(h_recv, recv_sem.at[2])
    far = dot_nt(h_recv[...], bv[0]).astype(BF)
    near_part(1, 2)
    near[...] += dot_nt(uv[...], far)
    for c in range(CHUNKS):
        wait_bytes(far_y.at[pl.ds(0, (ny - 1) * half)], recv_sem.at[11 + c])
    far_out[...] = far_y[...]

    wait_bytes(cl_recv.at[pl.ds(1, ny - 1)], send_sem.at[0])
    wait_bytes(rt.at[pl.ds(1, 4)], send_sem.at[1])
    wait_bytes(h_send, send_sem.at[2])
    wait_bytes(bt.at[pl.ds(1, 4)], send_sem.at[3])
    wait_bytes(zs_recv.at[pl.ds(1, nz - 1)], send_sem.at[4])
    for c in range(CHUNKS):
        wait_bytes(cy_recv.at[c, pl.ds(1, ny - 1)], send_sem.at[5 + c])
        wait_bytes(x_recv.at[c, pl.ds(1, nx - 1)], send_sem.at[7 + c])
        wait_bytes(cz_recv.at[c, pl.ds(1, nz - 1)], send_sem.at[9 + c])
        wait_bytes(far_y.at[pl.ds(0, (ny - 1) * half)], send_sem.at[11 + c])


def last_kernel(near, lift, far, o_hbm, far_t, ov, store_sem):
    leaf = near.shape[0]
    chunks = store_sem.shape[0]
    tile = leaf // chunks
    far_t[...] = jnp.concatenate([far[...].T] * 2, axis=0)
    stores = []
    for step in range(chunks):
        at = pl.ds(step * tile, tile)
        ov[at, :] = (near[at, :] + dot(lift[at, :], far_t[...])).astype(BF)
        store = pltpu.make_async_copy(ov.at[at], o_hbm.at[at], store_sem.at[step])
        store.start()
        stores.append(store)
    for store in stores:
        store.wait()


def solution(mesh):
    ly = 3
    lz = mesh.shape["sub"].bit_length() - 1 - ly
    lx = mesh.shape["grp"].bit_length() - 1
    ny, nz, nx = 1 << ly, 1 << lz, 1 << lx

    def body(vectors, blocks, basis, transfer, coupling):
        leaf, vecs = vectors.shape[2:]
        rank = basis.shape[3]
        levels = transfer.shape[2]
        yblk = vecs // ny
        scratch = [
            pltpu.VMEM((leaf, vecs), BF),
            pltpu.VMEM((leaf, leaf), BF),
            pltpu.VMEM((leaf, rank), BF),
            pltpu.VMEM((rank, leaf), BF),
            pltpu.VMEM((levels, rank, rank), BF),
            pltpu.VMEM((levels, rank, rank), BF),
            pltpu.VMEM((6, rank, rank), BF),
            pltpu.VMEM((6, rank, rank), BF),
            pltpu.VMEM((3 * rank, rank), BF),
            pltpu.VMEM((3 * rank, lx * rank), BF),
            pltpu.VMEM((3 * rank, max(1, lz - 1) * rank), BF),
            pltpu.VMEM(((3 * lx - 2) * rank, rank), BF),
            pltpu.VMEM(((3 * lz - 2) * rank, rank), BF),
            pltpu.VMEM((3 * rank, 4 * rank), BF),
            pltpu.VMEM((3 * rank, 4 * rank), BF),
            pltpu.VMEM((vecs, rank), BF),
            pltpu.VMEM((vecs, rank), BF),
            pltpu.VMEM((vecs, rank), BF),
            pltpu.VMEM((CHUNKS, ny, yblk // CHUNKS, rank), BF),
            pltpu.VMEM((vecs, rank), BF),
            pltpu.VMEM((ny, yblk, rank), BF),
            pltpu.VMEM((CHUNKS, yblk // CHUNKS, rank), BF),
            pltpu.VMEM((CHUNKS, nz, yblk // CHUNKS, rank), BF),
            pltpu.VMEM((lz, yblk, rank), BF),
            pltpu.VMEM((nz, yblk, rank), BF),
            pltpu.VMEM((CHUNKS, lx, yblk // CHUNKS, rank), BF),
            pltpu.VMEM((CHUNKS, nx, yblk // CHUNKS, rank), BF),
            pltpu.VMEM((4, yblk, rank), BF),
            pltpu.VMEM((vecs, rank), BF),
            pltpu.SemaphoreType.DMA((7,)),
            pltpu.SemaphoreType.REGULAR,
            pltpu.SemaphoreType.DMA((13,)),
            pltpu.SemaphoreType.DMA((13,)),
        ]
        vmem = pl.BlockSpec(memory_space=pltpu.VMEM)
        near, lift, far = pl.pallas_call(
            functools.partial(kernel, (lz, lx)),
            out_shape=[
                jax.ShapeDtypeStruct((leaf, vecs), F32),
                jax.ShapeDtypeStruct((leaf, 2 * rank), BF),
                jax.ShapeDtypeStruct((vecs, rank), BF),
            ],
            in_specs=[pl.BlockSpec(memory_space=pltpu.HBM)] * 5,
            out_specs=[vmem] * 3,
            scratch_shapes=scratch,
            compiler_params=pltpu.CompilerParams(
                collective_id=0, has_side_effects=True, vmem_limit_bytes=32 * 1024 * 1024,
            ),
        )(*(pltpu.with_memory_space_constraint(whole[0, 0], pltpu.HBM) for whole in (vectors, blocks, basis, transfer, coupling)))
        out = pl.pallas_call(
            last_kernel,
            out_shape=jax.ShapeDtypeStruct((leaf, vecs), BF),
            in_specs=[vmem] * 3,
            out_specs=pl.BlockSpec(memory_space=pltpu.HBM),
            scratch_shapes=[
                pltpu.VMEM((2 * rank, vecs), BF),
                pltpu.VMEM((leaf, vecs), BF),
                pltpu.SemaphoreType.DMA((4,)),
            ],
            compiler_params=pltpu.CompilerParams(vmem_limit_bytes=24 * 1024 * 1024),
        )(near, lift, far)
        return out[None, None]

    return jax.shard_map(
        body,
        mesh=mesh,
        in_specs=(
            P("grp", "sub", None, None),
            P("grp", "sub", None, None),
            P("grp", "sub", None, None),
            P("grp", "sub", None, None, None),
            P("grp", "sub", None, None, None),
        ),
        out_specs=P("grp", "sub", None, None),
        check_vma=False,
    )
```

```python
import functools

import jax
import jax.numpy as jnp
from jax import lax
from jax.experimental import pallas as pl
from jax.experimental.pallas import tpu as pltpu
from jax.sharding import PartitionSpec as P

MESH = pl.DeviceIdType.MESH
BF = jnp.bfloat16
F32 = jnp.float32
CHUNKS = 1


def dot(left, right):
    return jnp.dot(left, right, preferred_element_type=F32)


def dot_nt(left, right):
    return lax.dot_general(left, right, (((1,), (1,)), ((), ())), preferred_element_type=F32)


def dot_tn(left, right):
    return lax.dot_general(left, right, (((0,), (0,)), ((), ())), preferred_element_type=F32)


def split(value):
    high = value.astype(BF)
    return high, (value - high.astype(F32)).astype(BF)


def flip(index, offset):
    out = index
    for bit in range(offset.bit_length()):
        if offset >> bit & 1:
            out = out + (1 << bit) - (2 << bit) * lax.rem(lax.div(index, 1 << bit), 2)
    return out


def xor(left, right, bits):
    out = 0
    for bit in range(bits):
        out = out + (1 << bit) * lax.rem(lax.div(left, 1 << bit) + lax.div(right, 1 << bit), 2)
    return out


def level_of(offset):
    return offset.bit_length() - 1


def far_first(count):
    return [j for j in (4, 5, 3, 7, 6, 2, 1) if j < count]


def later(index, k):
    return jnp.where(index > k, 0, 1)


def wait_bytes(ref, sem):
    pltpu.make_async_copy(ref, ref, sem).wait()


def up_weight(product):
    high, low = split(product)
    return jnp.concatenate([high, high, low], axis=0)


def up_exact(matrix):
    return jnp.concatenate([matrix, matrix, jnp.zeros_like(matrix)], axis=0)


def wide(value):
    high, low = split(value)
    return jnp.concatenate([high, low, high], axis=1)


def times_exact(product, matrix):
    high, low = split(product)
    return dot(high, matrix) + dot(low, matrix)


def kernel(dims, x_hbm, d_hbm, u_hbm, t_hbm, b_hbm, near, lift_out, far_out,
           xv, dv, uv, ut, tv, bv,
           rt, bt, wy, wx, wzl, vx, vz, vw, vg,
           h_send, h_recv, cy_send, cy_recv, cl_send, cl_recv,
           cz_send, cz_recv, zs_send, zs_recv, x_send, x_recv,
           far_y_send, far_y,
           load_sem, z_sem, send_sem, recv_sem):
    lz, lx = dims
    ly = 3
    ny, nz, nx = 1 << ly, 1 << lz, 1 << lx
    leaf, vecs = x_hbm.shape
    rank = u_hbm.shape[1]
    yblk = vecs // ny
    half = yblk // CHUNKS
    sub, grp = lax.axis_index("sub"), lax.axis_index("grp")
    y, z = lax.rem(sub, ny), lax.div(sub, ny)

    def y_peer(j):
        return {"sub": z * ny + flip(y, j)}

    def z_peer(j):
        return {"sub": flip(z, j) * ny + y}

    def x_peer(j):
        return {"grp": flip(grp, j)}

    def rows(index, size):
        return pl.ds(pl.multiple_of(index * size, size), size)

    def part(index, c):
        return pl.ds(pl.multiple_of(index * yblk + c * half, half), half)

    def send(src, dst, group, peer):
        pltpu.make_async_remote_copy(
            src_ref=src, dst_ref=dst, send_sem=send_sem.at[group], recv_sem=recv_sem.at[group],
            device_id=peer, device_id_type=MESH,
        ).start()

    head = leaf // 2
    loads = {}
    for i, (name, src, dst) in enumerate((
        ("t", t_hbm.at[pl.ds(0, ly)], tv.at[pl.ds(0, ly)]),
        ("u", u_hbm, uv),
        ("x0", x_hbm.at[pl.ds(0, head)], xv.at[pl.ds(0, head)]),
        ("x1", x_hbm.at[pl.ds(head, head)], xv.at[pl.ds(head, head)]),
        ("t1", t_hbm.at[pl.ds(ly, lz + lx)], tv.at[pl.ds(ly, lz + lx)]),
        ("b", b_hbm, bv),
        ("d", d_hbm, dv),
    )):
        loads[name] = pltpu.make_async_copy(src, dst, load_sem.at[i])
    for name in ("t", "u", "x0", "x1"):
        loads[name].start()

    first = (grp == 1) & (y > 0)
    chips = sorted(range(1, nx // 2), key=lambda place: min(place, nx // 2 - place))
    places = [1, 0] + [2 * chip + core for chip in chips for core in range(2)]
    rank_x = sum(jnp.where(grp == place, k, 0) for k, place in enumerate(places))
    barrier = pltpu.get_barrier_semaphore()

    def greet(sem, peer):
        pl.semaphore_signal(sem, inc=1, device_id=peer, device_id_type=MESH)

    for j in far_first(ny):
        greet(barrier, y_peer(j))
    for place in reversed(range(nz)):
        @pl.when(z < place)
        def _():
            greet(barrier, {"sub": place * ny + y})
    for j in far_first(nx):
        greet(barrier, x_peer(j))

    pair = lax.div(y, 2)
    outward = 2 * lax.rem(y, 2) - 1

    def spread(src, dst, group):
        for k in (3, 2, 1):
            target = lax.rem(y + k * outward + ny, ny)
            other = lax.div(target, 2)
            slot = lax.rem(pair + other, 2) + 2 * lax.rem(lax.div(pair, 2) + lax.div(other, 2), 2)
            send(src.at[1], dst.at[slot], group, {"sub": z * ny + target})
        send(src.at[2], dst.at[4], group, y_peer(6))

    def climb(base, levels):
        product = tv[base].astype(F32)
        chain = [product]
        for level in range(1, levels):
            product = times_exact(product, tv[base + level])
            chain.append(product)
        return chain

    def down(products, base, levels):
        parts = [bv[base].T]
        for i in range(1, levels):
            parts.append(up_weight(times_exact(products[i - 1], bv[base + i]).T))
        return jnp.concatenate(parts, axis=0)

    def near_part(part, parts):
        size = vecs // parts
        at = pl.ds(part * size, size)
        near[:, at] = dot(dv[...], xv[:, at])

    loads["t"].wait()
    ty = climb(0, ly)
    wy[...] = up_weight(ty[ly - 1])
    loads["u"].wait()
    ut[...] = uv[...].T
    loads["x0"].wait()
    hat_t = dot(ut[:, :head], xv[:head, :])
    loads["x1"].wait()
    for name in ("t1", "b", "d"):
        loads[name].start()
    hat = (hat_t + dot(ut[:, head:], xv[head:, :])).T
    hat_w = wide(hat)
    cy_send[...] = dot(hat_w, wy[...]).astype(BF)
    pl.semaphore_wait(barrier, ny - 1 + nx - 1 + z)
    for c in range(CHUNKS):
        for j in far_first(ny):
            send(cy_send.at[part(flip(y, j), c)], cy_recv.at[c, j], 5 + c, y_peer(j))
    for place in range(nz):
        @pl.when(z > place)
        def _():
            greet(z_sem, {"sub": place * ny + y})

    cl_send[...] = dot(hat_w[:, :2 * rank], jnp.concatenate([tv[0], tv[0]], axis=0)).astype(BF)
    h_send[...] = hat.astype(BF)
    loads["t1"].wait()
    tz = climb(ly, lz + lx - 1)
    wx[...] = jnp.concatenate([up_weight(product) for product in tz[lz - 1:]], axis=1)
    loads["b"].wait()
    vx[...] = down(climb(ly + lz, lx), ly + lz, lx)

    mids = []
    for c in range(CHUNKS):
        wait_bytes(cy_recv.at[c, pl.ds(1, ny - 1)], recv_sem.at[5 + c])
        mid = cy_send[part(y, c), :].astype(F32)
        for j in range(1, ny):
            mid = mid + cy_recv[c, j].astype(F32)
        mids.append(wide(mid))
        share = dot(mids[c], wx[...])
        for i in range(lx):
            x_send[c, i] = share[:, i * rank:(i + 1) * rank].astype(BF)
        for k in range(nx - 1):
            target = jnp.where(rank_x > k, places[k], places[k + 1])
            apart = xor(grp, target, lx)
            level = sum(jnp.where(apart >= 1 << i, 1, 0) for i in range(1, lx))
            send(x_send.at[c, level], x_recv.at[c, apart], 7 + c, {"grp": target})

    mid_w = jnp.concatenate(mids, axis=0)
    zs_send[0] = mid_w[:, :rank]
    if lz > 1:
        wzl[...] = jnp.concatenate([up_exact(tv[ly])] + [up_weight(tz[i]) for i in range(1, lz - 1)], axis=1)
        zl = dot(mid_w, wzl[...])
        for i in range(lz - 1):
            zs_send[i + 1] = zl[:, i * rank:(i + 1) * rank].astype(BF)

    @pl.when(z < nz - 1)
    def _():
        pl.semaphore_wait(z_sem, nz - 1 - z)

    for j in far_first(nz):
        send(zs_send.at[level_of(j)], zs_recv.at[j], 4, z_peer(j))
    for j in far_first(ny):
        send(cl_send.at[rows(flip(y, j), yblk)], cl_recv.at[j], 0, y_peer(j))
    spread(t_hbm, rt, 1)
    spread(b_hbm, bt, 3)
    send(h_send, h_recv, 2, y_peer(1))

    for c in range(CHUNKS):
        wait_bytes(x_recv.at[c, pl.ds(1, nx - 1)], recv_sem.at[7 + c])
        parts = [x_recv[c, 1]]
        for level in range(1, lx):
            parts.append(wide(functools.reduce(jnp.add, [x_recv[c, j].astype(F32) for j in range(1 << level, 2 << level)])))
        top = dot(jnp.concatenate(parts, axis=1), vx[...])
        cz_send[c] = top.astype(BF)
        for k in range(nz - 1):
            send(cz_send.at[c], cz_recv.at[c, z], 9 + c, {"sub": (k + later(z, k)) * ny + y})
        cz_recv[c, z] = cz_send[c]

    vz[...] = down(tz, ly, lz)

    lift_out[...] = jnp.concatenate(split(dot(uv[...], tv[0])), axis=1)
    loads["d"].wait()
    near_part(0, 2)
    rt[0] = tv[1]
    rt[5] = tv[2]
    bt[0] = bv[1]
    bt[5] = bv[2]
    wait_bytes(rt.at[pl.ds(1, 4)], recv_sem.at[1])
    lifts = []
    for quad in range(2):
        both = jnp.concatenate([rt[2 * quad], rt[2 * quad + 1]], axis=0)
        lifts.append(dot(both, rt[5 - quad]))
    lifts = jnp.concatenate(lifts, axis=0)
    whole = dot(wide(lifts), wx[:, :rank])
    for r in range(4):
        at = slice(r * rank, (r + 1) * rank)
        vw[:, at] = up_weight(lifts[at].T)
        vg[:, at] = up_weight(whole[at].T)
    wait_bytes(zs_recv.at[pl.ds(1, nz - 1)], recv_sem.at[4])
    parts = [zs_recv[1]]
    for level in range(1, lz):
        parts.append(wide(functools.reduce(jnp.add, [zs_recv[j].astype(F32) for j in range(1 << level, 2 << level)])))
    mid_far = dot(jnp.concatenate(parts, axis=1), vz[...])

    wait_bytes(cl_recv.at[pl.ds(1, ny - 1)], recv_sem.at[0])
    given = [cl_send[rows(y, yblk), :]] + [cl_recv[j] for j in range(1, ny)]
    sums = [given[2 * r].astype(F32) + given[2 * r + 1].astype(F32) for r in range(4)]
    quads = []
    for quad in range(2):
        left = jnp.concatenate([*split(sums[2 * quad]), *split(sums[2 * quad + 1])], axis=1)
        right = [rt[2 * quad]] * 2 + [rt[2 * quad + 1]] * 2
        quads.append(dot(left, jnp.concatenate(right, axis=0)))
    wait_bytes(bt.at[pl.ds(1, 4)], recv_sem.at[3])
    local = []
    for quad in range(2):
        both = jnp.concatenate([rt[2 * quad], rt[2 * quad + 1]], axis=0)
        high, low = split(dot(both, bt[5 - quad]))
        seen = dot_nt(wide(quads[1 - quad]), jnp.concatenate([high, high, low], axis=1))
        for side in range(2):
            r = 2 * quad + side
            sibling = jnp.concatenate(split(sums[r ^ 1]), axis=1)
            local.append(seen[:, side * rank:(side + 1) * rank] + dot_nt(sibling, jnp.concatenate([bt[r]] * 2, axis=1)))
    local = jnp.concatenate(local, axis=1) + dot(wide(mid_far), vw[...])

    for c in range(CHUNKS):
        wait_bytes(cz_recv.at[c, pl.ds(0, nz - 1)], recv_sem.at[9 + c])
        top = functools.reduce(jnp.add, [cz_recv[c, place].astype(F32) for place in range(nz)])
        at = pl.ds(c * half, half)
        pair_far = (local[c * half:(c + 1) * half] + dot(wide(top), vg[...])).astype(BF)
        for r in range(4):
            far_y_send[flip(pair, r), at, :] = pair_far[:, r * rank:(r + 1) * rank]
        apart = far_first(ny)
        own = sum(jnp.where(y == j, k, 0) for k, j in enumerate(apart))
        for k, j in enumerate(apart):
            j = jnp.where(first, jnp.where(own >= k, apart[max(k - 1, 0)], j) if k else y, j)
            place = xor(y, j, ly)
            send(far_y_send.at[lax.div(place, 2), at], far_y.at[part(y, c)], 11 + c, {"sub": z * ny + place})
        far_y[part(y, c), :] = pair_far[:, :rank]

    wait_bytes(h_recv, recv_sem.at[2])
    far = dot_nt(h_recv[...], bv[0]).astype(BF)
    near_part(1, 2)
    near[...] += dot_nt(uv[...], far)
    for c in range(CHUNKS):
        wait_bytes(far_y.at[pl.ds(0, (ny - 1) * half)], recv_sem.at[11 + c])
    far_out[...] = far_y[...]

    wait_bytes(cl_recv.at[pl.ds(1, ny - 1)], send_sem.at[0])
    wait_bytes(rt.at[pl.ds(1, 4)], send_sem.at[1])
    wait_bytes(h_send, send_sem.at[2])
    wait_bytes(bt.at[pl.ds(1, 4)], send_sem.at[3])
    wait_bytes(zs_recv.at[pl.ds(1, nz - 1)], send_sem.at[4])
    for c in range(CHUNKS):
        wait_bytes(cy_recv.at[c, pl.ds(1, ny - 1)], send_sem.at[5 + c])
        wait_bytes(x_recv.at[c, pl.ds(1, nx - 1)], send_sem.at[7 + c])
        wait_bytes(cz_recv.at[c, pl.ds(1, nz - 1)], send_sem.at[9 + c])
        wait_bytes(far_y.at[pl.ds(0, (ny - 1) * half)], send_sem.at[11 + c])


def last_kernel(near, lift, far, o_hbm, far_t, ov, store_sem):
    leaf = near.shape[0]
    chunks = store_sem.shape[0]
    tile = leaf // chunks
    far_t[...] = jnp.concatenate([far[...].T] * 2, axis=0)
    stores = []
    for step in range(chunks):
        at = pl.ds(step * tile, tile)
        ov[at, :] = (near[at, :] + dot(lift[at, :], far_t[...])).astype(BF)
        store = pltpu.make_async_copy(ov.at[at], o_hbm.at[at], store_sem.at[step])
        store.start()
        stores.append(store)
    for store in stores:
        store.wait()


def solution(mesh):
    ly = 3
    lz = mesh.shape["sub"].bit_length() - 1 - ly
    lx = mesh.shape["grp"].bit_length() - 1
    ny, nz, nx = 1 << ly, 1 << lz, 1 << lx

    def body(vectors, blocks, basis, transfer, coupling):
        leaf, vecs = vectors.shape[2:]
        rank = basis.shape[3]
        levels = transfer.shape[2]
        yblk = vecs // ny
        scratch = [
            pltpu.VMEM((leaf, vecs), BF),
            pltpu.VMEM((leaf, leaf), BF),
            pltpu.VMEM((leaf, rank), BF),
            pltpu.VMEM((rank, leaf), BF),
            pltpu.VMEM((levels, rank, rank), BF),
            pltpu.VMEM((levels, rank, rank), BF),
            pltpu.VMEM((6, rank, rank), BF),
            pltpu.VMEM((6, rank, rank), BF),
            pltpu.VMEM((3 * rank, rank), BF),
            pltpu.VMEM((3 * rank, lx * rank), BF),
            pltpu.VMEM((3 * rank, max(1, lz - 1) * rank), BF),
            pltpu.VMEM(((3 * lx - 2) * rank, rank), BF),
            pltpu.VMEM(((3 * lz - 2) * rank, rank), BF),
            pltpu.VMEM((3 * rank, 4 * rank), BF),
            pltpu.VMEM((3 * rank, 4 * rank), BF),
            pltpu.VMEM((vecs, rank), BF),
            pltpu.VMEM((vecs, rank), BF),
            pltpu.VMEM((vecs, rank), BF),
            pltpu.VMEM((CHUNKS, ny, yblk // CHUNKS, rank), BF),
            pltpu.VMEM((vecs, rank), BF),
            pltpu.VMEM((ny, yblk, rank), BF),
            pltpu.VMEM((CHUNKS, yblk // CHUNKS, rank), BF),
            pltpu.VMEM((CHUNKS, nz, yblk // CHUNKS, rank), BF),
            pltpu.VMEM((lz, yblk, rank), BF),
            pltpu.VMEM((nz, yblk, rank), BF),
            pltpu.VMEM((CHUNKS, lx, yblk // CHUNKS, rank), BF),
            pltpu.VMEM((CHUNKS, nx, yblk // CHUNKS, rank), BF),
            pltpu.VMEM((4, yblk, rank), BF),
            pltpu.VMEM((vecs, rank), BF),
            pltpu.SemaphoreType.DMA((7,)),
            pltpu.SemaphoreType.REGULAR,
            pltpu.SemaphoreType.DMA((13,)),
            pltpu.SemaphoreType.DMA((13,)),
        ]
        vmem = pl.BlockSpec(memory_space=pltpu.VMEM)
        near, lift, far = pl.pallas_call(
            functools.partial(kernel, (lz, lx)),
            out_shape=[
                jax.ShapeDtypeStruct((leaf, vecs), F32),
                jax.ShapeDtypeStruct((leaf, 2 * rank), BF),
                jax.ShapeDtypeStruct((vecs, rank), BF),
            ],
            in_specs=[pl.BlockSpec(memory_space=pltpu.HBM)] * 5,
            out_specs=[vmem] * 3,
            scratch_shapes=scratch,
            compiler_params=pltpu.CompilerParams(
                collective_id=0, has_side_effects=True, vmem_limit_bytes=32 * 1024 * 1024,
            ),
        )(*(pltpu.with_memory_space_constraint(whole[0, 0], pltpu.HBM) for whole in (vectors, blocks, basis, transfer, coupling)))
        out = pl.pallas_call(
            last_kernel,
            out_shape=jax.ShapeDtypeStruct((leaf, vecs), BF),
            in_specs=[vmem] * 3,
            out_specs=pl.BlockSpec(memory_space=pltpu.HBM),
            scratch_shapes=[
                pltpu.VMEM((2 * rank, vecs), BF),
                pltpu.VMEM((leaf, vecs), BF),
                pltpu.SemaphoreType.DMA((4,)),
            ],
            compiler_params=pltpu.CompilerParams(vmem_limit_bytes=24 * 1024 * 1024),
        )(near, lift, far)
        return out[None, None]

    return jax.shard_map(
        body,
        mesh=mesh,
        in_specs=(
            P("grp", "sub", None, None),
            P("grp", "sub", None, None),
            P("grp", "sub", None, None),
            P("grp", "sub", None, None, None),
            P("grp", "sub", None, None, None),
        ),
        out_specs=P("grp", "sub", None, None),
        check_vma=False,
    )
```

```python
import functools

import jax
import jax.numpy as jnp
from jax import lax
from jax.experimental import pallas as pl
from jax.experimental.pallas import tpu as pltpu
from jax.sharding import PartitionSpec as P

MESH = pl.DeviceIdType.MESH
BF = jnp.bfloat16
F32 = jnp.float32


def dot(left, right):
    return jnp.dot(left, right, preferred_element_type=F32)


def dot_nt(left, right):
    return lax.dot_general(left, right, (((1,), (1,)), ((), ())), preferred_element_type=F32)


def dot_tn(left, right):
    return lax.dot_general(left, right, (((0,), (0,)), ((), ())), preferred_element_type=F32)


def split(value):
    high = value.astype(BF)
    return high, (value - high.astype(F32)).astype(BF)


def flip(index, offset):
    out = index
    for bit in range(offset.bit_length()):
        if offset >> bit & 1:
            out = out + (1 << bit) - (2 << bit) * lax.rem(lax.div(index, 1 << bit), 2)
    return out


def level_of(offset):
    return offset.bit_length() - 1


def far_first(count):
    return [j for j in (4, 5, 3, 7, 6, 2, 1) if j < count]


def early(count, cores):
    ring = sorted(range(count), key=lambda place: place if place < count // 2 else count - place + 1.5)
    return [place * cores + core for place in ring for core in reversed(range(cores))]


def wait_bytes(ref, sem):
    pltpu.make_async_copy(ref, ref, sem).wait()


def up_weight(product):
    high, low = split(product)
    return jnp.concatenate([high, high, low], axis=0)


def up_exact(matrix):
    return jnp.concatenate([matrix, matrix, jnp.zeros_like(matrix)], axis=0)


def wide(value):
    high, low = split(value)
    return jnp.concatenate([high, low, high], axis=1)


def twice(product):
    return jnp.concatenate([product.astype(BF)] * 2, axis=0)


def tight(value):
    return jnp.concatenate(split(value), axis=1)


def times_exact(product, matrix):
    high, low = split(product)
    return dot(high, matrix) + dot(low, matrix)


def kernel(dims, x_hbm, d_hbm, u_hbm, t_hbm, b_hbm, near, lift_out, far_out,
           xv, dv, uv, ut, tv, bv,
           rt, bt, wy, wx, wzl, vx, vz, vw, vg,
           h_send, h_recv, cy_send, cy_recv, cl_send, cl_recv,
           cz_send, cz_recv, zs_send, zs_recv, x_send, x_recv,
           far_y_send, far_y,
           load_sem, z_sem, send_sem, recv_sem):
    lz, lx = dims
    ly = 3
    ny, nz, nx = 1 << ly, 1 << lz, 1 << lx
    leaf, vecs = x_hbm.shape
    rank = u_hbm.shape[1]
    yblk = vecs // ny
    sub, grp = lax.axis_index("sub"), lax.axis_index("grp")
    y, z = lax.rem(sub, ny), lax.div(sub, ny)

    def y_peer(j):
        return {"sub": z * ny + flip(y, j)}

    def z_peer(j):
        return {"sub": flip(z, j) * ny + y}

    def x_peer(j):
        return {"grp": flip(grp, j)}

    def rows(index, size):
        return pl.ds(pl.multiple_of(index * size, size), size)

    def send(src, dst, group, peer):
        pltpu.make_async_remote_copy(
            src_ref=src, dst_ref=dst, send_sem=send_sem.at[group], recv_sem=recv_sem.at[group],
            device_id=peer, device_id_type=MESH,
        ).start()

    barrier = pltpu.get_barrier_semaphore()

    def greet(sem, peer):
        pl.semaphore_signal(sem, inc=1, device_id=peer, device_id_type=MESH)

    for j in far_first(ny):
        greet(barrier, y_peer(j))
    for place in reversed(range(nz)):
        @pl.when(z < place)
        def _():
            greet(barrier, {"sub": place * ny + y})
    for j in far_first(nx):
        greet(barrier, x_peer(j))

    head = leaf // 2
    loads = {}
    for i, (name, src, dst) in enumerate((
        ("u", u_hbm, uv),
        ("x0", x_hbm.at[pl.ds(0, head)], xv.at[pl.ds(0, head)]),
        ("x1", x_hbm.at[pl.ds(head, head)], xv.at[pl.ds(head, head)]),
        ("t", t_hbm, tv),
        ("d", d_hbm, dv),
        ("b", b_hbm, bv),
    )):
        loads[name] = pltpu.make_async_copy(src, dst, load_sem.at[i])
        loads[name].start()

    pair = lax.div(y, 2)
    outward = 2 * lax.rem(y, 2) - 1

    def spread(src, dst, group):
        for k in (3, 2, 1):
            target = lax.rem(y + k * outward + ny, ny)
            other = lax.div(target, 2)
            slot = lax.rem(pair + other, 2) + 2 * lax.rem(lax.div(pair, 2) + lax.div(other, 2), 2)
            send(src.at[1], dst.at[slot], group, {"sub": z * ny + target})
        send(src.at[2], dst.at[4], group, y_peer(6))

    def climb(base, levels):
        product = tv[base].astype(F32)
        chain = [product]
        for level in range(1, levels):
            product = times_exact(product, tv[base + level])
            chain.append(product)
        return chain

    def down(products, base, levels, rows_of):
        parts = [bv[base].T]
        for i in range(1, levels):
            parts.append(rows_of(times_exact(products[i - 1], bv[base + i]).T))
        return jnp.concatenate(parts, axis=0)

    def near_part(part, parts):
        size = vecs // parts
        at = pl.ds(part * size, size)
        near[:, at] = dot(dv[...], xv[:, at])

    loads["t"].wait()
    ty = climb(0, ly)
    wy[...] = up_weight(ty[ly - 1])
    loads["u"].wait()
    ut[...] = uv[...].T
    loads["x0"].wait()
    hat_t = dot(ut[:, :head], xv[:head, :])
    loads["x1"].wait()
    hat = (hat_t + dot(ut[:, head:], xv[head:, :])).T
    hat_w = wide(hat)
    cy_send[...] = dot(hat_w, wy[...]).astype(BF)
    pl.semaphore_wait(barrier, ny - 1 + nx - 1 + z)
    for place in range(nz):
        @pl.when(z > place)
        def _():
            greet(z_sem, {"sub": place * ny + y})
    for j in far_first(ny):
        send(cy_send.at[rows(flip(y, j), yblk)], cy_recv.at[j], 0, y_peer(j))

    cl_send[...] = dot(hat_w[:, :2 * rank], jnp.concatenate([tv[0], tv[0]], axis=0)).astype(BF)
    h_send[...] = hat.astype(BF)
    tz = climb(ly, lz + lx - 1)
    wx[...] = jnp.concatenate([twice(product) for product in tz[lz - 1:]], axis=1)
    if lz > 1:
        wzl[...] = jnp.concatenate([up_exact(tv[ly])] + [up_weight(tz[i]) for i in range(1, lz - 1)], axis=1)
    lift_out[...] = jnp.concatenate(split(dot(uv[...], tv[0])), axis=1)
    loads["d"].wait()
    near_part(0, 2)
    loads["b"].wait()
    vx[...] = down(climb(ly + lz, lx), ly + lz, lx, twice)

    wait_bytes(cy_recv.at[pl.ds(1, ny - 1)], recv_sem.at[0])
    mid = cy_send[rows(y, yblk), :].astype(F32)
    for j in range(1, ny):
        mid = mid + cy_recv[j].astype(F32)
    mid_w = wide(mid)
    share = dot(mid_w[:, :2 * rank], wx[...])
    for i in range(lx):
        x_send[i] = share[:, i * rank:(i + 1) * rank].astype(BF)
    for place in early(nx // 2, 2):
        @pl.when(grp != place)
        def _():
            apart = flip(grp, place)
            level = sum(jnp.where(apart >= 1 << i, 1, 0) for i in range(1, lx))
            send(x_send.at[level], x_recv.at[apart], 6, {"grp": place})
    zs_send[0] = mid.astype(BF)
    if lz > 1:
        zl = dot(mid_w, wzl[...])
        for i in range(lz - 1):
            zs_send[i + 1] = zl[:, i * rank:(i + 1) * rank].astype(BF)

    @pl.when(z < nz - 1)
    def _():
        pl.semaphore_wait(z_sem, nz - 1 - z)

    for j in far_first(nz):
        send(zs_send.at[level_of(j)], zs_recv.at[j], 4, z_peer(j))
    for j in far_first(ny):
        send(cl_send.at[rows(flip(y, j), yblk)], cl_recv.at[j], 8, y_peer(j))
    spread(t_hbm, rt, 1)
    spread(b_hbm, bt, 5)
    send(h_send, h_recv, 2, y_peer(1))

    wait_bytes(x_recv.at[pl.ds(1, nx - 1)], recv_sem.at[6])
    parts = [x_recv[1]]
    for level in range(1, lx):
        parts.append(tight(functools.reduce(jnp.add, [x_recv[j].astype(F32) for j in range(1 << level, 2 << level)])))
    top = dot(jnp.concatenate(parts, axis=1), vx[...])
    cz_send[...] = top.astype(BF)
    for place in range(nz):
        @pl.when(z != place)
        def _():
            send(cz_send, cz_recv.at[flip(z, place)], 3, {"sub": place * ny + y})

    vz[...] = down(tz, ly, lz, up_weight)

    rt[0] = tv[1]
    rt[5] = tv[2]
    bt[0] = bv[1]
    bt[5] = bv[2]
    wait_bytes(rt.at[pl.ds(1, 4)], recv_sem.at[1])
    lifts = []
    for quad in range(2):
        both = jnp.concatenate([rt[2 * quad], rt[2 * quad + 1]], axis=0)
        lifts.append(dot(both, rt[5 - quad]))
    lifts = jnp.concatenate(lifts, axis=0)
    whole = dot(wide(lifts), up_weight(tz[lz - 1]))
    for r in range(4):
        at = slice(r * rank, (r + 1) * rank)
        vw[:, at] = up_weight(lifts[at].T)
        vg[:, at] = twice(whole[at].T)
    wait_bytes(zs_recv.at[pl.ds(1, nz - 1)], recv_sem.at[4])
    parts = [zs_recv[1]]
    for level in range(1, lz):
        parts.append(wide(functools.reduce(jnp.add, [zs_recv[j].astype(F32) for j in range(1 << level, 2 << level)])))
    mid_far = dot(jnp.concatenate(parts, axis=1), vz[...])

    wait_bytes(cl_recv.at[pl.ds(1, ny - 1)], recv_sem.at[8])
    given = [cl_send[rows(y, yblk), :]] + [cl_recv[j] for j in range(1, ny)]
    sums = [given[2 * r].astype(F32) + given[2 * r + 1].astype(F32) for r in range(4)]
    quads = []
    for quad in range(2):
        left = jnp.concatenate([*split(sums[2 * quad]), *split(sums[2 * quad + 1])], axis=1)
        right = [rt[2 * quad]] * 2 + [rt[2 * quad + 1]] * 2
        quads.append(dot(left, jnp.concatenate(right, axis=0)))
    wait_bytes(bt.at[pl.ds(1, 4)], recv_sem.at[5])
    local = []
    for quad in range(2):
        both = jnp.concatenate([rt[2 * quad], rt[2 * quad + 1]], axis=0)
        high, low = split(dot(both, bt[5 - quad]))
        seen = dot_nt(wide(quads[1 - quad]), jnp.concatenate([high, high, low], axis=1))
        for half in range(2):
            r = 2 * quad + half
            sibling = jnp.concatenate(split(sums[r ^ 1]), axis=1)
            local.append(seen[:, half * rank:(half + 1) * rank] + dot_nt(sibling, jnp.concatenate([bt[r]] * 2, axis=1)))
    local = jnp.concatenate(local, axis=1) + dot(wide(mid_far), vw[...])

    wait_bytes(cz_recv.at[pl.ds(1, nz - 1)], recv_sem.at[3])
    for j in range(1, nz):
        top = top + cz_recv[j].astype(F32)
    pair_far = (local + dot(tight(top), vg[...])).astype(BF)
    for r in range(4):
        far_y_send[r] = pair_far[:, r * rank:(r + 1) * rank]
    for place in early(ny, 1):
        @pl.when(y != place)
        def _():
            send(far_y_send.at[lax.div(flip(y, place), 2)], far_y.at[rows(y, yblk)], 7, {"sub": z * ny + place})
    far_y[rows(y, yblk), :] = far_y_send[0]

    wait_bytes(h_recv, recv_sem.at[2])
    far = dot_nt(h_recv[...], bv[0]).astype(BF)
    near_part(1, 2)
    near[...] += dot_nt(uv[...], far)
    wait_bytes(far_y.at[pl.ds(0, (ny - 1) * yblk)], recv_sem.at[7])
    far_out[...] = far_y[...]

    wait_bytes(cy_recv.at[pl.ds(1, ny - 1)], send_sem.at[0])
    wait_bytes(rt.at[pl.ds(1, 4)], send_sem.at[1])
    wait_bytes(h_send, send_sem.at[2])
    wait_bytes(cz_recv.at[pl.ds(1, nz - 1)], send_sem.at[3])
    wait_bytes(zs_recv.at[pl.ds(1, nz - 1)], send_sem.at[4])
    wait_bytes(bt.at[pl.ds(1, 4)], send_sem.at[5])
    wait_bytes(x_recv.at[pl.ds(1, nx - 1)], send_sem.at[6])
    wait_bytes(far_y.at[pl.ds(0, (ny - 1) * yblk)], send_sem.at[7])
    wait_bytes(cl_recv.at[pl.ds(1, ny - 1)], send_sem.at[8])


def last_kernel(near, lift, far, o_hbm, far_t, ov, store_sem):
    leaf = near.shape[0]
    chunks = store_sem.shape[0]
    tile = leaf // chunks
    far_t[...] = jnp.concatenate([far[...].T] * 2, axis=0)
    stores = []
    for step in range(chunks):
        at = pl.ds(step * tile, tile)
        ov[at, :] = (near[at, :] + dot(lift[at, :], far_t[...])).astype(BF)
        store = pltpu.make_async_copy(ov.at[at], o_hbm.at[at], store_sem.at[step])
        store.start()
        stores.append(store)
    for store in stores:
        store.wait()


def solution(mesh):
    ly = 3
    lz = mesh.shape["sub"].bit_length() - 1 - ly
    lx = mesh.shape["grp"].bit_length() - 1
    ny, nz, nx = 1 << ly, 1 << lz, 1 << lx

    def body(vectors, blocks, basis, transfer, coupling):
        leaf, vecs = vectors.shape[2:]
        rank = basis.shape[3]
        levels = transfer.shape[2]
        yblk = vecs // ny
        scratch = [
            pltpu.VMEM((leaf, vecs), BF),
            pltpu.VMEM((leaf, leaf), BF),
            pltpu.VMEM((leaf, rank), BF),
            pltpu.VMEM((rank, leaf), BF),
            pltpu.VMEM((levels, rank, rank), BF),
            pltpu.VMEM((levels, rank, rank), BF),
            pltpu.VMEM((6, rank, rank), BF),
            pltpu.VMEM((6, rank, rank), BF),
            pltpu.VMEM((3 * rank, rank), BF),
            pltpu.VMEM((2 * rank, lx * rank), BF),
            pltpu.VMEM((3 * rank, max(1, lz - 1) * rank), BF),
            pltpu.VMEM(((2 * lx - 1) * rank, rank), BF),
            pltpu.VMEM(((3 * lz - 2) * rank, rank), BF),
            pltpu.VMEM((3 * rank, 4 * rank), BF),
            pltpu.VMEM((2 * rank, 4 * rank), BF),
            pltpu.VMEM((vecs, rank), BF),
            pltpu.VMEM((vecs, rank), BF),
            pltpu.VMEM((vecs, rank), BF),
            pltpu.VMEM((ny, yblk, rank), BF),
            pltpu.VMEM((vecs, rank), BF),
            pltpu.VMEM((ny, yblk, rank), BF),
            pltpu.VMEM((yblk, rank), BF),
            pltpu.VMEM((nz, yblk, rank), BF),
            pltpu.VMEM((lz, yblk, rank), BF),
            pltpu.VMEM((nz, yblk, rank), BF),
            pltpu.VMEM((lx, yblk, rank), BF),
            pltpu.VMEM((nx, yblk, rank), BF),
            pltpu.VMEM((4, yblk, rank), BF),
            pltpu.VMEM((vecs, rank), BF),
            pltpu.SemaphoreType.DMA((6,)),
            pltpu.SemaphoreType.REGULAR,
            pltpu.SemaphoreType.DMA((9,)),
            pltpu.SemaphoreType.DMA((9,)),
        ]
        vmem = pl.BlockSpec(memory_space=pltpu.VMEM)
        near, lift, far = pl.pallas_call(
            functools.partial(kernel, (lz, lx)),
            out_shape=[
                jax.ShapeDtypeStruct((leaf, vecs), F32),
                jax.ShapeDtypeStruct((leaf, 2 * rank), BF),
                jax.ShapeDtypeStruct((vecs, rank), BF),
            ],
            in_specs=[pl.BlockSpec(memory_space=pltpu.HBM)] * 5,
            out_specs=[vmem] * 3,
            scratch_shapes=scratch,
            compiler_params=pltpu.CompilerParams(
                collective_id=0, has_side_effects=True, vmem_limit_bytes=32 * 1024 * 1024,
            ),
        )(*(pltpu.with_memory_space_constraint(whole[0, 0], pltpu.HBM) for whole in (vectors, blocks, basis, transfer, coupling)))
        out = pl.pallas_call(
            last_kernel,
            out_shape=jax.ShapeDtypeStruct((leaf, vecs), BF),
            in_specs=[vmem] * 3,
            out_specs=pl.BlockSpec(memory_space=pltpu.HBM),
            scratch_shapes=[
                pltpu.VMEM((2 * rank, vecs), BF),
                pltpu.VMEM((leaf, vecs), BF),
                pltpu.SemaphoreType.DMA((4,)),
            ],
            compiler_params=pltpu.CompilerParams(vmem_limit_bytes=24 * 1024 * 1024),
        )(near, lift, far)
        return out[None, None]

    return jax.shard_map(
        body,
        mesh=mesh,
        in_specs=(
            P("grp", "sub", None, None),
            P("grp", "sub", None, None),
            P("grp", "sub", None, None),
            P("grp", "sub", None, None, None),
            P("grp", "sub", None, None, None),
        ),
        out_specs=P("grp", "sub", None, None),
        check_vma=False,
    )
```

```python
import functools

import jax
import jax.numpy as jnp
from jax import lax
from jax.experimental import pallas as pl
from jax.experimental.pallas import tpu as pltpu
from jax.sharding import PartitionSpec as P

MESH = pl.DeviceIdType.MESH
BF = jnp.bfloat16
F32 = jnp.float32


def dot(left, right):
    return jnp.dot(left, right, preferred_element_type=F32)


def dot_nt(left, right):
    return lax.dot_general(left, right, (((1,), (1,)), ((), ())), preferred_element_type=F32)


def dot_tn(left, right):
    return lax.dot_general(left, right, (((0,), (0,)), ((), ())), preferred_element_type=F32)


def split(value):
    high = value.astype(BF)
    return high, (value - high.astype(F32)).astype(BF)


def flip(index, offset):
    out = index
    for bit in range(offset.bit_length()):
        if offset >> bit & 1:
            out = out + (1 << bit) - (2 << bit) * lax.rem(lax.div(index, 1 << bit), 2)
    return out


def level_of(offset):
    return offset.bit_length() - 1


def far_first(count):
    return [j for j in (4, 5, 3, 7, 6, 2, 1) if j < count]


def early(count, cores):
    ring = sorted(range(count), key=lambda place: place if place < count // 2 else count - place + 1.5)
    return [place * cores + core for place in ring for core in reversed(range(cores))]


def wait_bytes(ref, sem):
    pltpu.make_async_copy(ref, ref, sem).wait()


def up_weight(product):
    high, low = split(product)
    return jnp.concatenate([high, high, low], axis=0)


def up_exact(matrix):
    return jnp.concatenate([matrix, matrix, jnp.zeros_like(matrix)], axis=0)


def wide(value):
    high, low = split(value)
    return jnp.concatenate([high, low, high], axis=1)


def times_exact(product, matrix):
    high, low = split(product)
    return dot(high, matrix) + dot(low, matrix)


def kernel(dims, x_hbm, d_hbm, u_hbm, t_hbm, b_hbm, near, lift_out, far_out,
           xv, dv, uv, ut, tv, bv,
           rt, bt, wy, wx, wzl, vx, vz, vw, vg,
           h_send, h_recv, cy_send, cy_recv, cl_send, cl_recv,
           cz_send, cz_recv, zs_send, zs_recv, x_send, x_recv,
           far_y_send, far_y,
           load_sem, z_sem, send_sem, recv_sem):
    lz, lx = dims
    ly = 3
    ny, nz, nx = 1 << ly, 1 << lz, 1 << lx
    leaf, vecs = x_hbm.shape
    rank = u_hbm.shape[1]
    yblk = vecs // ny
    sub, grp = lax.axis_index("sub"), lax.axis_index("grp")
    y, z = lax.rem(sub, ny), lax.div(sub, ny)

    def y_peer(j):
        return {"sub": z * ny + flip(y, j)}

    def z_peer(j):
        return {"sub": flip(z, j) * ny + y}

    def x_peer(j):
        return {"grp": flip(grp, j)}

    def rows(index, size):
        return pl.ds(pl.multiple_of(index * size, size), size)

    def send(src, dst, group, peer):
        pltpu.make_async_remote_copy(
            src_ref=src, dst_ref=dst, send_sem=send_sem.at[group], recv_sem=recv_sem.at[group],
            device_id=peer, device_id_type=MESH,
        ).start()

    barrier = pltpu.get_barrier_semaphore()

    def greet(sem, peer):
        pl.semaphore_signal(sem, inc=1, device_id=peer, device_id_type=MESH)

    for j in far_first(ny):
        greet(barrier, y_peer(j))
    for place in reversed(range(nz)):
        @pl.when(z < place)
        def _():
            greet(barrier, {"sub": place * ny + y})
    for j in far_first(nx):
        greet(barrier, x_peer(j))

    head = leaf // 2
    loads = {}
    for i, (name, src, dst) in enumerate((
        ("u", u_hbm, uv),
        ("x0", x_hbm.at[pl.ds(0, head)], xv.at[pl.ds(0, head)]),
        ("x1", x_hbm.at[pl.ds(head, head)], xv.at[pl.ds(head, head)]),
        ("t", t_hbm, tv),
        ("d", d_hbm, dv),
        ("b", b_hbm, bv),
    )):
        loads[name] = pltpu.make_async_copy(src, dst, load_sem.at[i])
        loads[name].start()

    pair = lax.div(y, 2)
    outward = 2 * lax.rem(y, 2) - 1

    def spread(src, dst, group):
        for k in (3, 2, 1):
            target = lax.rem(y + k * outward + ny, ny)
            other = lax.div(target, 2)
            slot = lax.rem(pair + other, 2) + 2 * lax.rem(lax.div(pair, 2) + lax.div(other, 2), 2)
            send(src.at[1], dst.at[slot], group, {"sub": z * ny + target})
        send(src.at[2], dst.at[4], group, y_peer(6))

    def climb(base, levels):
        product = tv[base].astype(F32)
        chain = [product]
        for level in range(1, levels):
            product = times_exact(product, tv[base + level])
            chain.append(product)
        return chain

    def down(products, base, levels):
        parts = [bv[base].T]
        for i in range(1, levels):
            parts.append(up_weight(times_exact(products[i - 1], bv[base + i]).T))
        return jnp.concatenate(parts, axis=0)

    def near_part(part, parts):
        size = vecs // parts
        at = pl.ds(part * size, size)
        near[:, at] = dot(dv[...], xv[:, at])

    loads["t"].wait()
    ty = climb(0, ly)
    wy[...] = up_weight(ty[ly - 1])
    loads["u"].wait()
    ut[...] = uv[...].T
    loads["x0"].wait()
    hat_t = dot(ut[:, :head], xv[:head, :])
    loads["x1"].wait()
    hat = (hat_t + dot(ut[:, head:], xv[head:, :])).T
    hat_w = wide(hat)
    cy_send[...] = dot(hat_w, wy[...]).astype(BF)
    pl.semaphore_wait(barrier, ny - 1 + nx - 1 + z)
    for place in range(nz):
        @pl.when(z > place)
        def _():
            greet(z_sem, {"sub": place * ny + y})
    for j in far_first(ny):
        send(cy_send.at[rows(flip(y, j), yblk)], cy_recv.at[j], 0, y_peer(j))

    cl_send[...] = dot(hat_w[:, :2 * rank], jnp.concatenate([tv[0], tv[0]], axis=0)).astype(BF)
    h_send[...] = hat.astype(BF)
    tz = climb(ly, lz + lx - 1)
    wx[...] = jnp.concatenate([up_weight(product) for product in tz[lz - 1:]], axis=1)
    if lz > 1:
        wzl[...] = jnp.concatenate([up_exact(tv[ly])] + [up_weight(tz[i]) for i in range(1, lz - 1)], axis=1)
    lift_out[...] = jnp.concatenate(split(dot(uv[...], tv[0])), axis=1)
    loads["d"].wait()
    near_part(0, 2)
    loads["b"].wait()
    vx[...] = down(climb(ly + lz, lx), ly + lz, lx)

    wait_bytes(cy_recv.at[pl.ds(1, ny - 1)], recv_sem.at[0])
    mid = cy_send[rows(y, yblk), :].astype(F32)
    for j in range(1, ny):
        mid = mid + cy_recv[j].astype(F32)
    mid_w = wide(mid)
    share = dot(mid_w, wx[...])
    for i in range(lx):
        x_send[i] = share[:, i * rank:(i + 1) * rank].astype(BF)
    for place in early(nx // 2, 2):
        @pl.when(grp != place)
        def _():
            apart = flip(grp, place)
            level = sum(jnp.where(apart >= 1 << i, 1, 0) for i in range(1, lx))
            send(x_send.at[level], x_recv.at[apart], 6, {"grp": place})
    zs_send[0] = mid.astype(BF)
    if lz > 1:
        zl = dot(mid_w, wzl[...])
        for i in range(lz - 1):
            zs_send[i + 1] = zl[:, i * rank:(i + 1) * rank].astype(BF)

    @pl.when(z < nz - 1)
    def _():
        pl.semaphore_wait(z_sem, nz - 1 - z)

    for j in far_first(nz):
        send(zs_send.at[level_of(j)], zs_recv.at[j], 4, z_peer(j))
    for j in far_first(ny):
        send(cl_send.at[rows(flip(y, j), yblk)], cl_recv.at[j], 8, y_peer(j))
    spread(t_hbm, rt, 1)
    spread(b_hbm, bt, 5)
    send(h_send, h_recv, 2, y_peer(1))

    wait_bytes(x_recv.at[pl.ds(1, nx - 1)], recv_sem.at[6])
    parts = [x_recv[1]]
    for level in range(1, lx):
        parts.append(wide(functools.reduce(jnp.add, [x_recv[j].astype(F32) for j in range(1 << level, 2 << level)])))
    top = dot(jnp.concatenate(parts, axis=1), vx[...])
    cz_send[...] = top.astype(BF)
    for place in range(nz):
        @pl.when(z != place)
        def _():
            send(cz_send, cz_recv.at[flip(z, place)], 3, {"sub": place * ny + y})

    vz[...] = down(tz, ly, lz)

    rt[0] = tv[1]
    rt[5] = tv[2]
    bt[0] = bv[1]
    bt[5] = bv[2]
    wait_bytes(rt.at[pl.ds(1, 4)], recv_sem.at[1])
    lifts = []
    for quad in range(2):
        both = jnp.concatenate([rt[2 * quad], rt[2 * quad + 1]], axis=0)
        lifts.append(dot(both, rt[5 - quad]))
    lifts = jnp.concatenate(lifts, axis=0)
    whole = dot(wide(lifts), wx[:, :rank])
    for r in range(4):
        at = slice(r * rank, (r + 1) * rank)
        vw[:, at] = up_weight(lifts[at].T)
        vg[:, at] = up_weight(whole[at].T)
    wait_bytes(zs_recv.at[pl.ds(1, nz - 1)], recv_sem.at[4])
    parts = [zs_recv[1]]
    for level in range(1, lz):
        parts.append(wide(functools.reduce(jnp.add, [zs_recv[j].astype(F32) for j in range(1 << level, 2 << level)])))
    mid_far = dot(jnp.concatenate(parts, axis=1), vz[...])

    wait_bytes(cl_recv.at[pl.ds(1, ny - 1)], recv_sem.at[8])
    given = [cl_send[rows(y, yblk), :]] + [cl_recv[j] for j in range(1, ny)]
    sums = [given[2 * r].astype(F32) + given[2 * r + 1].astype(F32) for r in range(4)]
    quads = []
    for quad in range(2):
        left = jnp.concatenate([*split(sums[2 * quad]), *split(sums[2 * quad + 1])], axis=1)
        right = [rt[2 * quad]] * 2 + [rt[2 * quad + 1]] * 2
        quads.append(dot(left, jnp.concatenate(right, axis=0)))
    wait_bytes(bt.at[pl.ds(1, 4)], recv_sem.at[5])
    local = []
    for quad in range(2):
        both = jnp.concatenate([rt[2 * quad], rt[2 * quad + 1]], axis=0)
        high, low = split(dot(both, bt[5 - quad]))
        seen = dot_nt(wide(quads[1 - quad]), jnp.concatenate([high, high, low], axis=1))
        for half in range(2):
            r = 2 * quad + half
            sibling = jnp.concatenate(split(sums[r ^ 1]), axis=1)
            local.append(seen[:, half * rank:(half + 1) * rank] + dot_nt(sibling, jnp.concatenate([bt[r]] * 2, axis=1)))
    local = jnp.concatenate(local, axis=1) + dot(wide(mid_far), vw[...])

    wait_bytes(cz_recv.at[pl.ds(1, nz - 1)], recv_sem.at[3])
    for j in range(1, nz):
        top = top + cz_recv[j].astype(F32)
    pair_far = (local + dot(wide(top), vg[...])).astype(BF)
    for r in range(4):
        far_y_send[r] = pair_far[:, r * rank:(r + 1) * rank]
    for place in early(ny, 1):
        @pl.when(y != place)
        def _():
            send(far_y_send.at[lax.div(flip(y, place), 2)], far_y.at[rows(y, yblk)], 7, {"sub": z * ny + place})
    far_y[rows(y, yblk), :] = far_y_send[0]

    wait_bytes(h_recv, recv_sem.at[2])
    far = dot_nt(h_recv[...], bv[0]).astype(BF)
    near_part(1, 2)
    near[...] += dot_nt(uv[...], far)
    wait_bytes(far_y.at[pl.ds(0, (ny - 1) * yblk)], recv_sem.at[7])
    far_out[...] = far_y[...]

    wait_bytes(cy_recv.at[pl.ds(1, ny - 1)], send_sem.at[0])
    wait_bytes(rt.at[pl.ds(1, 4)], send_sem.at[1])
    wait_bytes(h_send, send_sem.at[2])
    wait_bytes(cz_recv.at[pl.ds(1, nz - 1)], send_sem.at[3])
    wait_bytes(zs_recv.at[pl.ds(1, nz - 1)], send_sem.at[4])
    wait_bytes(bt.at[pl.ds(1, 4)], send_sem.at[5])
    wait_bytes(x_recv.at[pl.ds(1, nx - 1)], send_sem.at[6])
    wait_bytes(far_y.at[pl.ds(0, (ny - 1) * yblk)], send_sem.at[7])
    wait_bytes(cl_recv.at[pl.ds(1, ny - 1)], send_sem.at[8])


def last_kernel(near, lift, far, o_hbm, far_t, ov, store_sem):
    leaf = near.shape[0]
    chunks = store_sem.shape[0]
    tile = leaf // chunks
    far_t[...] = jnp.concatenate([far[...].T] * 2, axis=0)
    stores = []
    for step in range(chunks):
        at = pl.ds(step * tile, tile)
        ov[at, :] = (near[at, :] + dot(lift[at, :], far_t[...])).astype(BF)
        store = pltpu.make_async_copy(ov.at[at], o_hbm.at[at], store_sem.at[step])
        store.start()
        stores.append(store)
    for store in stores:
        store.wait()


def solution(mesh):
    ly = 3
    lz = mesh.shape["sub"].bit_length() - 1 - ly
    lx = mesh.shape["grp"].bit_length() - 1
    ny, nz, nx = 1 << ly, 1 << lz, 1 << lx

    def body(vectors, blocks, basis, transfer, coupling):
        leaf, vecs = vectors.shape[2:]
        rank = basis.shape[3]
        levels = transfer.shape[2]
        yblk = vecs // ny
        scratch = [
            pltpu.VMEM((leaf, vecs), BF),
            pltpu.VMEM((leaf, leaf), BF),
            pltpu.VMEM((leaf, rank), BF),
            pltpu.VMEM((rank, leaf), BF),
            pltpu.VMEM((levels, rank, rank), BF),
            pltpu.VMEM((levels, rank, rank), BF),
            pltpu.VMEM((6, rank, rank), BF),
            pltpu.VMEM((6, rank, rank), BF),
            pltpu.VMEM((3 * rank, rank), BF),
            pltpu.VMEM((3 * rank, lx * rank), BF),
            pltpu.VMEM((3 * rank, max(1, lz - 1) * rank), BF),
            pltpu.VMEM(((3 * lx - 2) * rank, rank), BF),
            pltpu.VMEM(((3 * lz - 2) * rank, rank), BF),
            pltpu.VMEM((3 * rank, 4 * rank), BF),
            pltpu.VMEM((3 * rank, 4 * rank), BF),
            pltpu.VMEM((vecs, rank), BF),
            pltpu.VMEM((vecs, rank), BF),
            pltpu.VMEM((vecs, rank), BF),
            pltpu.VMEM((ny, yblk, rank), BF),
            pltpu.VMEM((vecs, rank), BF),
            pltpu.VMEM((ny, yblk, rank), BF),
            pltpu.VMEM((yblk, rank), BF),
            pltpu.VMEM((nz, yblk, rank), BF),
            pltpu.VMEM((lz, yblk, rank), BF),
            pltpu.VMEM((nz, yblk, rank), BF),
            pltpu.VMEM((lx, yblk, rank), BF),
            pltpu.VMEM((nx, yblk, rank), BF),
            pltpu.VMEM((4, yblk, rank), BF),
            pltpu.VMEM((vecs, rank), BF),
            pltpu.SemaphoreType.DMA((6,)),
            pltpu.SemaphoreType.REGULAR,
            pltpu.SemaphoreType.DMA((9,)),
            pltpu.SemaphoreType.DMA((9,)),
        ]
        vmem = pl.BlockSpec(memory_space=pltpu.VMEM)
        near, lift, far = pl.pallas_call(
            functools.partial(kernel, (lz, lx)),
            out_shape=[
                jax.ShapeDtypeStruct((leaf, vecs), F32),
                jax.ShapeDtypeStruct((leaf, 2 * rank), BF),
                jax.ShapeDtypeStruct((vecs, rank), BF),
            ],
            in_specs=[pl.BlockSpec(memory_space=pltpu.HBM)] * 5,
            out_specs=[vmem] * 3,
            scratch_shapes=scratch,
            compiler_params=pltpu.CompilerParams(
                collective_id=0, has_side_effects=True, vmem_limit_bytes=32 * 1024 * 1024,
            ),
        )(*(pltpu.with_memory_space_constraint(whole[0, 0], pltpu.HBM) for whole in (vectors, blocks, basis, transfer, coupling)))
        out = pl.pallas_call(
            last_kernel,
            out_shape=jax.ShapeDtypeStruct((leaf, vecs), BF),
            in_specs=[vmem] * 3,
            out_specs=pl.BlockSpec(memory_space=pltpu.HBM),
            scratch_shapes=[
                pltpu.VMEM((2 * rank, vecs), BF),
                pltpu.VMEM((leaf, vecs), BF),
                pltpu.SemaphoreType.DMA((4,)),
            ],
            compiler_params=pltpu.CompilerParams(vmem_limit_bytes=24 * 1024 * 1024),
        )(near, lift, far)
        return out[None, None]

    return jax.shard_map(
        body,
        mesh=mesh,
        in_specs=(
            P("grp", "sub", None, None),
            P("grp", "sub", None, None),
            P("grp", "sub", None, None),
            P("grp", "sub", None, None, None),
            P("grp", "sub", None, None, None),
        ),
        out_specs=P("grp", "sub", None, None),
        check_vma=False,
    )
```

```python
import functools

import jax
import jax.numpy as jnp
from jax import lax
from jax.experimental import pallas as pl
from jax.experimental.pallas import tpu as pltpu
from jax.sharding import PartitionSpec as P

MESH = pl.DeviceIdType.MESH
BF = jnp.bfloat16
F32 = jnp.float32


def dot(left, right):
    return jnp.dot(left, right, preferred_element_type=F32)


def dot_nt(left, right):
    return lax.dot_general(left, right, (((1,), (1,)), ((), ())), preferred_element_type=F32)


def dot_tn(left, right):
    return lax.dot_general(left, right, (((0,), (0,)), ((), ())), preferred_element_type=F32)


def split(value):
    high = value.astype(BF)
    return high, (value - high.astype(F32)).astype(BF)


def flip(index, offset):
    out = index
    for bit in range(offset.bit_length()):
        if offset >> bit & 1:
            out = out + (1 << bit) - (2 << bit) * lax.rem(lax.div(index, 1 << bit), 2)
    return out


def level_of(offset):
    return offset.bit_length() - 1


def far_first(count):
    return [j for j in (4, 5, 3, 7, 6, 2, 1) if j < count]


def early(count, cores):
    ring = sorted(range(count), key=lambda place: place if place < count // 2 else count - place + 1.5)
    return [place * cores + core for place in ring for core in reversed(range(cores))]


def wait_bytes(ref, sem):
    pltpu.make_async_copy(ref, ref, sem).wait()


def up_weight(product):
    high, low = split(product)
    return jnp.concatenate([high, high, low], axis=0)


def up_exact(matrix):
    return jnp.concatenate([matrix, matrix, jnp.zeros_like(matrix)], axis=0)


def wide(value):
    high, low = split(value)
    return jnp.concatenate([high, low, high], axis=1)


def times_exact(product, matrix):
    high, low = split(product)
    return dot(high, matrix) + dot(low, matrix)


def kernel(dims, x_hbm, d_hbm, u_hbm, t_hbm, b_hbm, near, lift_out, far_out,
           xv, dv, uv, ut, tv, bv,
           rt, bt, wy, wx, wzl, vx, vz, vw, vg,
           h_send, h_recv, cy_send, cy_recv, cl_send, cl_recv,
           cz_send, cz_recv, zs_send, zs_recv, x_send, x_recv,
           far_y_send, far_y,
           load_sem, z_sem, send_sem, recv_sem):
    lz, lx = dims
    ly = 3
    ny, nz, nx = 1 << ly, 1 << lz, 1 << lx
    leaf, vecs = x_hbm.shape
    rank = u_hbm.shape[1]
    yblk = vecs // ny
    sub, grp = lax.axis_index("sub"), lax.axis_index("grp")
    y, z = lax.rem(sub, ny), lax.div(sub, ny)

    def y_peer(j):
        return {"sub": z * ny + flip(y, j)}

    def z_peer(j):
        return {"sub": flip(z, j) * ny + y}

    def x_peer(j):
        return {"grp": flip(grp, j)}

    def rows(index, size):
        return pl.ds(pl.multiple_of(index * size, size), size)

    def send(src, dst, group, peer):
        pltpu.make_async_remote_copy(
            src_ref=src, dst_ref=dst, send_sem=send_sem.at[group], recv_sem=recv_sem.at[group],
            device_id=peer, device_id_type=MESH,
        ).start()

    barrier = pltpu.get_barrier_semaphore()

    def greet(sem, peer):
        pl.semaphore_signal(sem, inc=1, device_id=peer, device_id_type=MESH)

    for j in far_first(ny):
        greet(barrier, y_peer(j))
    for place in reversed(range(nz)):
        @pl.when(z < place)
        def _():
            greet(barrier, {"sub": place * ny + y})
    for j in far_first(nx):
        greet(barrier, x_peer(j))

    head = leaf // 2
    loads = {}
    for i, (name, src, dst) in enumerate((
        ("u", u_hbm, uv),
        ("x0", x_hbm.at[pl.ds(0, head)], xv.at[pl.ds(0, head)]),
        ("x1", x_hbm.at[pl.ds(head, head)], xv.at[pl.ds(head, head)]),
        ("t", t_hbm, tv),
        ("d", d_hbm, dv),
        ("b", b_hbm, bv),
    )):
        loads[name] = pltpu.make_async_copy(src, dst, load_sem.at[i])
        if name not in ("b", "d"):
            loads[name].start()

    pair = lax.div(y, 2)
    outward = 2 * lax.rem(y, 2) - 1

    def spread(src, dst, group):
        for k in (3, 2, 1):
            target = lax.rem(y + k * outward + ny, ny)
            other = lax.div(target, 2)
            slot = lax.rem(pair + other, 2) + 2 * lax.rem(lax.div(pair, 2) + lax.div(other, 2), 2)
            send(src.at[1], dst.at[slot], group, {"sub": z * ny + target})
        send(src.at[2], dst.at[4], group, y_peer(6))

    def climb(base, levels):
        product = tv[base].astype(F32)
        chain = [product]
        for level in range(1, levels):
            product = times_exact(product, tv[base + level])
            chain.append(product)
        return chain

    def down(products, base, levels):
        parts = [bv[base].T]
        for i in range(1, levels):
            parts.append(up_weight(times_exact(products[i - 1], bv[base + i]).T))
        return jnp.concatenate(parts, axis=0)

    def near_part(part, parts):
        size = vecs // parts
        at = pl.ds(part * size, size)
        near[:, at] = dot(dv[...], xv[:, at])

    loads["t"].wait()
    ty = climb(0, ly)
    wy[...] = up_weight(ty[ly - 1])
    loads["u"].wait()
    ut[...] = uv[...].T
    loads["x0"].wait()
    hat_t = dot(ut[:, :head], xv[:head, :])
    loads["x1"].wait()
    loads["b"].start()
    loads["d"].start()
    hat = (hat_t + dot(ut[:, head:], xv[head:, :])).T
    hat_w = wide(hat)
    cy_send[...] = dot(hat_w, wy[...]).astype(BF)
    pl.semaphore_wait(barrier, ny - 1 + nx - 1 + z)
    for j in far_first(ny):
        send(cy_send.at[rows(flip(y, j), yblk)], cy_recv.at[j], 0, y_peer(j))
    for place in range(nz):
        @pl.when(z > place)
        def _():
            greet(z_sem, {"sub": place * ny + y})

    cl_send[...] = dot(hat_w[:, :2 * rank], jnp.concatenate([tv[0], tv[0]], axis=0)).astype(BF)
    h_send[...] = hat.astype(BF)
    tz = climb(ly, lz + lx - 1)
    wx[...] = jnp.concatenate([up_weight(product) for product in tz[lz - 1:]], axis=1)
    if lz > 1:
        wzl[...] = jnp.concatenate([up_exact(tv[ly])] + [up_weight(tz[i]) for i in range(1, lz - 1)], axis=1)
    lift_out[...] = jnp.concatenate(split(dot(uv[...], tv[0])), axis=1)
    loads["d"].wait()
    near_part(0, 2)
    loads["b"].wait()
    vx[...] = down(climb(ly + lz, lx), ly + lz, lx)

    wait_bytes(cy_recv.at[pl.ds(1, ny - 1)], recv_sem.at[0])
    mid = cy_send[rows(y, yblk), :].astype(F32)
    for j in range(1, ny):
        mid = mid + cy_recv[j].astype(F32)
    mid_w = wide(mid)
    share = dot(mid_w, wx[...])
    for i in range(lx):
        x_send[i] = share[:, i * rank:(i + 1) * rank].astype(BF)
    for place in early(nx // 2, 2):
        @pl.when(grp != place)
        def _():
            apart = flip(grp, place)
            level = sum(jnp.where(apart >= 1 << i, 1, 0) for i in range(1, lx))
            send(x_send.at[level], x_recv.at[apart], 6, {"grp": place})
    zs_send[0] = mid.astype(BF)
    if lz > 1:
        zl = dot(mid_w, wzl[...])
        for i in range(lz - 1):
            zs_send[i + 1] = zl[:, i * rank:(i + 1) * rank].astype(BF)

    @pl.when(z < nz - 1)
    def _():
        pl.semaphore_wait(z_sem, nz - 1 - z)

    for j in far_first(nz):
        send(zs_send.at[level_of(j)], zs_recv.at[j], 4, z_peer(j))
    for j in far_first(ny):
        send(cl_send.at[rows(flip(y, j), yblk)], cl_recv.at[j], 8, y_peer(j))
    spread(t_hbm, rt, 1)
    spread(b_hbm, bt, 5)
    send(h_send, h_recv, 2, y_peer(1))

    wait_bytes(x_recv.at[pl.ds(1, nx - 1)], recv_sem.at[6])
    parts = [x_recv[1]]
    for level in range(1, lx):
        parts.append(wide(functools.reduce(jnp.add, [x_recv[j].astype(F32) for j in range(1 << level, 2 << level)])))
    top = dot(jnp.concatenate(parts, axis=1), vx[...])
    cz_send[...] = top.astype(BF)
    for place in range(nz):
        @pl.when(z != place)
        def _():
            send(cz_send, cz_recv.at[flip(z, place)], 3, {"sub": place * ny + y})

    vz[...] = down(tz, ly, lz)

    rt[0] = tv[1]
    rt[5] = tv[2]
    bt[0] = bv[1]
    bt[5] = bv[2]
    wait_bytes(rt.at[pl.ds(1, 4)], recv_sem.at[1])
    lifts = []
    for quad in range(2):
        both = jnp.concatenate([rt[2 * quad], rt[2 * quad + 1]], axis=0)
        lifts.append(dot(both, rt[5 - quad]))
    lifts = jnp.concatenate(lifts, axis=0)
    whole = dot(wide(lifts), wx[:, :rank])
    for r in range(4):
        at = slice(r * rank, (r + 1) * rank)
        vw[:, at] = up_weight(lifts[at].T)
        vg[:, at] = up_weight(whole[at].T)
    wait_bytes(zs_recv.at[pl.ds(1, nz - 1)], recv_sem.at[4])
    parts = [zs_recv[1]]
    for level in range(1, lz):
        parts.append(wide(functools.reduce(jnp.add, [zs_recv[j].astype(F32) for j in range(1 << level, 2 << level)])))
    mid_far = dot(jnp.concatenate(parts, axis=1), vz[...])

    wait_bytes(cl_recv.at[pl.ds(1, ny - 1)], recv_sem.at[8])
    given = [cl_send[rows(y, yblk), :]] + [cl_recv[j] for j in range(1, ny)]
    sums = [given[2 * r].astype(F32) + given[2 * r + 1].astype(F32) for r in range(4)]
    quads = []
    for quad in range(2):
        left = jnp.concatenate([*split(sums[2 * quad]), *split(sums[2 * quad + 1])], axis=1)
        right = [rt[2 * quad]] * 2 + [rt[2 * quad + 1]] * 2
        quads.append(dot(left, jnp.concatenate(right, axis=0)))
    wait_bytes(bt.at[pl.ds(1, 4)], recv_sem.at[5])
    local = []
    for quad in range(2):
        both = jnp.concatenate([rt[2 * quad], rt[2 * quad + 1]], axis=0)
        high, low = split(dot(both, bt[5 - quad]))
        seen = dot_nt(wide(quads[1 - quad]), jnp.concatenate([high, high, low], axis=1))
        for half in range(2):
            r = 2 * quad + half
            sibling = jnp.concatenate(split(sums[r ^ 1]), axis=1)
            local.append(seen[:, half * rank:(half + 1) * rank] + dot_nt(sibling, jnp.concatenate([bt[r]] * 2, axis=1)))
    local = jnp.concatenate(local, axis=1) + dot(wide(mid_far), vw[...])

    wait_bytes(cz_recv.at[pl.ds(1, nz - 1)], recv_sem.at[3])
    for j in range(1, nz):
        top = top + cz_recv[j].astype(F32)
    pair_far = (local + dot(wide(top), vg[...])).astype(BF)
    for r in range(4):
        far_y_send[r] = pair_far[:, r * rank:(r + 1) * rank]
    for place in early(ny, 1):
        @pl.when(y != place)
        def _():
            send(far_y_send.at[lax.div(flip(y, place), 2)], far_y.at[rows(y, yblk)], 7, {"sub": z * ny + place})
    far_y[rows(y, yblk), :] = far_y_send[0]

    wait_bytes(h_recv, recv_sem.at[2])
    far = dot_nt(h_recv[...], bv[0]).astype(BF)
    near_part(1, 2)
    near[...] += dot_nt(uv[...], far)
    wait_bytes(far_y.at[pl.ds(0, (ny - 1) * yblk)], recv_sem.at[7])
    far_out[...] = far_y[...]

    wait_bytes(cy_recv.at[pl.ds(1, ny - 1)], send_sem.at[0])
    wait_bytes(rt.at[pl.ds(1, 4)], send_sem.at[1])
    wait_bytes(h_send, send_sem.at[2])
    wait_bytes(cz_recv.at[pl.ds(1, nz - 1)], send_sem.at[3])
    wait_bytes(zs_recv.at[pl.ds(1, nz - 1)], send_sem.at[4])
    wait_bytes(bt.at[pl.ds(1, 4)], send_sem.at[5])
    wait_bytes(x_recv.at[pl.ds(1, nx - 1)], send_sem.at[6])
    wait_bytes(far_y.at[pl.ds(0, (ny - 1) * yblk)], send_sem.at[7])
    wait_bytes(cl_recv.at[pl.ds(1, ny - 1)], send_sem.at[8])


def last_kernel(near, lift, far, o_hbm, far_t, ov, store_sem):
    leaf = near.shape[0]
    chunks = store_sem.shape[0]
    tile = leaf // chunks
    far_t[...] = jnp.concatenate([far[...].T] * 2, axis=0)
    stores = []
    for step in range(chunks):
        at = pl.ds(step * tile, tile)
        ov[at, :] = (near[at, :] + dot(lift[at, :], far_t[...])).astype(BF)
        store = pltpu.make_async_copy(ov.at[at], o_hbm.at[at], store_sem.at[step])
        store.start()
        stores.append(store)
    for store in stores:
        store.wait()


def solution(mesh):
    ly = 3
    lz = mesh.shape["sub"].bit_length() - 1 - ly
    lx = mesh.shape["grp"].bit_length() - 1
    ny, nz, nx = 1 << ly, 1 << lz, 1 << lx

    def body(vectors, blocks, basis, transfer, coupling):
        leaf, vecs = vectors.shape[2:]
        rank = basis.shape[3]
        levels = transfer.shape[2]
        yblk = vecs // ny
        scratch = [
            pltpu.VMEM((leaf, vecs), BF),
            pltpu.VMEM((leaf, leaf), BF),
            pltpu.VMEM((leaf, rank), BF),
            pltpu.VMEM((rank, leaf), BF),
            pltpu.VMEM((levels, rank, rank), BF),
            pltpu.VMEM((levels, rank, rank), BF),
            pltpu.VMEM((6, rank, rank), BF),
            pltpu.VMEM((6, rank, rank), BF),
            pltpu.VMEM((3 * rank, rank), BF),
            pltpu.VMEM((3 * rank, lx * rank), BF),
            pltpu.VMEM((3 * rank, max(1, lz - 1) * rank), BF),
            pltpu.VMEM(((3 * lx - 2) * rank, rank), BF),
            pltpu.VMEM(((3 * lz - 2) * rank, rank), BF),
            pltpu.VMEM((3 * rank, 4 * rank), BF),
            pltpu.VMEM((3 * rank, 4 * rank), BF),
            pltpu.VMEM((vecs, rank), BF),
            pltpu.VMEM((vecs, rank), BF),
            pltpu.VMEM((vecs, rank), BF),
            pltpu.VMEM((ny, yblk, rank), BF),
            pltpu.VMEM((vecs, rank), BF),
            pltpu.VMEM((ny, yblk, rank), BF),
            pltpu.VMEM((yblk, rank), BF),
            pltpu.VMEM((nz, yblk, rank), BF),
            pltpu.VMEM((lz, yblk, rank), BF),
            pltpu.VMEM((nz, yblk, rank), BF),
            pltpu.VMEM((lx, yblk, rank), BF),
            pltpu.VMEM((nx, yblk, rank), BF),
            pltpu.VMEM((4, yblk, rank), BF),
            pltpu.VMEM((vecs, rank), BF),
            pltpu.SemaphoreType.DMA((6,)),
            pltpu.SemaphoreType.REGULAR,
            pltpu.SemaphoreType.DMA((9,)),
            pltpu.SemaphoreType.DMA((9,)),
        ]
        vmem = pl.BlockSpec(memory_space=pltpu.VMEM)
        near, lift, far = pl.pallas_call(
            functools.partial(kernel, (lz, lx)),
            out_shape=[
                jax.ShapeDtypeStruct((leaf, vecs), F32),
                jax.ShapeDtypeStruct((leaf, 2 * rank), BF),
                jax.ShapeDtypeStruct((vecs, rank), BF),
            ],
            in_specs=[pl.BlockSpec(memory_space=pltpu.HBM)] * 5,
            out_specs=[vmem] * 3,
            scratch_shapes=scratch,
            compiler_params=pltpu.CompilerParams(
                collective_id=0, has_side_effects=True, vmem_limit_bytes=32 * 1024 * 1024,
            ),
        )(*(pltpu.with_memory_space_constraint(whole[0, 0], pltpu.HBM) for whole in (vectors, blocks, basis, transfer, coupling)))
        out = pl.pallas_call(
            last_kernel,
            out_shape=jax.ShapeDtypeStruct((leaf, vecs), BF),
            in_specs=[vmem] * 3,
            out_specs=pl.BlockSpec(memory_space=pltpu.HBM),
            scratch_shapes=[
                pltpu.VMEM((2 * rank, vecs), BF),
                pltpu.VMEM((leaf, vecs), BF),
                pltpu.SemaphoreType.DMA((4,)),
            ],
            compiler_params=pltpu.CompilerParams(vmem_limit_bytes=24 * 1024 * 1024),
        )(near, lift, far)
        return out[None, None]

    return jax.shard_map(
        body,
        mesh=mesh,
        in_specs=(
            P("grp", "sub", None, None),
            P("grp", "sub", None, None),
            P("grp", "sub", None, None),
            P("grp", "sub", None, None, None),
            P("grp", "sub", None, None, None),
        ),
        out_specs=P("grp", "sub", None, None),
        check_vma=False,
    )
```
